32 devices in a mesh: lat: 8 (over z, y), lon: 4 (over x, core).
Axes of the slice: x: 2, y: 2, z: 4, core: 2. Of those that a mesh axis runs over, the one named last changes fastest.
Arguments:
- grid_state: bfloat16 [16, 720, 640], P('lat', 'lon'), may hold values from -6 to 6
- conv_weight: float32 [3, 3, 640], replicated, may hold values from -2.4 to 2.4
- spectral_gain: float32 [2, 256, 640], P(None, None, 'lon'), may hold values from -4 to 4
- spectral_weight: bfloat16 [2, 640, 640], P(None, None, 'lon'), may hold values from -0.125 to 0.125
- norm_gain: float32 [640], replicated, may hold values from 0.1 to 1.9
- expand_weight: bfloat16 [640, 1280], replicated, may hold values from -0.25 to 0.25
- reduce_weight: bfloat16 [1280, 640], replicated, may hold values from -0.15625 to 0.15625
Outputs:
- block_output: bfloat16 [16, 720, 640], P('lat', 'lon')
The draws below stay inside these ranges and needn't reach their ends.
All inputs are finite; a program needn't handle non-finite values.
Results may differ from the reference program's by a relative error of at most 0.015.
Values may be sent and summed in bfloat16 or wider, within the bound.
No kernel may reach another device: no remote copies, remote signals or barrier semaphores. Data moves between devices by JAX's collectives and lax.ppermute only.
A program may use at most 128 MiB of HBM per device.

```python
import math
import jax
import jax.numpy as jnp
from jax import lax

C = 640
FFN = 1280
M = 256
NLON = 720
NLAT = 16


def levels(key, dims, split, low, largest):
    loudness = 1.0
    for position, blocks in split:
        draws = jax.random.uniform(jax.random.fold_in(jax.random.fold_in(key, 6), position), (blocks,), jnp.float32, low / len(split), largest / len(split))
        loudness = loudness * jnp.repeat(jnp.exp(draws), dims[position] // blocks).reshape((-1,) + (1,) * (len(dims) - 1 - position))
    return loudness


def normal_values(own_key, extent, spread, limit, pieces=(), kind=jnp.bfloat16):
    values = spread * jax.random.normal(own_key, extent, jnp.float32)
    if pieces:
        values = values * levels(own_key, extent, pieces, -0.22, 0.18)
    return jnp.clip(values, -limit, limit).astype(kind)


def setup_inputs(seed: int = 0) -> dict:
    key_of = jax.random.split(jax.random.key(seed), 8)
    return {
        "grid_state": normal_values(key_of[0], (NLAT, NLON, C), 1.0, 6.0, ((0, 8), (1, 4))),
        "conv_weight": normal_values(key_of[1], (3, 3, C), 0.4, 2.4, (), jnp.float32),
        "spectral_gain": normal_values(key_of[2], (2, M, C), 1.0, 4.0, ((2, 4),), jnp.float32),
        "spectral_weight": normal_values(key_of[3], (2, C, C), (4 * C) ** -0.5, 0.125, ((2, 4),)),
        "norm_gain": jnp.clip(1.0 + 0.18 * jax.random.normal(key_of[4], (C,), jnp.float32), 0.1, 1.9),
        "expand_weight": normal_values(key_of[5], (C, FFN), C ** -0.5, 0.25),
        "reduce_weight": normal_values(key_of[6], (FFN, C), FFN ** -0.5, 0.15625),
    }


norm_eps = 1e-06
underflow_cut = -60.0

def legendre_table(orders, lat_total, degree_count):
    colatitude = (jnp.arange(lat_total, dtype=jnp.float32) + 0.5) * (math.pi / lat_total)
    cosines = jnp.cos(colatitude)
    sine_values = jnp.sin(colatitude)
    rank_values = jnp.arange(1, degree_count + 1, dtype=jnp.int32)
    rank_float = rank_values.astype(jnp.float32)
    log_terms = 0.5 * jnp.log((2.0 * rank_float + 1.0) / (2.0 * rank_float))
    log_norm = lax.optimization_barrier(jnp.sum(jnp.where(rank_values[None, :] <= orders[:, None], log_terms[None, :], jnp.float32(0.0)), axis=1))
    order_float = orders.astype(jnp.float32)[:, None]
    log_start = -0.5 * math.log(4.0 * math.pi) + log_norm[:, None] + order_float * jnp.log(sine_values)[None, :]
    start_value = jnp.where(log_start > underflow_cut, jnp.exp(jnp.maximum(log_start, underflow_cut)), jnp.float32(0.0))

    def advance(totals, degree):
        previous, earlier = totals
        degree_float = degree.astype(jnp.float32)
        raise_coef = jnp.sqrt(jnp.maximum(4.0 * degree_float * degree_float - 1.0, 0.0) / jnp.maximum(degree_float * degree_float - order_float * order_float, 1.0))
        lower_coef = jnp.sqrt(jnp.maximum((degree_float - 1.0) ** 2 - order_float * order_float, 0.0) / jnp.maximum(4.0 * (degree_float - 1.0) ** 2 - 1.0, 1.0))
        recurred = raise_coef * (cosines[None, :] * previous - lower_coef * earlier)
        current = jnp.where(degree < orders[:, None], jnp.float32(0.0), jnp.where(degree == orders[:, None], start_value, recurred))
        return ((current, previous), current)
    blank = jnp.zeros((orders.shape[0], lat_total), jnp.float32)
    unused, table_values = lax.scan(advance, (blank, blank), jnp.arange(degree_count, dtype=jnp.int32))
    return table_values

def quadrature(lat_total):
    colatitude = (jnp.arange(lat_total, dtype=jnp.float32) + 0.5) * (math.pi / lat_total)
    return 2.0 * math.pi * math.pi / lat_total * jnp.sin(colatitude)

def fourier_table(longitudes, lon_total, mode_count):
    mode_index = jnp.arange(mode_count, dtype=jnp.int32)
    phase_index = longitudes[:, None] * mode_index[None, :] % lon_total
    angles = phase_index.astype(jnp.float32) * (2.0 * math.pi / lon_total)
    return (jnp.stack([jnp.cos(angles), -jnp.sin(angles)], axis=1) / lon_total).astype(jnp.bfloat16)

def synthesis_table(longitudes, lon_total, mode_count):
    mode_index = jnp.arange(mode_count, dtype=jnp.int32)
    phase_index = mode_index[:, None] * longitudes[None, :] % lon_total
    angles = phase_index.astype(jnp.float32) * (2.0 * math.pi / lon_total)
    doubling = jnp.where(mode_index == 0, 1.0, 2.0).astype(jnp.float32)[:, None]
    return jnp.stack([doubling * jnp.cos(angles), -doubling * jnp.sin(angles)], axis=0).astype(jnp.bfloat16)

def reference(grid_state, conv_weight, spectral_gain, spectral_weight, norm_gain, expand_weight, reduce_weight):
    lat_total = grid_state.shape[0]
    values_wide = grid_state.astype(jnp.float32)
    padded = jnp.pad(values_wide, ((1, 1), (0, 0), (0, 0)))
    padded = jnp.concatenate([padded[:, -1:], padded, padded[:, :1]], axis=1)
    filtered = jnp.zeros_like(values_wide)
    for row_shift in range(3):
        for col_shift in range(3):
            filtered = filtered + conv_weight[row_shift, col_shift] * padded[row_shift:row_shift + lat_total, col_shift:col_shift + NLON]
    first_section = (values_wide + jax.nn.gelu(filtered)).astype(jnp.bfloat16)
    longitudes = jnp.arange(NLON, dtype=jnp.int32)
    forward_table = fourier_table(longitudes, NLON, M)
    spectrum = jnp.einsum('tpc,prm->tmrc', first_section.astype(jnp.float32), forward_table.astype(jnp.float32), precision=lax.Precision.HIGHEST).astype(jnp.bfloat16)
    legendre = legendre_table(jnp.arange(M, dtype=jnp.int32), lat_total, M)
    analysis_table = (legendre * quadrature(lat_total)[None, None, :]).astype(jnp.bfloat16)
    coefficients = jnp.einsum('lmt,tmrc->lmrc', analysis_table.astype(jnp.float32), spectrum.astype(jnp.float32), precision=lax.Precision.HIGHEST)
    gain_real = spectral_gain[0][:, None, :]
    gain_imag = spectral_gain[1][:, None, :]
    coef_real = coefficients[:, :, 0, :]
    coef_imag = coefficients[:, :, 1, :]
    gained = jnp.stack([gain_real * coef_real - gain_imag * coef_imag, gain_real * coef_imag + gain_imag * coef_real], axis=2).astype(jnp.bfloat16)
    real_in = gained[:, :, 0, :].astype(jnp.float32)
    imag_in = gained[:, :, 1, :].astype(jnp.float32)
    mix_real = spectral_weight[0].astype(jnp.float32)
    mix_imag = spectral_weight[1].astype(jnp.float32)
    real_out = jnp.einsum('lmc,cd->lmd', real_in, mix_real, precision=lax.Precision.HIGHEST) - jnp.einsum('lmc,cd->lmd', imag_in, mix_imag, precision=lax.Precision.HIGHEST)
    imag_out = jnp.einsum('lmc,cd->lmd', real_in, mix_imag, precision=lax.Precision.HIGHEST) + jnp.einsum('lmc,cd->lmd', imag_in, mix_real, precision=lax.Precision.HIGHEST)
    mixed = jnp.stack([real_out, imag_out], axis=2).astype(jnp.bfloat16)
    synthesis_legendre = legendre.astype(jnp.bfloat16)
    cycle_modes = jnp.einsum('lmt,lmrc->tmrc', synthesis_legendre.astype(jnp.float32), mixed.astype(jnp.float32), precision=lax.Precision.HIGHEST).astype(jnp.bfloat16)
    inverse_table = synthesis_table(longitudes, NLON, M)
    spectral_out = jnp.einsum('tmrc,rmp->tpc', cycle_modes.astype(jnp.float32), inverse_table.astype(jnp.float32), precision=lax.Precision.HIGHEST)
    second_section = (first_section.astype(jnp.float32) + spectral_out).astype(jnp.bfloat16)
    second_wide = second_section.astype(jnp.float32)
    scale_values = lax.rsqrt(lax.optimization_barrier(jnp.mean(second_wide * second_wide, axis=-1, keepdims=True)) + norm_eps)
    normed = (second_wide * norm_gain * scale_values).astype(jnp.bfloat16)
    flat_rows = normed.reshape(-1, C)
    hidden = jax.nn.gelu(jnp.dot(flat_rows, expand_weight, preferred_element_type=jnp.float32)).astype(jnp.bfloat16)
    update = jnp.dot(hidden, reduce_weight, preferred_element_type=jnp.float32)
    block_output = (second_wide.reshape(-1, C) + update).astype(jnp.bfloat16)
    return block_output.reshape(grid_state.shape)
```

```python
import functools
import math

import jax
import jax.numpy as jnp
import numpy as np
from jax import lax
from jax.experimental import pallas as pl
from jax.experimental.pallas import tpu as pltpu
from jax.sharding import Mesh
from jax.sharding import PartitionSpec as P

M = 256
LANES = 128


norm_eps = 1e-06
underflow_cut = -60.0
degree_block = 16


def padded_2(value, sides, width, wrap):
    for axis, dim in sides:
        count, length = (lax.axis_size(axis), value.shape[dim])
        up = [(i, (i + 1) % count) for i in range(count if wrap else count - 1)]
        down = [(j, i) for i, j in up]
        last = lax.slice_in_dim(value, length - width, length, axis=dim)
        initial = lax.slice_in_dim(value, 0, width, axis=dim)
        before = lax.ppermute(last, axis, up)
        after = lax.ppermute(initial, axis, down)
        value = jnp.concatenate([before, value, after], axis=dim)
    return value


def legendre_table(orders, lat_total, degree_count):
    colatitude = (jnp.arange(lat_total, dtype=jnp.float32) + 0.5) * (math.pi / lat_total)
    cosines = jnp.cos(colatitude)
    sine_values = jnp.sin(colatitude)
    rank_values = jnp.arange(1, degree_count + 1, dtype=jnp.int32)
    rank_float = rank_values.astype(jnp.float32)
    log_terms = 0.5 * jnp.log((2.0 * rank_float + 1.0) / (2.0 * rank_float))
    log_norm = jnp.sum(
        jnp.where(rank_values[None, :] <= orders[:, None], log_terms[None, :], jnp.float32(0.0)),
        axis=1,
    )
    order_float = orders.astype(jnp.float32)[:, None]
    log_start = (
        -0.5 * math.log(4.0 * math.pi)
        + log_norm[:, None]
        + order_float * jnp.log(sine_values)[None, :]
    )
    start_value = jnp.where(
        log_start > underflow_cut, jnp.exp(jnp.maximum(log_start, underflow_cut)), jnp.float32(0.0)
    )

    def advance_block(totals, block_start):
        previous, earlier = totals
        rows_out = []
        for inner in range(degree_block):
            degree = block_start + inner
            degree_float = degree.astype(jnp.float32)
            raise_coef = jnp.sqrt(
                jnp.maximum(4.0 * degree_float * degree_float - 1.0, 0.0)
                / jnp.maximum(degree_float * degree_float - order_float * order_float, 1.0)
            )
            lower_coef = jnp.sqrt(
                jnp.maximum((degree_float - 1.0) ** 2 - order_float * order_float, 0.0)
                / jnp.maximum(4.0 * (degree_float - 1.0) ** 2 - 1.0, 1.0)
            )
            recurred = raise_coef * (cosines[None, :] * previous - lower_coef * earlier)
            current = jnp.where(
                degree < orders[:, None],
                jnp.float32(0.0),
                jnp.where(degree == orders[:, None], start_value, recurred),
            )
            earlier = previous
            previous = current
            rows_out.append(current)
        return ((previous, earlier), jnp.stack(rows_out, axis=0))

    blank = jnp.zeros((orders.shape[0], lat_total), jnp.float32)
    starts = jnp.arange(0, degree_count, degree_block, dtype=jnp.int32)
    unused, table_blocks = lax.scan(advance_block, (blank, blank), starts)
    return table_blocks.reshape(degree_count, orders.shape[0], lat_total)


def quadrature(lat_total):
    colatitude = (jnp.arange(lat_total, dtype=jnp.float32) + 0.5) * (math.pi / lat_total)
    return 2.0 * math.pi * math.pi / lat_total * jnp.sin(colatitude)


def fourier_table(longitudes, lon_total, mode_count):
    mode_index = jnp.arange(mode_count, dtype=jnp.int32)
    phase_index = longitudes[:, None] * mode_index[None, :] % lon_total
    angles = phase_index.astype(jnp.float32) * (2.0 * math.pi / lon_total)
    return (jnp.stack([jnp.cos(angles), -jnp.sin(angles)], axis=1) / lon_total).astype(jnp.bfloat16)


def synthesis_table(longitudes, lon_total, mode_count):
    mode_index = jnp.arange(mode_count, dtype=jnp.int32)
    phase_index = mode_index[:, None] * longitudes[None, :] % lon_total
    angles = phase_index.astype(jnp.float32) * (2.0 * math.pi / lon_total)
    doubling = jnp.where(mode_index == 0, 1.0, 2.0).astype(jnp.float32)[:, None]
    return jnp.stack([doubling * jnp.cos(angles), -doubling * jnp.sin(angles)], axis=0).astype(
        jnp.bfloat16
    )


def banded_shards(
    grid_state, conv_weight, spectral_gain, spectral_weight, norm_gain, expand_weight, reduce_weight
):
    lat_rows, sector_width, channel_total = grid_state.shape
    lat_count = lax.axis_size("lat")
    lon_count = lax.axis_size("lon")
    lat_total = lat_rows * lat_count
    lon_total = sector_width * lon_count
    mode_count = M
    order_share = mode_count // lat_count
    channel_share = channel_total // lon_count
    lat_position = lax.axis_index("lat")
    wrapped = padded_2(grid_state, (("lon", 1),), 1, True)
    padded = padded_2(wrapped, (("lat", 0),), 1, False)
    padded_wide = padded.astype(jnp.float32)
    filtered = jnp.zeros((lat_rows, sector_width, channel_total), jnp.float32)
    for row_shift in range(3):
        for col_shift in range(3):
            filtered = (
                filtered
                + conv_weight[row_shift, col_shift]
                * padded_wide[
                    row_shift : row_shift + lat_rows, col_shift : col_shift + sector_width
                ]
            )
    first_section = (grid_state.astype(jnp.float32) + jax.nn.gelu(filtered)).astype(jnp.bfloat16)
    gathered = lax.all_to_all(first_section, "lon", split_axis=2, concat_axis=1, tiled=True)
    forward_table = fourier_table(jnp.arange(lon_total, dtype=jnp.int32), lon_total, mode_count)
    spectrum = jnp.einsum(
        "tpc,prm->tmrc", gathered, forward_table, preferred_element_type=jnp.float32
    ).astype(jnp.bfloat16)
    cycle_spectrum = lax.all_to_all(spectrum, "lat", split_axis=1, concat_axis=0, tiled=True)
    orders = lat_position * order_share + jnp.arange(order_share, dtype=jnp.int32)
    legendre = legendre_table(orders, lat_total, mode_count)
    analysis_table = (legendre * quadrature(lat_total)[None, None, :]).astype(jnp.bfloat16)
    coefficients = jnp.einsum(
        "lmt,tmrc->lmrc", analysis_table, cycle_spectrum, preferred_element_type=jnp.float32
    )
    gain_real = spectral_gain[0][:, None, :]
    gain_imag = spectral_gain[1][:, None, :]
    coef_real = coefficients[:, :, 0, :]
    coef_imag = coefficients[:, :, 1, :]
    gained = jnp.stack(
        [
            gain_real * coef_real - gain_imag * coef_imag,
            gain_real * coef_imag + gain_imag * coef_real,
        ],
        axis=2,
    ).astype(jnp.bfloat16)
    blank = jnp.zeros((mode_count * order_share, channel_share), jnp.float32)
    portion = lax.all_gather(gained, "lon", axis=3, tiled=True)
    width_part = portion.shape[3]
    weight_rows = lax.slice_in_dim(spectral_weight, 0, width_part, axis=1)
    real_part = portion[:, :, 0, :].reshape(-1, width_part)
    imag_part = portion[:, :, 1, :].reshape(-1, width_part)
    real_sum = (
        blank
        + jnp.dot(real_part, weight_rows[0], preferred_element_type=jnp.float32)
        - jnp.dot(imag_part, weight_rows[1], preferred_element_type=jnp.float32)
    )
    imag_sum = (
        blank
        + jnp.dot(real_part, weight_rows[1], preferred_element_type=jnp.float32)
        + jnp.dot(imag_part, weight_rows[0], preferred_element_type=jnp.float32)
    )
    mixed = jnp.stack(
        [
            real_sum.reshape(mode_count, order_share, channel_share),
            imag_sum.reshape(mode_count, order_share, channel_share),
        ],
        axis=2,
    ).astype(jnp.bfloat16)
    synthesis_legendre = legendre.astype(jnp.bfloat16)
    cycle_modes = jnp.einsum(
        "lmt,lmrc->tmrc", synthesis_legendre, mixed, preferred_element_type=jnp.float32
    ).astype(jnp.bfloat16)
    band_modes = lax.all_to_all(cycle_modes, "lat", split_axis=0, concat_axis=1, tiled=True)
    inverse_table = synthesis_table(jnp.arange(lon_total, dtype=jnp.int32), lon_total, mode_count)
    all_lons = jnp.einsum(
        "tmrc,rmp->tpc", band_modes, inverse_table, preferred_element_type=jnp.float32
    )
    spectral_out = lax.all_to_all(
        all_lons.astype(jnp.bfloat16), "lon", split_axis=1, concat_axis=2, tiled=True
    ).astype(all_lons.dtype)
    second_section = (first_section.astype(jnp.float32) + spectral_out).astype(jnp.bfloat16)
    second_wide = second_section.astype(jnp.float32)
    scale_values = lax.rsqrt(jnp.mean(second_wide * second_wide, axis=-1, keepdims=True) + norm_eps)
    normed = (second_wide * norm_gain * scale_values).astype(jnp.bfloat16)
    flat_rows = normed.reshape(-1, channel_total)
    hidden = jax.nn.gelu(
        jnp.dot(flat_rows, expand_weight, preferred_element_type=jnp.float32)
    ).astype(jnp.bfloat16)
    update = jnp.dot(hidden, reduce_weight, preferred_element_type=jnp.float32)
    block_output = (second_wide.reshape(-1, channel_total) + update).astype(jnp.bfloat16)
    return block_output.reshape(lat_rows, sector_width, channel_total)


def legendre_constant(lat_total, mode_count):
    colatitude = (np.arange(lat_total // 2) + 0.5) * (math.pi / lat_total)
    cosines, sines = np.cos(colatitude)[:, None], np.sin(colatitude)[:, None]
    orders = np.arange(mode_count, dtype=np.float64)
    ranks = np.arange(1, mode_count, dtype=np.float64)
    log_terms = 0.5 * np.log((2.0 * ranks + 1.0) / (2.0 * ranks))
    log_norm = np.concatenate([np.zeros(1), np.cumsum(log_terms)])
    log_start = -0.5 * math.log(4.0 * math.pi) + log_norm + orders * np.log(sines)
    start = np.where(
        log_start > underflow_cut, np.exp(np.maximum(log_start, underflow_cut)), 0.0
    )
    table = np.zeros((lat_total // 2, mode_count, mode_count))
    previous = np.zeros_like(start)
    earlier = np.zeros_like(start)
    for degree in range(mode_count):
        raised = np.sqrt(
            np.maximum(4.0 * degree * degree - 1.0, 0.0)
            / np.maximum(degree * degree - orders * orders, 1.0)
        )
        lowered = np.sqrt(
            np.maximum((degree - 1.0) ** 2 - orders * orders, 0.0)
            / max(4.0 * (degree - 1.0) ** 2 - 1.0, 1.0)
        )
        recurred = raised * (cosines * previous - lowered * earlier)
        current = np.where(degree < orders, 0.0, np.where(degree == orders, start, recurred))
        earlier, previous = previous, current
        table[:, degree, :] = current
    return table


def parity_tables(lat_total, mode_count):
    table = legendre_constant(lat_total, mode_count)
    return np.stack([table[:, :, 0::2], table[:, :, 1::2]]).astype(jnp.bfloat16)


def analysis_constant(sectors, width, span, mode_count):
    lon_total = sectors * width
    out = np.zeros((2, sectors, span, 2, mode_count // 2))
    for parity in range(2):
        modes = np.arange(parity, mode_count, 2)
        for sector in range(sectors):
            longitudes = sector * width + np.arange(width)
            angles = (longitudes[:, None] * modes[None, :] % lon_total) * (2 * math.pi / lon_total)
            out[parity, sector, :width, 0] = np.cos(angles) / lon_total
            out[parity, sector, :width, 1] = -np.sin(angles) / lon_total
    return out.reshape(2, sectors, span, mode_count).astype(jnp.bfloat16)


def synthesis_constant(sectors, width, padded, mode_count):
    lon_total = sectors * width
    out = np.zeros((sectors, 2, 2, padded, 2, mode_count // 2))
    for sector in range(sectors):
        longitudes = sector * width + np.arange(width)
        for half in range(2):
            modes = np.arange((sector + half) % 2, mode_count, 2)
            doubling = np.where(modes == 0, 1.0, 2.0)[None, :]
            angles = (longitudes[:, None] * modes[None, :] % lon_total) * (2 * math.pi / lon_total)
            cosine, sine = doubling * np.cos(angles), doubling * np.sin(angles)
            out[sector, half, 0, :width, 0] = cosine
            out[sector, half, 0, :width, 1] = -sine
            out[sector, half, 1, :width, 0] = sine
            out[sector, half, 1, :width, 1] = cosine
    return out.reshape(sectors, 2, 2 * padded, mode_count).astype(jnp.bfloat16)


def gelu(value):
    inner = value * (0.7978845608028654 + (0.7978845608028654 * 0.044715) * (value * value))
    half = 0.5 * value
    return half + half * jnp.tanh(inner)


def pack_body(chips, share, width, grid_ref, out_ref, wide_ref):
    span = wide_ref.shape[1]
    tail = width // 8 * 8
    flipped = []
    for row in range(2):
        wide_ref[row, tail:span, :] = jnp.zeros((span - tail, chips * share), jnp.float32)
        wide_ref[row, 0:width, :] = grid_ref[row].astype(jnp.float32)
        flipped.append(wide_ref[row].T)
    rest = flipped[0][:, LANES:] + pltpu.roll(flipped[1][:, LANES:], width - LANES, axis=1)
    for chip in range(chips):
        at = slice(chip * share, (chip + 1) * share)
        block = jnp.concatenate(
            [flipped[0][at, :LANES], flipped[1][at, :LANES], rest[at]], axis=0
        )
        out_ref[chip] = block.astype(jnp.bfloat16)


def spectral_body(
    lat_count, columns, share, width,
    parity_ref, own_ref, other_ref, gain_ref, tap_ref, legendre_ref, table_ref, out_ref,
    field_ref, first_ref, modes_ref,
):
    lat_total = 2 * lat_count
    north = lat_total // 2
    sectors = 2 * columns
    edge = width - LANES
    orders = legendre_ref.shape[2]
    parity = parity_ref[0]
    for source, core in ((own_ref, parity), (other_ref, 1 - parity)):
        for column in range(columns):
            sector = 2 * column + core
            for band in range(lat_count):
                block = source[column * lat_count + band].astype(jnp.float32)
                rest = block[2 * share :]
                field_ref[sector, 2 * band, :, 0:LANES] = block[:share]
                field_ref[sector, 2 * band, :, LANES:] = rest
                field_ref[sector, 2 * band + 1, :, 0:LANES] = block[share : 2 * share]
                field_ref[sector, 2 * band + 1, :, LANES:] = pltpu.roll(rest, LANES - edge, axis=1)

    lane = lax.broadcasted_iota(jnp.int32, (8, LANES), 1)

    def filter_sector(sector, unused):
        after = lax.rem(sector + 1, sectors)
        before = lax.rem(sector + sectors - 1, sectors)

        def filter_rows(tile, unused):
            rows = pl.ds(pl.multiple_of(tile * 8, 8), 8)
            taps = []
            for k in range(9):
                tap = tap_ref[k, rows, :]
                taps.append(jnp.concatenate([tap, tap], axis=1))
            held, total, ahead = None, None, None

            def finish(t, value, sum_):
                first_ref[sector, pl.ds(pl.multiple_of(t * share + tile * 8, 8), 8), :] = value + gelu(sum_)

            for t in range(lat_total):
                low = field_ref[sector, t, rows, 0:LANES]
                high = field_ref[sector, t, rows, LANES:]
                right = pltpu.roll(field_ref[after, t, rows, 0:LANES], edge, axis=1)
                left = pltpu.roll(field_ref[before, t, rows, LANES:], LANES - edge, axis=1)
                high = jnp.where(lane == edge, right, jnp.where(lane == LANES - 1, left, high))
                value = jnp.concatenate([low, high], axis=1)
                west = pltpu.roll(value, 1, axis=1)
                east = pltpu.roll(value, 2 * LANES - 1, axis=1)

                def weigh(row):
                    return (
                        taps[3 * row] * west + taps[3 * row + 1] * value + taps[3 * row + 2] * east
                    )

                if t > 0:
                    finish(t - 1, held, total + weigh(2))
                total = weigh(1) if t == 0 else ahead + weigh(1)
                ahead = weigh(0)
                held = value
            finish(lat_total - 1, held, total)
            return unused

        return lax.fori_loop(0, share // 8, filter_rows, unused)

    lax.fori_loop(0, sectors, filter_sector, 0)

    modes = None
    for sector in range(sectors):
        part = jnp.dot(
            first_ref[sector].astype(jnp.bfloat16),
            table_ref[sector],
            preferred_element_type=jnp.float32,
        )
        modes = part if modes is None else modes + part
    modes_ref[...] = modes

    sign = (1 - 2 * parity).astype(jnp.float32)
    folded = [[], []]
    for t in range(north):
        weight = 2.0 * math.pi * math.pi / lat_total * math.sin(math.pi * (t + 0.5) / lat_total)
        upper = weight * modes_ref[t * share : (t + 1) * share, :]
        mirror = lat_total - 1 - t
        lower = (weight * sign) * modes_ref[mirror * share : (mirror + 1) * share, :]
        folded[0].append(upper + lower)
        folded[1].append(upper - lower)

    sums = [[None] * north, [None] * north]

    def add(half, t, kernel, value):
        real = kernel[0] * value[:, :orders] - kernel[1] * value[:, orders:]
        imag = kernel[0] * value[:, orders:] + kernel[1] * value[:, :orders]
        had = sums[half][t]
        sums[half][t] = (real, imag) if had is None else (had[0] + real, had[1] + imag)

    for t in range(north):
        products = jnp.concatenate(
            [legendre_ref[t] * legendre_ref[s] for s in range(t, north)], axis=1
        )
        kernels = jnp.dot(gain_ref[...], products, preferred_element_type=jnp.float32)
        for s in range(t, north):
            at = slice((s - t) * orders, (s - t + 1) * orders)
            for half in range(2):
                base = 2 * half * share
                kernel = (kernels[base : base + share, at], kernels[base + share : base + 2 * share, at])
                add(half, t, kernel, folded[half][s])
                if s != t:
                    add(half, s, kernel, folded[half][t])

    for t in range(north):
        for part in range(2):
            even, odd = sums[0][t][part], sums[1][t][part]
            for place, value in ((t, even + odd), (lat_total - 1 - t, sign * (even - odd))):
                at = (place % 2) * 2 * orders + part * orders
                value = value.astype(jnp.bfloat16)
                for column in range(columns):
                    out_ref[column, place // 2, :, at : at + orders] = value


def finish_body(
    width, padded,
    own_ref, other_ref, table_ref, mix_ref, first_ref, gain_ref, expand_ref, reduce_ref, out_ref,
):
    contract_last = (((1,), (1,)), ((), ()))
    modes = table_ref.shape[2]
    real, imag = [], []
    for row in range(2):
        at = slice(row * modes, (row + 1) * modes)
        field = lax.dot_general(
            table_ref[0], own_ref[:, at], contract_last, preferred_element_type=jnp.float32
        ) + lax.dot_general(
            table_ref[1], other_ref[:, at], contract_last, preferred_element_type=jnp.float32
        )
        real.append(field[:padded])
        imag.append(field[padded:])
    real = jnp.concatenate(real, axis=0).astype(jnp.bfloat16)
    imag = jnp.concatenate(imag, axis=0).astype(jnp.bfloat16)
    spectral_out = jnp.dot(real, mix_ref[0], preferred_element_type=jnp.float32) - jnp.dot(
        imag, mix_ref[1], preferred_element_type=jnp.float32
    )
    second = (first_ref[...].astype(jnp.float32) + spectral_out).astype(jnp.bfloat16)
    wide = second.astype(jnp.float32)
    scale = lax.rsqrt(jnp.mean(wide * wide, axis=-1, keepdims=True) + norm_eps)
    normed = (wide * gain_ref[...] * scale).astype(jnp.bfloat16)
    hidden = gelu(jnp.dot(normed, expand_ref[...], preferred_element_type=jnp.float32))
    update = jnp.dot(
        hidden.astype(jnp.bfloat16), reduce_ref[...], preferred_element_type=jnp.float32
    )
    result = wide + update
    for row in range(2):
        out_ref[row] = result[row * padded : row * padded + width].astype(jnp.bfloat16)


def in_vmem(count):
    return [pl.BlockSpec(memory_space=pltpu.VMEM)] * count


def chip_shards(
    grid_state, conv_weight, spectral_gain, spectral_weight, norm_gain, expand_weight, reduce_weight
):
    lat_rows, width, channels = grid_state.shape
    lat_count, columns = lax.axis_size("lat"), lax.axis_size("x")
    chips, sectors = lat_count * columns, 2 * columns
    share = channels // chips
    lat_total = lat_rows * lat_count
    orders = M // 2
    span = 2 * LANES
    padded = -(-width // 8) * 8
    lat_at, column, core = lax.axis_index("lat"), lax.axis_index("x"), lax.axis_index("core")
    swap = [(0, 1), (1, 0)]
    over_chips = ("x", "lat")

    packed = pl.pallas_call(
        functools.partial(pack_body, chips, share, width),
        out_shape=jax.ShapeDtypeStruct((chips, 3 * share, LANES), jnp.bfloat16),
        in_specs=in_vmem(1),
        out_specs=in_vmem(1)[0],
        scratch_shapes=[pltpu.VMEM((2, span, channels), jnp.float32)],
        compiler_params=pltpu.CompilerParams(vmem_limit_bytes=24 << 20),
        name="pack",
    )(grid_state)
    own = lax.all_to_all(packed, over_chips, split_axis=0, concat_axis=0, tiled=True)
    other = lax.ppermute(own, "core", swap)

    lons = ("x", "core")
    wrapped = padded_2(grid_state, ((lons, 1),), 1, True)
    halo = padded_2(wrapped, (("lat", 0),), 1, False).astype(jnp.float32)
    filtered = jnp.zeros(grid_state.shape, jnp.float32)
    for row_shift in range(3):
        for col_shift in range(3):
            filtered = (
                filtered
                + conv_weight[row_shift, col_shift]
                * halo[row_shift : row_shift + lat_rows, col_shift : col_shift + width]
            )
    first_section = (grid_state.astype(jnp.float32) + jax.nn.gelu(filtered)).astype(jnp.bfloat16)
    first_rows = jnp.pad(first_section, ((0, 0), (0, padded - width), (0, 0))).reshape(-1, channels)

    held = spectral_weight.shape[2]
    across = lax.ppermute(spectral_weight, "x", [(i, (i + 1) % columns) for i in range(columns)])
    pair = jnp.where(
        column == 0, jnp.stack([spectral_weight, across]), jnp.stack([across, spectral_weight])
    )
    pair_other = lax.ppermute(pair, "core", swap)
    quad = jnp.where(
        core == 0,
        jnp.stack([pair, pair_other], axis=1),
        jnp.stack([pair_other, pair], axis=1),
    )
    mixing = jnp.concatenate(
        [quad[i, j] for i in range(columns) for j in range(2)], axis=2
    )

    blocks = held // share
    piece = lax.dynamic_slice_in_dim(
        spectral_gain, (lat_at % blocks) * share, share, axis=2
    ).transpose(0, 2, 1)
    piece_other = lax.ppermute(piece, "core", swap)
    gains = jnp.where(core == lat_at // blocks, piece, piece_other)
    even = (jnp.arange(M) % 2 == 0)[None, :]
    gain_rows = jnp.concatenate(
        [
            jnp.where(even, gains[0], 0.0),
            jnp.where(even, gains[1], 0.0),
            jnp.where(even, 0.0, gains[0]),
            jnp.where(even, 0.0, gains[1]),
        ],
        axis=0,
    ).astype(jnp.bfloat16)
    chip = column * lat_count + lat_at
    taps = lax.dynamic_slice_in_dim(conv_weight.reshape(9, channels), chip * share, share, axis=1)
    taps = jnp.broadcast_to(taps[:, :, None], (9, share, LANES))

    legendre = lax.dynamic_index_in_dim(
        jnp.asarray(parity_tables(lat_total, M)), core, 0, keepdims=False
    )
    analysis = lax.dynamic_index_in_dim(
        jnp.asarray(analysis_constant(sectors, width, span, M)), core, 0, keepdims=False
    )
    synthesis = lax.dynamic_index_in_dim(
        jnp.asarray(synthesis_constant(sectors, width, padded, M)),
        2 * column + core, 0, keepdims=False,
    )

    bands = pl.pallas_call(
        functools.partial(spectral_body, lat_count, columns, share, width),
        out_shape=jax.ShapeDtypeStruct((columns, lat_count, share, 2 * M), jnp.bfloat16),
        in_specs=[pl.BlockSpec(memory_space=pltpu.SMEM)] + in_vmem(6),
        out_specs=in_vmem(1)[0],
        scratch_shapes=[
            pltpu.VMEM((sectors, lat_total, share, span), jnp.float32),
            pltpu.VMEM((sectors, lat_total * share, span), jnp.float32),
            pltpu.VMEM((lat_total * share, M), jnp.float32),
        ],
        compiler_params=pltpu.CompilerParams(vmem_limit_bytes=40 << 20),
        name="spectral",
    )(core[None], own, other, gain_rows, taps, legendre, analysis)
    back = lax.all_to_all(
        bands.reshape(chips, share, 2 * M), over_chips, split_axis=0, concat_axis=0, tiled=True
    ).reshape(channels, 2 * M)
    back_other = lax.ppermute(back, "core", swap)

    return pl.pallas_call(
        functools.partial(finish_body, width, padded),
        out_shape=jax.ShapeDtypeStruct(grid_state.shape, jnp.bfloat16),
        in_specs=in_vmem(8),
        out_specs=in_vmem(1)[0],
        compiler_params=pltpu.CompilerParams(vmem_limit_bytes=40 << 20),
        name="finish",
    )(
        back, back_other, synthesis, mixing, first_rows, norm_gain[None, :],
        expand_weight, reduce_weight,
    )


def solution(mesh):
    lat_count, lon_count = mesh.shape["lat"], mesh.shape["lon"]
    columns = lon_count // 2
    cored = Mesh(mesh.devices.reshape(lat_count, columns, 2), ("lat", "x", "core"))

    def run(grid_state, *rest):
        lat_total, lon_total, channels = grid_state.shape
        chips = lat_count * columns
        width = lon_total // lon_count
        fits = (
            columns == 2
            and lat_total == 2 * lat_count
            and lat_total <= 32
            and channels % (8 * chips) == 0
            and lat_count % 2 == 0
            and (channels // lon_count) * 2 == (channels // chips) * lat_count
            and LANES + 2 <= width
            and 2 * (width - LANES) <= LANES
        )
        if fits:
            body, on, lat, lon = chip_shards, cored, "lat", ("x", "core")
        else:
            body, on, lat, lon = banded_shards, mesh, "lat", "lon"
        return jax.shard_map(
            body,
            mesh=on,
            in_specs=(
                P(lat, lon, None), P(), P(None, None, lon), P(None, None, lon), P(), P(), P(),
            ),
            out_specs=P(lat, lon, None),
            check_vma=False,
        )(grid_state, *rest)

    return run
```

```python
import functools
import math

import jax
import jax.numpy as jnp
import numpy as np
from jax import lax
from jax.experimental import pallas as pl
from jax.experimental.pallas import tpu as pltpu
from jax.sharding import Mesh
from jax.sharding import PartitionSpec as P

M = 256
LANES = 128


norm_eps = 1e-06
underflow_cut = -60.0
degree_block = 16


def padded_2(value, sides, width, wrap):
    for axis, dim in sides:
        count, length = (lax.axis_size(axis), value.shape[dim])
        up = [(i, (i + 1) % count) for i in range(count if wrap else count - 1)]
        down = [(j, i) for i, j in up]
        last = lax.slice_in_dim(value, length - width, length, axis=dim)
        initial = lax.slice_in_dim(value, 0, width, axis=dim)
        before = lax.ppermute(last, axis, up)
        after = lax.ppermute(initial, axis, down)
        value = jnp.concatenate([before, value, after], axis=dim)
    return value


def legendre_table(orders, lat_total, degree_count):
    colatitude = (jnp.arange(lat_total, dtype=jnp.float32) + 0.5) * (math.pi / lat_total)
    cosines = jnp.cos(colatitude)
    sine_values = jnp.sin(colatitude)
    rank_values = jnp.arange(1, degree_count + 1, dtype=jnp.int32)
    rank_float = rank_values.astype(jnp.float32)
    log_terms = 0.5 * jnp.log((2.0 * rank_float + 1.0) / (2.0 * rank_float))
    log_norm = jnp.sum(
        jnp.where(rank_values[None, :] <= orders[:, None], log_terms[None, :], jnp.float32(0.0)),
        axis=1,
    )
    order_float = orders.astype(jnp.float32)[:, None]
    log_start = (
        -0.5 * math.log(4.0 * math.pi)
        + log_norm[:, None]
        + order_float * jnp.log(sine_values)[None, :]
    )
    start_value = jnp.where(
        log_start > underflow_cut, jnp.exp(jnp.maximum(log_start, underflow_cut)), jnp.float32(0.0)
    )

    def advance_block(totals, block_start):
        previous, earlier = totals
        rows_out = []
        for inner in range(degree_block):
            degree = block_start + inner
            degree_float = degree.astype(jnp.float32)
            raise_coef = jnp.sqrt(
                jnp.maximum(4.0 * degree_float * degree_float - 1.0, 0.0)
                / jnp.maximum(degree_float * degree_float - order_float * order_float, 1.0)
            )
            lower_coef = jnp.sqrt(
                jnp.maximum((degree_float - 1.0) ** 2 - order_float * order_float, 0.0)
                / jnp.maximum(4.0 * (degree_float - 1.0) ** 2 - 1.0, 1.0)
            )
            recurred = raise_coef * (cosines[None, :] * previous - lower_coef * earlier)
            current = jnp.where(
                degree < orders[:, None],
                jnp.float32(0.0),
                jnp.where(degree == orders[:, None], start_value, recurred),
            )
            earlier = previous
            previous = current
            rows_out.append(current)
        return ((previous, earlier), jnp.stack(rows_out, axis=0))

    blank = jnp.zeros((orders.shape[0], lat_total), jnp.float32)
    starts = jnp.arange(0, degree_count, degree_block, dtype=jnp.int32)
    unused, table_blocks = lax.scan(advance_block, (blank, blank), starts)
    return table_blocks.reshape(degree_count, orders.shape[0], lat_total)


def quadrature(lat_total):
    colatitude = (jnp.arange(lat_total, dtype=jnp.float32) + 0.5) * (math.pi / lat_total)
    return 2.0 * math.pi * math.pi / lat_total * jnp.sin(colatitude)


def fourier_table(longitudes, lon_total, mode_count):
    mode_index = jnp.arange(mode_count, dtype=jnp.int32)
    phase_index = longitudes[:, None] * mode_index[None, :] % lon_total
    angles = phase_index.astype(jnp.float32) * (2.0 * math.pi / lon_total)
    return (jnp.stack([jnp.cos(angles), -jnp.sin(angles)], axis=1) / lon_total).astype(jnp.bfloat16)


def synthesis_table(longitudes, lon_total, mode_count):
    mode_index = jnp.arange(mode_count, dtype=jnp.int32)
    phase_index = mode_index[:, None] * longitudes[None, :] % lon_total
    angles = phase_index.astype(jnp.float32) * (2.0 * math.pi / lon_total)
    doubling = jnp.where(mode_index == 0, 1.0, 2.0).astype(jnp.float32)[:, None]
    return jnp.stack([doubling * jnp.cos(angles), -doubling * jnp.sin(angles)], axis=0).astype(
        jnp.bfloat16
    )


def banded_shards(
    grid_state, conv_weight, spectral_gain, spectral_weight, norm_gain, expand_weight, reduce_weight
):
    lat_rows, sector_width, channel_total = grid_state.shape
    lat_count = lax.axis_size("lat")
    lon_count = lax.axis_size("lon")
    lat_total = lat_rows * lat_count
    lon_total = sector_width * lon_count
    mode_count = M
    order_share = mode_count // lat_count
    channel_share = channel_total // lon_count
    lat_position = lax.axis_index("lat")
    wrapped = padded_2(grid_state, (("lon", 1),), 1, True)
    padded = padded_2(wrapped, (("lat", 0),), 1, False)
    padded_wide = padded.astype(jnp.float32)
    filtered = jnp.zeros((lat_rows, sector_width, channel_total), jnp.float32)
    for row_shift in range(3):
        for col_shift in range(3):
            filtered = (
                filtered
                + conv_weight[row_shift, col_shift]
                * padded_wide[
                    row_shift : row_shift + lat_rows, col_shift : col_shift + sector_width
                ]
            )
    first_section = (grid_state.astype(jnp.float32) + jax.nn.gelu(filtered)).astype(jnp.bfloat16)
    gathered = lax.all_to_all(first_section, "lon", split_axis=2, concat_axis=1, tiled=True)
    forward_table = fourier_table(jnp.arange(lon_total, dtype=jnp.int32), lon_total, mode_count)
    spectrum = jnp.einsum(
        "tpc,prm->tmrc", gathered, forward_table, preferred_element_type=jnp.float32
    ).astype(jnp.bfloat16)
    cycle_spectrum = lax.all_to_all(spectrum, "lat", split_axis=1, concat_axis=0, tiled=True)
    orders = lat_position * order_share + jnp.arange(order_share, dtype=jnp.int32)
    legendre = legendre_table(orders, lat_total, mode_count)
    analysis_table = (legendre * quadrature(lat_total)[None, None, :]).astype(jnp.bfloat16)
    coefficients = jnp.einsum(
        "lmt,tmrc->lmrc", analysis_table, cycle_spectrum, preferred_element_type=jnp.float32
    )
    gain_real = spectral_gain[0][:, None, :]
    gain_imag = spectral_gain[1][:, None, :]
    coef_real = coefficients[:, :, 0, :]
    coef_imag = coefficients[:, :, 1, :]
    gained = jnp.stack(
        [
            gain_real * coef_real - gain_imag * coef_imag,
            gain_real * coef_imag + gain_imag * coef_real,
        ],
        axis=2,
    ).astype(jnp.bfloat16)
    blank = jnp.zeros((mode_count * order_share, channel_share), jnp.float32)
    portion = lax.all_gather(gained, "lon", axis=3, tiled=True)
    width_part = portion.shape[3]
    weight_rows = lax.slice_in_dim(spectral_weight, 0, width_part, axis=1)
    real_part = portion[:, :, 0, :].reshape(-1, width_part)
    imag_part = portion[:, :, 1, :].reshape(-1, width_part)
    real_sum = (
        blank
        + jnp.dot(real_part, weight_rows[0], preferred_element_type=jnp.float32)
        - jnp.dot(imag_part, weight_rows[1], preferred_element_type=jnp.float32)
    )
    imag_sum = (
        blank
        + jnp.dot(real_part, weight_rows[1], preferred_element_type=jnp.float32)
        + jnp.dot(imag_part, weight_rows[0], preferred_element_type=jnp.float32)
    )
    mixed = jnp.stack(
        [
            real_sum.reshape(mode_count, order_share, channel_share),
            imag_sum.reshape(mode_count, order_share, channel_share),
        ],
        axis=2,
    ).astype(jnp.bfloat16)
    synthesis_legendre = legendre.astype(jnp.bfloat16)
    cycle_modes = jnp.einsum(
        "lmt,lmrc->tmrc", synthesis_legendre, mixed, preferred_element_type=jnp.float32
    ).astype(jnp.bfloat16)
    band_modes = lax.all_to_all(cycle_modes, "lat", split_axis=0, concat_axis=1, tiled=True)
    inverse_table = synthesis_table(jnp.arange(lon_total, dtype=jnp.int32), lon_total, mode_count)
    all_lons = jnp.einsum(
        "tmrc,rmp->tpc", band_modes, inverse_table, preferred_element_type=jnp.float32
    )
    spectral_out = lax.all_to_all(
        all_lons.astype(jnp.bfloat16), "lon", split_axis=1, concat_axis=2, tiled=True
    ).astype(all_lons.dtype)
    second_section = (first_section.astype(jnp.float32) + spectral_out).astype(jnp.bfloat16)
    second_wide = second_section.astype(jnp.float32)
    scale_values = lax.rsqrt(jnp.mean(second_wide * second_wide, axis=-1, keepdims=True) + norm_eps)
    normed = (second_wide * norm_gain * scale_values).astype(jnp.bfloat16)
    flat_rows = normed.reshape(-1, channel_total)
    hidden = jax.nn.gelu(
        jnp.dot(flat_rows, expand_weight, preferred_element_type=jnp.float32)
    ).astype(jnp.bfloat16)
    update = jnp.dot(hidden, reduce_weight, preferred_element_type=jnp.float32)
    block_output = (second_wide.reshape(-1, channel_total) + update).astype(jnp.bfloat16)
    return block_output.reshape(lat_rows, sector_width, channel_total)


contract_last = (((1,), (1,)), ((), ()))


def legendre_constant(lat_total, mode_count):
    colatitude = (np.arange(lat_total // 2) + 0.5) * (math.pi / lat_total)
    cosines, sines = np.cos(colatitude)[:, None], np.sin(colatitude)[:, None]
    orders = np.arange(mode_count, dtype=np.float64)
    ranks = np.arange(1, mode_count, dtype=np.float64)
    log_terms = 0.5 * np.log((2.0 * ranks + 1.0) / (2.0 * ranks))
    log_norm = np.concatenate([np.zeros(1), np.cumsum(log_terms)])
    log_start = -0.5 * math.log(4.0 * math.pi) + log_norm + orders * np.log(sines)
    start = np.where(
        log_start > underflow_cut, np.exp(np.maximum(log_start, underflow_cut)), 0.0
    )
    table = np.zeros((lat_total // 2, mode_count, mode_count))
    previous = np.zeros_like(start)
    earlier = np.zeros_like(start)
    for degree in range(mode_count):
        raised = np.sqrt(
            np.maximum(4.0 * degree * degree - 1.0, 0.0)
            / np.maximum(degree * degree - orders * orders, 1.0)
        )
        lowered = np.sqrt(
            np.maximum((degree - 1.0) ** 2 - orders * orders, 0.0)
            / max(4.0 * (degree - 1.0) ** 2 - 1.0, 1.0)
        )
        recurred = raised * (cosines * previous - lowered * earlier)
        current = np.where(degree < orders, 0.0, np.where(degree == orders, start, recurred))
        earlier, previous = previous, current
        table[:, degree, :] = current
    return table


def parity_tables(lat_total, mode_count):
    table = legendre_constant(lat_total, mode_count)
    return np.stack([table[:, :, 0::2], table[:, :, 1::2]]).astype(jnp.bfloat16)


def analysis_constant(sectors, width, span, mode_count):
    lon_total = sectors * width
    out = np.zeros((2, sectors, span, 2, mode_count // 2))
    for parity in range(2):
        modes = np.arange(parity, mode_count, 2)
        for sector in range(sectors):
            longitudes = sector * width + np.arange(width)
            angles = (longitudes[:, None] * modes[None, :] % lon_total) * (2 * math.pi / lon_total)
            out[parity, sector, :width, 0] = np.cos(angles) / lon_total
            out[parity, sector, :width, 1] = -np.sin(angles) / lon_total
    return out.reshape(2, sectors, span, mode_count).astype(jnp.bfloat16)


def synthesis_constant(sectors, width, padded, mode_count):
    lon_total = sectors * width
    out = np.zeros((sectors, 2, 2, padded, 2, mode_count // 2))
    for sector in range(sectors):
        longitudes = sector * width + np.arange(width)
        for half in range(2):
            modes = np.arange((sector + half) % 2, mode_count, 2)
            doubling = np.where(modes == 0, 1.0, 2.0)[None, :]
            angles = (longitudes[:, None] * modes[None, :] % lon_total) * (2 * math.pi / lon_total)
            cosine, sine = doubling * np.cos(angles), doubling * np.sin(angles)
            out[sector, half, 0, :width, 0] = cosine
            out[sector, half, 0, :width, 1] = -sine
            out[sector, half, 1, :width, 0] = sine
            out[sector, half, 1, :width, 1] = cosine
    return out.reshape(sectors, 2, 2 * padded, mode_count).astype(jnp.bfloat16)


def gelu(value):
    inner = value * (0.7978845608028654 + (0.7978845608028654 * 0.044715) * (value * value))
    half = 0.5 * value
    return half + half * jnp.tanh(inner)


def pack_body(chips, share, width, grid_ref, out_ref, wide_ref):
    span = wide_ref.shape[1]
    tail = width // 8 * 8
    flipped = []
    for row in range(2):
        wide_ref[row, tail:span, :] = jnp.zeros((span - tail, chips * share), jnp.float32)
        wide_ref[row, 0:width, :] = grid_ref[row].astype(jnp.float32)
        flipped.append(wide_ref[row].T)
    rest = flipped[0][:, LANES:] + pltpu.roll(flipped[1][:, LANES:], width - LANES, axis=1)
    for chip in range(chips):
        at = slice(chip * share, (chip + 1) * share)
        block = jnp.concatenate(
            [flipped[0][at, :LANES], flipped[1][at, :LANES], rest[at]], axis=0
        )
        out_ref[chip] = block.astype(jnp.bfloat16)


def spectral_body(
    lat_count, columns, share, width,
    parity_ref, own_ref, other_any, gain_ref, tap_ref, legendre_ref, table_ref, out_ref,
    field_ref, first_ref, modes_ref, other_ref, sem,
):
    lat_total = 2 * lat_count
    north = lat_total // 2
    sectors = 2 * columns
    edge = width - LANES
    orders = legendre_ref.shape[2]
    parity = parity_ref[0]
    arrival = pltpu.make_async_copy(other_any, other_ref, sem)
    arrival.start()
    for source, core in ((own_ref, parity), (other_ref, 1 - parity)):
        if source is other_ref:
            arrival.wait()
        for column in range(columns):
            sector = 2 * column + core
            for band in range(lat_count):
                block = source[column * lat_count + band].astype(jnp.float32)
                rest = block[2 * share :]
                field_ref[sector, 2 * band, :, 0:LANES] = block[:share]
                field_ref[sector, 2 * band, :, LANES:] = rest
                field_ref[sector, 2 * band + 1, :, 0:LANES] = block[share : 2 * share]
                field_ref[sector, 2 * band + 1, :, LANES:] = pltpu.roll(rest, LANES - edge, axis=1)

    lane = lax.broadcasted_iota(jnp.int32, (8, LANES), 1)

    def filter_sector(sector, unused):
        after = lax.rem(sector + 1, sectors)
        before = lax.rem(sector + sectors - 1, sectors)

        def filter_rows(tile, unused):
            rows = pl.ds(pl.multiple_of(tile * 8, 8), 8)
            taps = []
            for k in range(9):
                tap = tap_ref[k, rows, :]
                taps.append(jnp.concatenate([tap, tap], axis=1))
            held, total, ahead = None, None, None

            def finish(t, value, sum_):
                first_ref[sector, pl.ds(pl.multiple_of(t * share + tile * 8, 8), 8), :] = value + gelu(sum_)

            for t in range(lat_total):
                low = field_ref[sector, t, rows, 0:LANES]
                high = field_ref[sector, t, rows, LANES:]
                right = pltpu.roll(field_ref[after, t, rows, 0:LANES], edge, axis=1)
                left = pltpu.roll(field_ref[before, t, rows, LANES:], LANES - edge, axis=1)
                high = jnp.where(lane == edge, right, jnp.where(lane == LANES - 1, left, high))
                value = jnp.concatenate([low, high], axis=1)
                west = pltpu.roll(value, 1, axis=1)
                east = pltpu.roll(value, 2 * LANES - 1, axis=1)

                def weigh(row):
                    return (
                        taps[3 * row] * west + taps[3 * row + 1] * value + taps[3 * row + 2] * east
                    )

                if t > 0:
                    finish(t - 1, held, total + weigh(2))
                total = weigh(1) if t == 0 else ahead + weigh(1)
                ahead = weigh(0)
                held = value
            finish(lat_total - 1, held, total)
            return unused

        return lax.fori_loop(0, share // 8, filter_rows, unused)

    lax.fori_loop(0, sectors, filter_sector, 0)

    modes = None
    for sector in range(sectors):
        part = jnp.dot(
            first_ref[sector].astype(jnp.bfloat16),
            table_ref[sector],
            preferred_element_type=jnp.float32,
        )
        modes = part if modes is None else modes + part
    modes_ref[...] = modes

    sign = (1 - 2 * parity).astype(jnp.float32)
    folded = [[], []]
    for t in range(north):
        weight = 2.0 * math.pi * math.pi / lat_total * math.sin(math.pi * (t + 0.5) / lat_total)
        upper = weight * modes_ref[t * share : (t + 1) * share, :]
        mirror = lat_total - 1 - t
        lower = (weight * sign) * modes_ref[mirror * share : (mirror + 1) * share, :]
        folded[0].append(upper + lower)
        folded[1].append(upper - lower)

    sums = [[None] * north, [None] * north]

    def add(half, t, kernel, value):
        real = kernel[0] * value[:, :orders] - kernel[1] * value[:, orders:]
        imag = kernel[0] * value[:, orders:] + kernel[1] * value[:, :orders]
        had = sums[half][t]
        sums[half][t] = (real, imag) if had is None else (had[0] + real, had[1] + imag)

    for t in range(north):
        products = jnp.concatenate(
            [legendre_ref[t] * legendre_ref[s] for s in range(t, north)], axis=1
        )
        kernels = jnp.dot(gain_ref[...], products, preferred_element_type=jnp.float32)
        for s in range(t, north):
            at = slice((s - t) * orders, (s - t + 1) * orders)
            for half in range(2):
                base = 2 * half * share
                kernel = (kernels[base : base + share, at], kernels[base + share : base + 2 * share, at])
                add(half, t, kernel, folded[half][s])
                if s != t:
                    add(half, s, kernel, folded[half][t])

    for t in range(north):
        for part in range(2):
            even, odd = sums[0][t][part], sums[1][t][part]
            for place, value in ((t, even + odd), (lat_total - 1 - t, sign * (even - odd))):
                at = (place % 2) * 2 * orders + part * orders
                value = value.astype(jnp.bfloat16)
                for column in range(columns):
                    out_ref[column, place // 2, :, at : at + orders] = value


def stage_body(
    place_ref, own_ref, table_ref,
    mix_a_ref, mix_b_ref, mix_c_ref, mix_d_ref,
    field_ref, mix_ref, sems,
):
    place = place_ref[0]
    held = mix_a_ref.shape[1]
    loads = []
    for k, source in enumerate((mix_a_ref, mix_b_ref, mix_c_ref, mix_d_ref)):
        sector = 2 * (place // 2 if k < 2 else 1 - place // 2) + (
            place % 2 if k % 2 == 0 else 1 - place % 2
        )
        rows = pl.ds(pl.multiple_of(sector * held, held), held)
        loads.append(pltpu.make_async_copy(source, mix_ref.at[:, rows, :], sems.at[k]))
    for load in loads:
        load.start()
    modes = table_ref.shape[2]
    for row in range(2):
        field_ref[row] = lax.dot_general(
            table_ref[0], own_ref[:, row * modes : (row + 1) * modes], contract_last,
            preferred_element_type=jnp.float32,
        )
    for load in loads:
        load.wait()


def finish_body(
    width, padded,
    field_ref, other_ref, first_ref, gain_ref, table_ref, mix_ref, expand_ref, reduce_ref,
    marker_ref, out_ref,
):
    modes = table_ref.shape[2]
    real, imag = [], []
    for row in range(2):
        field = field_ref[row] + lax.dot_general(
            table_ref[1], other_ref[:, row * modes : (row + 1) * modes], contract_last,
            preferred_element_type=jnp.float32,
        )
        real.append(field[:padded])
        imag.append(field[padded:])
    real = jnp.concatenate(real, axis=0).astype(jnp.bfloat16)
    imag = jnp.concatenate(imag, axis=0).astype(jnp.bfloat16)
    spectral_out = lax.dot_general(
        real, mix_ref[0], contract_last, preferred_element_type=jnp.float32
    ) - lax.dot_general(imag, mix_ref[1], contract_last, preferred_element_type=jnp.float32)
    second = (first_ref[...].astype(jnp.float32) + spectral_out).astype(jnp.bfloat16)
    wide = second.astype(jnp.float32)
    scale = lax.rsqrt(jnp.mean(wide * wide, axis=-1, keepdims=True) + norm_eps)
    normed = (wide * gain_ref[...] * scale).astype(jnp.bfloat16)
    hidden = gelu(jnp.dot(normed, expand_ref[...], preferred_element_type=jnp.float32))
    update = jnp.dot(
        hidden.astype(jnp.bfloat16), reduce_ref[...], preferred_element_type=jnp.float32
    )
    result = wide + update
    for row in range(2):
        out_ref[row] = result[row * padded : row * padded + width].astype(jnp.bfloat16)


def local_body(
    width, padded, above_ref, grid_ref, below_ref, west_ref, east_ref, tap_ref,
    out_ref, marker_ref, tall_ref,
):
    marker_ref[...] = jnp.zeros_like(marker_ref)
    west, east = west_ref[...].astype(jnp.float32), east_ref[...].astype(jnp.float32)
    for k, row in enumerate((above_ref[...], grid_ref[0], grid_ref[1], below_ref[...])):
        tall_ref[k, 8 + width // 8 * 8 :, :] = jnp.zeros(
            (padded + 8 - width // 8 * 8, row.shape[1]), jnp.float32
        )
        tall_ref[k, 8 : 8 + width, :] = row.astype(jnp.float32)
        tall_ref[k, 7:8, :] = west[k : k + 1]
        tall_ref[k, 8 + width : 9 + width, :] = east[k : k + 1]
    inside = lax.broadcasted_iota(jnp.int32, (padded, LANES), 0) < width
    for piece in range(tall_ref.shape[2] // LANES):
        lanes = slice(piece * LANES, (piece + 1) * LANES)
        total = [None, None]
        for k in range(4):
            for col in range(3):
                value = tall_ref[k, 7 + col : 7 + col + padded, lanes]
                for row in range(2):
                    if 0 <= k - row < 3:
                        tap = tap_ref[3 * (k - row) + col : 3 * (k - row) + col + 1, lanes]
                        part = tap * value
                        total[row] = part if total[row] is None else total[row] + part
        for row in range(2):
            value = tall_ref[1 + row, 8 : 8 + padded, lanes] + gelu(total[row])
            value = jnp.where(inside, value, 0.0)
            total[row] = value
        out_ref[:, lanes] = jnp.concatenate(total, axis=0).astype(jnp.bfloat16)


def own_part(constant, at):
    return lax.dynamic_index_in_dim(jnp.asarray(constant), at, 0, keepdims=False)


def in_hbm(count):
    return [pl.BlockSpec(memory_space=pl.ANY)] * count


def in_vmem(count):
    return [pl.BlockSpec(memory_space=pltpu.VMEM)] * count


def chip_shards(
    grid_state, conv_weight, spectral_gain, spectral_weight, norm_gain, expand_weight, reduce_weight
):
    lat_rows, width, channels = grid_state.shape
    lat_count, columns = lax.axis_size("lat"), lax.axis_size("x")
    chips, sectors = lat_count * columns, 2 * columns
    share = channels // chips
    lat_total = lat_rows * lat_count
    orders = M // 2
    span = 2 * LANES
    padded = -(-width // 8) * 8
    lat_at, column, core = lax.axis_index("lat"), lax.axis_index("x"), lax.axis_index("core")
    swap = [(0, 1), (1, 0)]
    over_chips = ("x", "lat")

    packed = pl.pallas_call(
        functools.partial(pack_body, chips, share, width),
        out_shape=jax.ShapeDtypeStruct((chips, 3 * share, LANES), jnp.bfloat16),
        in_specs=in_vmem(1),
        out_specs=in_vmem(1)[0],
        scratch_shapes=[pltpu.VMEM((2, span, channels), jnp.float32)],
        compiler_params=pltpu.CompilerParams(vmem_limit_bytes=16 << 20),
        name="pack",
    )(grid_state)
    packed, later = lax.optimization_barrier(
        (packed, (grid_state, conv_weight, spectral_gain, spectral_weight))
    )
    grid_state, conv_weight, spectral_gain, spectral_weight = later
    own = lax.all_to_all(packed, over_chips, split_axis=0, concat_axis=0, tiled=True)

    own_mix = spectral_weight.transpose(0, 2, 1)
    across_mix = lax.ppermute(own_mix, "x", [(i, 1 - i) for i in range(columns)])
    held = own_mix.shape[1]

    blocks = held // share
    piece = lax.dynamic_slice_in_dim(
        spectral_gain, (lat_at % blocks) * share, share, axis=2
    ).transpose(0, 2, 1)
    piece_other = lax.ppermute(piece, "core", swap)
    gains = jnp.where(core == lat_at // blocks, piece, piece_other)
    even = (jnp.arange(M) % 2 == 0)[None, :]
    gain_rows = jnp.concatenate(
        [
            jnp.where(even, gains[0], 0.0),
            jnp.where(even, gains[1], 0.0),
            jnp.where(even, 0.0, gains[0]),
            jnp.where(even, 0.0, gains[1]),
        ],
        axis=0,
    ).astype(jnp.bfloat16)
    chip = column * lat_count + lat_at
    taps = lax.dynamic_slice_in_dim(conv_weight.reshape(9, channels), chip * share, share, axis=1)
    taps = jnp.broadcast_to(taps[:, :, None], (9, share, LANES))

    legendre = own_part(parity_tables(lat_total, M), core)
    analysis = own_part(analysis_constant(sectors, width, span, M), core)
    table = own_part(synthesis_constant(sectors, width, padded, M), 2 * column + core)

    own, grid_late, across_mix = lax.optimization_barrier((own, grid_state, across_mix))
    other = lax.ppermute(own, "core", swap)
    above = lax.ppermute(grid_late[1], "lat", [(i, i + 1) for i in range(lat_count - 1)])
    below = lax.ppermute(grid_late[0], "lat", [(i + 1, i) for i in range(lat_count - 1)])

    bands = pl.pallas_call(
        functools.partial(spectral_body, lat_count, columns, share, width),
        out_shape=jax.ShapeDtypeStruct((columns, lat_count, share, 2 * M), jnp.bfloat16),
        in_specs=[pl.BlockSpec(memory_space=pltpu.SMEM)]
        + in_vmem(1) + in_hbm(1) + in_vmem(4),
        out_specs=in_vmem(1)[0],
        scratch_shapes=[
            pltpu.VMEM((sectors, lat_total, share, span), jnp.float32),
            pltpu.VMEM((sectors, lat_total * share, span), jnp.float32),
            pltpu.VMEM((lat_total * share, M), jnp.float32),
            pltpu.VMEM(own.shape, jnp.bfloat16),
            pltpu.SemaphoreType.DMA,
        ],
        cost_estimate=pl.CostEstimate(flops=9 * 10**9, bytes_accessed=0, transcendentals=0),
        compiler_params=pltpu.CompilerParams(vmem_limit_bytes=20 << 20),
        name="spectral",
    )(core[None], own, other, gain_rows, taps, legendre, analysis)
    bands, above, below, across_mix = lax.optimization_barrier((bands, above, below, across_mix))
    beside_mix = lax.ppermute(own_mix, "core", swap)
    far_mix = lax.ppermute(across_mix, "core", swap)
    ring = [(i, (i + 1) % sectors) for i in range(sectors)]
    tall = (above, grid_state[0], grid_state[1], below)
    west = lax.ppermute(
        jnp.stack([row[width - 1] for row in tall]), ("x", "core"), ring
    )
    east = lax.ppermute(
        jnp.stack([row[0] for row in tall]), ("x", "core"), [(j, i) for i, j in ring]
    )
    first_rows, marker = pl.pallas_call(
        functools.partial(local_body, width, padded),
        out_shape=[
            jax.ShapeDtypeStruct((2 * padded, channels), jnp.bfloat16),
            jax.ShapeDtypeStruct((8, LANES), jnp.float32),
        ],
        in_specs=in_vmem(6),
        out_specs=in_vmem(2),
        scratch_shapes=[pltpu.VMEM((4, padded + 16, channels), jnp.float32)],
        cost_estimate=pl.CostEstimate(flops=8 * 10**9, bytes_accessed=0, transcendentals=0),
        compiler_params=pltpu.CompilerParams(vmem_limit_bytes=16 << 20),
        name="local",
    )(above, grid_state, below, west, east, conv_weight.reshape(9, channels))
    back = lax.all_to_all(
        bands.reshape(chips, share, 2 * M), over_chips, split_axis=0, concat_axis=0, tiled=True
    ).reshape(channels, 2 * M)
    back, marker, table = lax.optimization_barrier((back, marker, table))
    back_other = lax.ppermute(back, "core", swap)

    field, mixing = pl.pallas_call(
        stage_body,
        out_shape=[
            jax.ShapeDtypeStruct((2, 2 * padded, channels), jnp.float32),
            jax.ShapeDtypeStruct((2, channels, channels), jnp.bfloat16),
        ],
        in_specs=[pl.BlockSpec(memory_space=pltpu.SMEM)] + in_vmem(2) + in_hbm(4),
        out_specs=in_vmem(2),
        scratch_shapes=[pltpu.SemaphoreType.DMA((4,))],
        cost_estimate=pl.CostEstimate(flops=12 * 10**9, bytes_accessed=0, transcendentals=0),
        compiler_params=pltpu.CompilerParams(vmem_limit_bytes=16 << 20),
        name="stage",
    )(
        (2 * column + core)[None], back, table,
        own_mix, beside_mix, across_mix, far_mix,
    )

    return pl.pallas_call(
        functools.partial(finish_body, width, padded),
        out_shape=jax.ShapeDtypeStruct(grid_state.shape, jnp.bfloat16),
        in_specs=in_vmem(9),
        out_specs=in_vmem(1)[0],
        cost_estimate=pl.CostEstimate(flops=3 * 10**9, bytes_accessed=0, transcendentals=0),
        compiler_params=pltpu.CompilerParams(vmem_limit_bytes=16 << 20),
        name="finish",
    )(
        field, back_other, first_rows, norm_gain[None, :], table, mixing, expand_weight,
        reduce_weight, marker,
    )


def solution(mesh):
    lat_count, lon_count = mesh.shape["lat"], mesh.shape["lon"]
    columns = lon_count // 2
    cored = Mesh(mesh.devices.reshape(lat_count, columns, 2), ("lat", "x", "core"))

    def run(grid_state, *rest):
        lat_total, lon_total, channels = grid_state.shape
        chips = lat_count * columns
        width = lon_total // lon_count
        fits = (
            columns == 2
            and lat_total == 2 * lat_count
            and lat_total <= 32
            and channels % (8 * chips) == 0
            and lat_count % 2 == 0
            and (channels // lon_count) * 2 == (channels // chips) * lat_count
            and LANES + 2 <= width
            and 2 * (width - LANES) <= LANES
        )
        if fits:
            body, on, lat, lon = chip_shards, cored, "lat", ("x", "core")
        else:
            body, on, lat, lon = banded_shards, mesh, "lat", "lon"
        return jax.shard_map(
            body,
            mesh=on,
            in_specs=(
                P(lat, lon, None), P(), P(None, None, lon), P(None, None, lon), P(), P(), P(),
            ),
            out_specs=P(lat, lon, None),
            check_vma=False,
        )(grid_state, *rest)

    return run
```

```python
import functools
import math

import jax
import jax.numpy as jnp
import numpy as np
from jax import lax
from jax.experimental import pallas as pl
from jax.experimental.pallas import tpu as pltpu
from jax.sharding import Mesh
from jax.sharding import PartitionSpec as P

M = 256
LANES = 128


norm_eps = 1e-06
underflow_cut = -60.0
degree_block = 16


def padded_2(value, sides, width, wrap):
    for axis, dim in sides:
        count, length = (lax.axis_size(axis), value.shape[dim])
        up = [(i, (i + 1) % count) for i in range(count if wrap else count - 1)]
        down = [(j, i) for i, j in up]
        last = lax.slice_in_dim(value, length - width, length, axis=dim)
        initial = lax.slice_in_dim(value, 0, width, axis=dim)
        before = lax.ppermute(last, axis, up)
        after = lax.ppermute(initial, axis, down)
        value = jnp.concatenate([before, value, after], axis=dim)
    return value


def legendre_table(orders, lat_total, degree_count):
    colatitude = (jnp.arange(lat_total, dtype=jnp.float32) + 0.5) * (math.pi / lat_total)
    cosines = jnp.cos(colatitude)
    sine_values = jnp.sin(colatitude)
    rank_values = jnp.arange(1, degree_count + 1, dtype=jnp.int32)
    rank_float = rank_values.astype(jnp.float32)
    log_terms = 0.5 * jnp.log((2.0 * rank_float + 1.0) / (2.0 * rank_float))
    log_norm = jnp.sum(
        jnp.where(rank_values[None, :] <= orders[:, None], log_terms[None, :], jnp.float32(0.0)),
        axis=1,
    )
    order_float = orders.astype(jnp.float32)[:, None]
    log_start = (
        -0.5 * math.log(4.0 * math.pi)
        + log_norm[:, None]
        + order_float * jnp.log(sine_values)[None, :]
    )
    start_value = jnp.where(
        log_start > underflow_cut, jnp.exp(jnp.maximum(log_start, underflow_cut)), jnp.float32(0.0)
    )

    def advance_block(totals, block_start):
        previous, earlier = totals
        rows_out = []
        for inner in range(degree_block):
            degree = block_start + inner
            degree_float = degree.astype(jnp.float32)
            raise_coef = jnp.sqrt(
                jnp.maximum(4.0 * degree_float * degree_float - 1.0, 0.0)
                / jnp.maximum(degree_float * degree_float - order_float * order_float, 1.0)
            )
            lower_coef = jnp.sqrt(
                jnp.maximum((degree_float - 1.0) ** 2 - order_float * order_float, 0.0)
                / jnp.maximum(4.0 * (degree_float - 1.0) ** 2 - 1.0, 1.0)
            )
            recurred = raise_coef * (cosines[None, :] * previous - lower_coef * earlier)
            current = jnp.where(
                degree < orders[:, None],
                jnp.float32(0.0),
                jnp.where(degree == orders[:, None], start_value, recurred),
            )
            earlier = previous
            previous = current
            rows_out.append(current)
        return ((previous, earlier), jnp.stack(rows_out, axis=0))

    blank = jnp.zeros((orders.shape[0], lat_total), jnp.float32)
    starts = jnp.arange(0, degree_count, degree_block, dtype=jnp.int32)
    unused, table_blocks = lax.scan(advance_block, (blank, blank), starts)
    return table_blocks.reshape(degree_count, orders.shape[0], lat_total)


def quadrature(lat_total):
    colatitude = (jnp.arange(lat_total, dtype=jnp.float32) + 0.5) * (math.pi / lat_total)
    return 2.0 * math.pi * math.pi / lat_total * jnp.sin(colatitude)


def fourier_table(longitudes, lon_total, mode_count):
    mode_index = jnp.arange(mode_count, dtype=jnp.int32)
    phase_index = longitudes[:, None] * mode_index[None, :] % lon_total
    angles = phase_index.astype(jnp.float32) * (2.0 * math.pi / lon_total)
    return (jnp.stack([jnp.cos(angles), -jnp.sin(angles)], axis=1) / lon_total).astype(jnp.bfloat16)


def synthesis_table(longitudes, lon_total, mode_count):
    mode_index = jnp.arange(mode_count, dtype=jnp.int32)
    phase_index = mode_index[:, None] * longitudes[None, :] % lon_total
    angles = phase_index.astype(jnp.float32) * (2.0 * math.pi / lon_total)
    doubling = jnp.where(mode_index == 0, 1.0, 2.0).astype(jnp.float32)[:, None]
    return jnp.stack([doubling * jnp.cos(angles), -doubling * jnp.sin(angles)], axis=0).astype(
        jnp.bfloat16
    )


def banded_shards(
    grid_state, conv_weight, spectral_gain, spectral_weight, norm_gain, expand_weight, reduce_weight
):
    lat_rows, sector_width, channel_total = grid_state.shape
    lat_count = lax.axis_size("lat")
    lon_count = lax.axis_size("lon")
    lat_total = lat_rows * lat_count
    lon_total = sector_width * lon_count
    mode_count = M
    order_share = mode_count // lat_count
    channel_share = channel_total // lon_count
    lat_position = lax.axis_index("lat")
    wrapped = padded_2(grid_state, (("lon", 1),), 1, True)
    padded = padded_2(wrapped, (("lat", 0),), 1, False)
    padded_wide = padded.astype(jnp.float32)
    filtered = jnp.zeros((lat_rows, sector_width, channel_total), jnp.float32)
    for row_shift in range(3):
        for col_shift in range(3):
            filtered = (
                filtered
                + conv_weight[row_shift, col_shift]
                * padded_wide[
                    row_shift : row_shift + lat_rows, col_shift : col_shift + sector_width
                ]
            )
    first_section = (grid_state.astype(jnp.float32) + jax.nn.gelu(filtered)).astype(jnp.bfloat16)
    gathered = lax.all_to_all(first_section, "lon", split_axis=2, concat_axis=1, tiled=True)
    forward_table = fourier_table(jnp.arange(lon_total, dtype=jnp.int32), lon_total, mode_count)
    spectrum = jnp.einsum(
        "tpc,prm->tmrc", gathered, forward_table, preferred_element_type=jnp.float32
    ).astype(jnp.bfloat16)
    cycle_spectrum = lax.all_to_all(spectrum, "lat", split_axis=1, concat_axis=0, tiled=True)
    orders = lat_position * order_share + jnp.arange(order_share, dtype=jnp.int32)
    legendre = legendre_table(orders, lat_total, mode_count)
    analysis_table = (legendre * quadrature(lat_total)[None, None, :]).astype(jnp.bfloat16)
    coefficients = jnp.einsum(
        "lmt,tmrc->lmrc", analysis_table, cycle_spectrum, preferred_element_type=jnp.float32
    )
    gain_real = spectral_gain[0][:, None, :]
    gain_imag = spectral_gain[1][:, None, :]
    coef_real = coefficients[:, :, 0, :]
    coef_imag = coefficients[:, :, 1, :]
    gained = jnp.stack(
        [
            gain_real * coef_real - gain_imag * coef_imag,
            gain_real * coef_imag + gain_imag * coef_real,
        ],
        axis=2,
    ).astype(jnp.bfloat16)
    blank = jnp.zeros((mode_count * order_share, channel_share), jnp.float32)
    portion = lax.all_gather(gained, "lon", axis=3, tiled=True)
    width_part = portion.shape[3]
    weight_rows = lax.slice_in_dim(spectral_weight, 0, width_part, axis=1)
    real_part = portion[:, :, 0, :].reshape(-1, width_part)
    imag_part = portion[:, :, 1, :].reshape(-1, width_part)
    real_sum = (
        blank
        + jnp.dot(real_part, weight_rows[0], preferred_element_type=jnp.float32)
        - jnp.dot(imag_part, weight_rows[1], preferred_element_type=jnp.float32)
    )
    imag_sum = (
        blank
        + jnp.dot(real_part, weight_rows[1], preferred_element_type=jnp.float32)
        + jnp.dot(imag_part, weight_rows[0], preferred_element_type=jnp.float32)
    )
    mixed = jnp.stack(
        [
            real_sum.reshape(mode_count, order_share, channel_share),
            imag_sum.reshape(mode_count, order_share, channel_share),
        ],
        axis=2,
    ).astype(jnp.bfloat16)
    synthesis_legendre = legendre.astype(jnp.bfloat16)
    cycle_modes = jnp.einsum(
        "lmt,lmrc->tmrc", synthesis_legendre, mixed, preferred_element_type=jnp.float32
    ).astype(jnp.bfloat16)
    band_modes = lax.all_to_all(cycle_modes, "lat", split_axis=0, concat_axis=1, tiled=True)
    inverse_table = synthesis_table(jnp.arange(lon_total, dtype=jnp.int32), lon_total, mode_count)
    all_lons = jnp.einsum(
        "tmrc,rmp->tpc", band_modes, inverse_table, preferred_element_type=jnp.float32
    )
    spectral_out = lax.all_to_all(
        all_lons.astype(jnp.bfloat16), "lon", split_axis=1, concat_axis=2, tiled=True
    ).astype(all_lons.dtype)
    second_section = (first_section.astype(jnp.float32) + spectral_out).astype(jnp.bfloat16)
    second_wide = second_section.astype(jnp.float32)
    scale_values = lax.rsqrt(jnp.mean(second_wide * second_wide, axis=-1, keepdims=True) + norm_eps)
    normed = (second_wide * norm_gain * scale_values).astype(jnp.bfloat16)
    flat_rows = normed.reshape(-1, channel_total)
    hidden = jax.nn.gelu(
        jnp.dot(flat_rows, expand_weight, preferred_element_type=jnp.float32)
    ).astype(jnp.bfloat16)
    update = jnp.dot(hidden, reduce_weight, preferred_element_type=jnp.float32)
    block_output = (second_wide.reshape(-1, channel_total) + update).astype(jnp.bfloat16)
    return block_output.reshape(lat_rows, sector_width, channel_total)


contract_last = (((1,), (1,)), ((), ()))


def legendre_constant(lat_total, mode_count):
    colatitude = (np.arange(lat_total // 2) + 0.5) * (math.pi / lat_total)
    cosines, sines = np.cos(colatitude)[:, None], np.sin(colatitude)[:, None]
    orders = np.arange(mode_count, dtype=np.float64)
    ranks = np.arange(1, mode_count, dtype=np.float64)
    log_terms = 0.5 * np.log((2.0 * ranks + 1.0) / (2.0 * ranks))
    log_norm = np.concatenate([np.zeros(1), np.cumsum(log_terms)])
    log_start = -0.5 * math.log(4.0 * math.pi) + log_norm + orders * np.log(sines)
    start = np.where(
        log_start > underflow_cut, np.exp(np.maximum(log_start, underflow_cut)), 0.0
    )
    table = np.zeros((lat_total // 2, mode_count, mode_count))
    previous = np.zeros_like(start)
    earlier = np.zeros_like(start)
    for degree in range(mode_count):
        raised = np.sqrt(
            np.maximum(4.0 * degree * degree - 1.0, 0.0)
            / np.maximum(degree * degree - orders * orders, 1.0)
        )
        lowered = np.sqrt(
            np.maximum((degree - 1.0) ** 2 - orders * orders, 0.0)
            / max(4.0 * (degree - 1.0) ** 2 - 1.0, 1.0)
        )
        recurred = raised * (cosines * previous - lowered * earlier)
        current = np.where(degree < orders, 0.0, np.where(degree == orders, start, recurred))
        earlier, previous = previous, current
        table[:, degree, :] = current
    return table


def parity_tables(lat_total, mode_count):
    table = legendre_constant(lat_total, mode_count)
    return np.stack([table[:, :, 0::2], table[:, :, 1::2]]).astype(jnp.bfloat16)


def analysis_constant(sectors, width, span, mode_count):
    lon_total = sectors * width
    out = np.zeros((2, sectors, span, 2, mode_count // 2))
    for parity in range(2):
        modes = np.arange(parity, mode_count, 2)
        for sector in range(sectors):
            longitudes = sector * width + np.arange(width)
            angles = (longitudes[:, None] * modes[None, :] % lon_total) * (2 * math.pi / lon_total)
            out[parity, sector, :width, 0] = np.cos(angles) / lon_total
            out[parity, sector, :width, 1] = -np.sin(angles) / lon_total
    return out.reshape(2, sectors, span, mode_count).astype(jnp.bfloat16)


def synthesis_constant(sectors, width, padded, mode_count):
    lon_total = sectors * width
    out = np.zeros((sectors, 2, 2, padded, 2, mode_count // 2))
    for sector in range(sectors):
        longitudes = sector * width + np.arange(width)
        for half in range(2):
            modes = np.arange((sector + half) % 2, mode_count, 2)
            doubling = np.where(modes == 0, 1.0, 2.0)[None, :]
            angles = (longitudes[:, None] * modes[None, :] % lon_total) * (2 * math.pi / lon_total)
            cosine, sine = doubling * np.cos(angles), doubling * np.sin(angles)
            out[sector, half, 0, :width, 0] = cosine
            out[sector, half, 0, :width, 1] = -sine
            out[sector, half, 1, :width, 0] = sine
            out[sector, half, 1, :width, 1] = cosine
    return out.reshape(sectors, 2, 2 * padded, mode_count).astype(jnp.bfloat16)


def gelu(value):
    inner = value * (0.7978845608028654 + (0.7978845608028654 * 0.044715) * (value * value))
    half = 0.5 * value
    return half + half * jnp.tanh(inner)


def pack_body(chips, share, width, grid_ref, out_ref, wide_ref):
    span = wide_ref.shape[1]
    tail = width // 8 * 8
    flipped = []
    for row in range(2):
        wide_ref[row, tail:span, :] = jnp.zeros((span - tail, chips * share), jnp.float32)
        wide_ref[row, 0:width, :] = grid_ref[row].astype(jnp.float32)
        flipped.append(wide_ref[row].T)
    rest = flipped[0][:, LANES:] + pltpu.roll(flipped[1][:, LANES:], width - LANES, axis=1)
    for chip in range(chips):
        at = slice(chip * share, (chip + 1) * share)
        block = jnp.concatenate(
            [flipped[0][at, :LANES], flipped[1][at, :LANES], rest[at]], axis=0
        )
        out_ref[chip] = block.astype(jnp.bfloat16)


def spectral_body(
    lat_count, columns, share, width,
    parity_ref, own_ref, other_any, gain_ref, tap_ref, legendre_ref, table_ref, out_ref,
    field_ref, first_ref, modes_ref, other_ref, sem,
):
    lat_total = 2 * lat_count
    north = lat_total // 2
    sectors = 2 * columns
    edge = width - LANES
    orders = legendre_ref.shape[2]
    parity = parity_ref[0]
    arrival = pltpu.make_async_copy(other_any, other_ref, sem)
    arrival.start()
    for source, core in ((own_ref, parity), (other_ref, 1 - parity)):
        if source is other_ref:
            arrival.wait()
        for column in range(columns):
            sector = 2 * column + core
            for band in range(lat_count):
                block = source[column * lat_count + band].astype(jnp.float32)
                rest = block[2 * share :]
                field_ref[sector, 2 * band, :, 0:LANES] = block[:share]
                field_ref[sector, 2 * band, :, LANES:] = rest
                field_ref[sector, 2 * band + 1, :, 0:LANES] = block[share : 2 * share]
                field_ref[sector, 2 * band + 1, :, LANES:] = pltpu.roll(rest, LANES - edge, axis=1)

    lane = lax.broadcasted_iota(jnp.int32, (8, LANES), 1)

    def filter_sector(sector, unused):
        after = lax.rem(sector + 1, sectors)
        before = lax.rem(sector + sectors - 1, sectors)

        def filter_rows(tile, unused):
            rows = pl.ds(pl.multiple_of(tile * 8, 8), 8)
            taps = []
            for k in range(9):
                tap = tap_ref[k, rows, :]
                taps.append(jnp.concatenate([tap, tap], axis=1))
            held, total, ahead = None, None, None

            def finish(t, value, sum_):
                first_ref[sector, pl.ds(pl.multiple_of(t * share + tile * 8, 8), 8), :] = value + gelu(sum_)

            for t in range(lat_total):
                low = field_ref[sector, t, rows, 0:LANES]
                high = field_ref[sector, t, rows, LANES:]
                right = pltpu.roll(field_ref[after, t, rows, 0:LANES], edge, axis=1)
                left = pltpu.roll(field_ref[before, t, rows, LANES:], LANES - edge, axis=1)
                high = jnp.where(lane == edge, right, jnp.where(lane == LANES - 1, left, high))
                value = jnp.concatenate([low, high], axis=1)
                west = pltpu.roll(value, 1, axis=1)
                east = pltpu.roll(value, 2 * LANES - 1, axis=1)

                def weigh(row):
                    return (
                        taps[3 * row] * west + taps[3 * row + 1] * value + taps[3 * row + 2] * east
                    )

                if t > 0:
                    finish(t - 1, held, total + weigh(2))
                total = weigh(1) if t == 0 else ahead + weigh(1)
                ahead = weigh(0)
                held = value
            finish(lat_total - 1, held, total)
            return unused

        return lax.fori_loop(0, share // 8, filter_rows, unused)

    lax.fori_loop(0, sectors, filter_sector, 0)

    modes = None
    for sector in range(sectors):
        part = jnp.dot(
            first_ref[sector].astype(jnp.bfloat16),
            table_ref[sector],
            preferred_element_type=jnp.float32,
        )
        modes = part if modes is None else modes + part
    modes_ref[...] = modes

    sign = (1 - 2 * parity).astype(jnp.float32)
    folded = [[], []]
    for t in range(north):
        weight = 2.0 * math.pi * math.pi / lat_total * math.sin(math.pi * (t + 0.5) / lat_total)
        upper = weight * modes_ref[t * share : (t + 1) * share, :]
        mirror = lat_total - 1 - t
        lower = (weight * sign) * modes_ref[mirror * share : (mirror + 1) * share, :]
        folded[0].append(upper + lower)
        folded[1].append(upper - lower)

    sums = [[None] * north, [None] * north]

    def add(half, t, kernel, value):
        real = kernel[0] * value[:, :orders] - kernel[1] * value[:, orders:]
        imag = kernel[0] * value[:, orders:] + kernel[1] * value[:, :orders]
        had = sums[half][t]
        sums[half][t] = (real, imag) if had is None else (had[0] + real, had[1] + imag)

    for t in range(north):
        products = jnp.concatenate(
            [legendre_ref[t] * legendre_ref[s] for s in range(t, north)], axis=1
        )
        kernels = jnp.dot(gain_ref[...], products, preferred_element_type=jnp.float32)
        for s in range(t, north):
            at = slice((s - t) * orders, (s - t + 1) * orders)
            for half in range(2):
                base = 2 * half * share
                kernel = (kernels[base : base + share, at], kernels[base + share : base + 2 * share, at])
                add(half, t, kernel, folded[half][s])
                if s != t:
                    add(half, s, kernel, folded[half][t])

    for t in range(north):
        for part in range(2):
            even, odd = sums[0][t][part], sums[1][t][part]
            for place, value in ((t, even + odd), (lat_total - 1 - t, sign * (even - odd))):
                at = (place % 2) * 2 * orders + part * orders
                value = value.astype(jnp.bfloat16)
                for column in range(columns):
                    out_ref[column, place // 2, :, at : at + orders] = value


def stage_body(
    place_ref, own_ref, table_ref,
    mix_a_ref, mix_b_ref, mix_c_ref, mix_d_ref,
    field_ref, mix_ref, sems,
):
    place = place_ref[0]
    held = mix_a_ref.shape[1]
    loads = []
    for k, source in enumerate((mix_a_ref, mix_b_ref, mix_c_ref, mix_d_ref)):
        sector = 2 * (place // 2 if k < 2 else 1 - place // 2) + (
            place % 2 if k % 2 == 0 else 1 - place % 2
        )
        rows = pl.ds(pl.multiple_of(sector * held, held), held)
        loads.append(pltpu.make_async_copy(source, mix_ref.at[:, rows, :], sems.at[k]))
    for load in loads:
        load.start()
    modes = table_ref.shape[2]
    for row in range(2):
        field_ref[row] = lax.dot_general(
            table_ref[0], own_ref[:, row * modes : (row + 1) * modes], contract_last,
            preferred_element_type=jnp.float32,
        )
    for load in loads:
        load.wait()


def finish_body(
    width, padded,
    field_ref, other_ref, first_ref, gain_ref, table_ref, mix_ref, expand_ref, reduce_ref,
    marker_ref, out_ref,
):
    modes = table_ref.shape[2]
    real, imag = [], []
    for row in range(2):
        field = field_ref[row] + lax.dot_general(
            table_ref[1], other_ref[:, row * modes : (row + 1) * modes], contract_last,
            preferred_element_type=jnp.float32,
        )
        real.append(field[:padded])
        imag.append(field[padded:])
    real = jnp.concatenate(real, axis=0).astype(jnp.bfloat16)
    imag = jnp.concatenate(imag, axis=0).astype(jnp.bfloat16)
    spectral_out = lax.dot_general(
        real, mix_ref[0], contract_last, preferred_element_type=jnp.float32
    ) - lax.dot_general(imag, mix_ref[1], contract_last, preferred_element_type=jnp.float32)
    second = (first_ref[...].astype(jnp.float32) + spectral_out).astype(jnp.bfloat16)
    wide = second.astype(jnp.float32)
    scale = lax.rsqrt(jnp.mean(wide * wide, axis=-1, keepdims=True) + norm_eps)
    normed = (wide * gain_ref[...] * scale).astype(jnp.bfloat16)
    hidden = gelu(jnp.dot(normed, expand_ref[...], preferred_element_type=jnp.float32))
    update = jnp.dot(
        hidden.astype(jnp.bfloat16), reduce_ref[...], preferred_element_type=jnp.float32
    )
    result = wide + update
    for row in range(2):
        out_ref[row] = result[row * padded : row * padded + width].astype(jnp.bfloat16)


def local_body(
    width, padded, above_ref, grid_ref, below_ref, west_ref, east_ref, tap_ref,
    out_ref, marker_ref, tall_ref,
):
    marker_ref[...] = jnp.zeros_like(marker_ref)
    west, east = west_ref[...].astype(jnp.float32), east_ref[...].astype(jnp.float32)
    for k, row in enumerate((above_ref[...], grid_ref[0], grid_ref[1], below_ref[...])):
        tall_ref[k, 8 + width // 8 * 8 :, :] = jnp.zeros(
            (padded + 8 - width // 8 * 8, row.shape[1]), jnp.float32
        )
        tall_ref[k, 8 : 8 + width, :] = row.astype(jnp.float32)
        tall_ref[k, 7:8, :] = west[k : k + 1]
        tall_ref[k, 8 + width : 9 + width, :] = east[k : k + 1]
    inside = lax.broadcasted_iota(jnp.int32, (padded, LANES), 0) < width
    for piece in range(tall_ref.shape[2] // LANES):
        lanes = slice(piece * LANES, (piece + 1) * LANES)
        total = [None, None]
        for k in range(4):
            for col in range(3):
                value = tall_ref[k, 7 + col : 7 + col + padded, lanes]
                for row in range(2):
                    if 0 <= k - row < 3:
                        tap = tap_ref[3 * (k - row) + col : 3 * (k - row) + col + 1, lanes]
                        part = tap * value
                        total[row] = part if total[row] is None else total[row] + part
        for row in range(2):
            value = tall_ref[1 + row, 8 : 8 + padded, lanes] + gelu(total[row])
            value = jnp.where(inside, value, 0.0)
            total[row] = value
        out_ref[:, lanes] = jnp.concatenate(total, axis=0).astype(jnp.bfloat16)


def own_part(constant, at):
    return lax.dynamic_index_in_dim(jnp.asarray(constant), at, 0, keepdims=False)


def in_hbm(count):
    return [pl.BlockSpec(memory_space=pl.ANY)] * count


def in_vmem(count):
    return [pl.BlockSpec(memory_space=pltpu.VMEM)] * count


def chip_shards(
    grid_state, conv_weight, spectral_gain, spectral_weight, norm_gain, expand_weight, reduce_weight
):
    lat_rows, width, channels = grid_state.shape
    lat_count, columns = lax.axis_size("lat"), lax.axis_size("x")
    chips, sectors = lat_count * columns, 2 * columns
    share = channels // chips
    lat_total = lat_rows * lat_count
    orders = M // 2
    span = 2 * LANES
    padded = -(-width // 8) * 8
    lat_at, column, core = lax.axis_index("lat"), lax.axis_index("x"), lax.axis_index("core")
    swap = [(0, 1), (1, 0)]
    over_chips = ("x", "lat")

    packed = pl.pallas_call(
        functools.partial(pack_body, chips, share, width),
        out_shape=jax.ShapeDtypeStruct((chips, 3 * share, LANES), jnp.bfloat16),
        in_specs=in_vmem(1),
        out_specs=in_vmem(1)[0],
        scratch_shapes=[pltpu.VMEM((2, span, channels), jnp.float32)],
        compiler_params=pltpu.CompilerParams(vmem_limit_bytes=16 << 20),
        name="pack",
    )(grid_state)
    grid_first = grid_state
    packed, later = lax.optimization_barrier(
        (packed, (grid_state, conv_weight, spectral_gain, spectral_weight))
    )
    grid_state, conv_weight, spectral_gain, spectral_weight = later
    own = lax.all_to_all(packed, over_chips, split_axis=0, concat_axis=0, tiled=True)

    own_mix = spectral_weight.transpose(0, 2, 1)
    held = own_mix.shape[1]

    blocks = held // share
    piece = lax.dynamic_slice_in_dim(
        spectral_gain, (lat_at % blocks) * share, share, axis=2
    ).transpose(0, 2, 1)
    piece_other = lax.ppermute(piece, "core", swap)
    gains = jnp.where(core == lat_at // blocks, piece, piece_other)
    even = (jnp.arange(M) % 2 == 0)[None, :]
    gain_rows = jnp.concatenate(
        [
            jnp.where(even, gains[0], 0.0),
            jnp.where(even, gains[1], 0.0),
            jnp.where(even, 0.0, gains[0]),
            jnp.where(even, 0.0, gains[1]),
        ],
        axis=0,
    ).astype(jnp.bfloat16)
    chip = column * lat_count + lat_at
    taps = lax.dynamic_slice_in_dim(conv_weight.reshape(9, channels), chip * share, share, axis=1)
    taps = jnp.broadcast_to(taps[:, :, None], (9, share, LANES))

    legendre = own_part(parity_tables(lat_total, M), core)
    analysis = own_part(analysis_constant(sectors, width, span, M), core)
    table = own_part(synthesis_constant(sectors, width, padded, M), 2 * column + core)

    across_mix = lax.ppermute(own_mix, "x", [(i, 1 - i) for i in range(columns)])
    own, across_mix = lax.optimization_barrier((own, across_mix))
    other = lax.ppermute(own, "core", swap)
    above = lax.ppermute(grid_first[1], "lat", [(i, i + 1) for i in range(lat_count - 1)])
    below = lax.ppermute(grid_first[0], "lat", [(i + 1, i) for i in range(lat_count - 1)])

    bands = pl.pallas_call(
        functools.partial(spectral_body, lat_count, columns, share, width),
        out_shape=jax.ShapeDtypeStruct((columns, lat_count, share, 2 * M), jnp.bfloat16),
        in_specs=[pl.BlockSpec(memory_space=pltpu.SMEM)]
        + in_vmem(1) + in_hbm(1) + in_vmem(4),
        out_specs=in_vmem(1)[0],
        scratch_shapes=[
            pltpu.VMEM((sectors, lat_total, share, span), jnp.float32),
            pltpu.VMEM((sectors, lat_total * share, span), jnp.float32),
            pltpu.VMEM((lat_total * share, M), jnp.float32),
            pltpu.VMEM(own.shape, jnp.bfloat16),
            pltpu.SemaphoreType.DMA,
        ],
        cost_estimate=pl.CostEstimate(flops=9 * 10**9, bytes_accessed=0, transcendentals=0),
        compiler_params=pltpu.CompilerParams(vmem_limit_bytes=20 << 20),
        name="spectral",
    )(core[None], own, other, gain_rows, taps, legendre, analysis)
    bands, above, below, across_mix = lax.optimization_barrier((bands, above, below, across_mix))
    beside_mix = lax.ppermute(own_mix, "core", swap)
    far_mix = lax.ppermute(across_mix, "core", swap)
    ring = [(i, (i + 1) % sectors) for i in range(sectors)]
    tall = (above, grid_state[0], grid_state[1], below)
    west = lax.ppermute(
        jnp.stack([row[width - 1] for row in tall]), ("x", "core"), ring
    )
    east = lax.ppermute(
        jnp.stack([row[0] for row in tall]), ("x", "core"), [(j, i) for i, j in ring]
    )
    first_rows, marker = pl.pallas_call(
        functools.partial(local_body, width, padded),
        out_shape=[
            jax.ShapeDtypeStruct((2 * padded, channels), jnp.bfloat16),
            jax.ShapeDtypeStruct((8, LANES), jnp.float32),
        ],
        in_specs=in_vmem(6),
        out_specs=in_vmem(2),
        scratch_shapes=[pltpu.VMEM((4, padded + 16, channels), jnp.float32)],
        cost_estimate=pl.CostEstimate(flops=8 * 10**9, bytes_accessed=0, transcendentals=0),
        compiler_params=pltpu.CompilerParams(vmem_limit_bytes=16 << 20),
        name="local",
    )(above, grid_state, below, west, east, conv_weight.reshape(9, channels))
    back = lax.all_to_all(
        bands.reshape(chips, share, 2 * M), over_chips, split_axis=0, concat_axis=0, tiled=True
    ).reshape(channels, 2 * M)
    back, marker, table = lax.optimization_barrier((back, marker, table))
    back_other = lax.ppermute(back, "core", swap)

    field, mixing = pl.pallas_call(
        stage_body,
        out_shape=[
            jax.ShapeDtypeStruct((2, 2 * padded, channels), jnp.float32),
            jax.ShapeDtypeStruct((2, channels, channels), jnp.bfloat16),
        ],
        in_specs=[pl.BlockSpec(memory_space=pltpu.SMEM)] + in_vmem(2) + in_hbm(4),
        out_specs=in_vmem(2),
        scratch_shapes=[pltpu.SemaphoreType.DMA((4,))],
        cost_estimate=pl.CostEstimate(flops=12 * 10**9, bytes_accessed=0, transcendentals=0),
        compiler_params=pltpu.CompilerParams(vmem_limit_bytes=16 << 20),
        name="stage",
    )(
        (2 * column + core)[None], back, table,
        own_mix, beside_mix, across_mix, far_mix,
    )

    return pl.pallas_call(
        functools.partial(finish_body, width, padded),
        out_shape=jax.ShapeDtypeStruct(grid_state.shape, jnp.bfloat16),
        in_specs=in_vmem(9),
        out_specs=in_vmem(1)[0],
        cost_estimate=pl.CostEstimate(flops=3 * 10**9, bytes_accessed=0, transcendentals=0),
        compiler_params=pltpu.CompilerParams(vmem_limit_bytes=16 << 20),
        name="finish",
    )(
        field, back_other, first_rows, norm_gain[None, :], table, mixing, expand_weight,
        reduce_weight, marker,
    )


def solution(mesh):
    lat_count, lon_count = mesh.shape["lat"], mesh.shape["lon"]
    columns = lon_count // 2
    cored = Mesh(mesh.devices.reshape(lat_count, columns, 2), ("lat", "x", "core"))

    def run(grid_state, *rest):
        lat_total, lon_total, channels = grid_state.shape
        chips = lat_count * columns
        width = lon_total // lon_count
        fits = (
            columns == 2
            and lat_total == 2 * lat_count
            and lat_total <= 32
            and channels % (8 * chips) == 0
            and lat_count % 2 == 0
            and (channels // lon_count) * 2 == (channels // chips) * lat_count
            and LANES + 2 <= width
            and 2 * (width - LANES) <= LANES
        )
        if fits:
            body, on, lat, lon = chip_shards, cored, "lat", ("x", "core")
        else:
            body, on, lat, lon = banded_shards, mesh, "lat", "lon"
        return jax.shard_map(
            body,
            mesh=on,
            in_specs=(
                P(lat, lon, None), P(), P(None, None, lon), P(None, None, lon), P(), P(), P(),
            ),
            out_specs=P(lat, lon, None),
            check_vma=False,
        )(grid_state, *rest)

    return run
```

```python
import functools
import math

import jax
import jax.numpy as jnp
import numpy as np
from jax import lax
from jax.experimental import pallas as pl
from jax.experimental.pallas import tpu as pltpu
from jax.sharding import Mesh
from jax.sharding import PartitionSpec as P

M = 256
LANES = 128


norm_eps = 1e-06
underflow_cut = -60.0
degree_block = 16


def padded_2(value, sides, width, wrap):
    for axis, dim in sides:
        count, length = (lax.axis_size(axis), value.shape[dim])
        up = [(i, (i + 1) % count) for i in range(count if wrap else count - 1)]
        down = [(j, i) for i, j in up]
        last = lax.slice_in_dim(value, length - width, length, axis=dim)
        initial = lax.slice_in_dim(value, 0, width, axis=dim)
        before = lax.ppermute(last, axis, up)
        after = lax.ppermute(initial, axis, down)
        value = jnp.concatenate([before, value, after], axis=dim)
    return value


def legendre_table(orders, lat_total, degree_count):
    colatitude = (jnp.arange(lat_total, dtype=jnp.float32) + 0.5) * (math.pi / lat_total)
    cosines = jnp.cos(colatitude)
    sine_values = jnp.sin(colatitude)
    rank_values = jnp.arange(1, degree_count + 1, dtype=jnp.int32)
    rank_float = rank_values.astype(jnp.float32)
    log_terms = 0.5 * jnp.log((2.0 * rank_float + 1.0) / (2.0 * rank_float))
    log_norm = jnp.sum(
        jnp.where(rank_values[None, :] <= orders[:, None], log_terms[None, :], jnp.float32(0.0)),
        axis=1,
    )
    order_float = orders.astype(jnp.float32)[:, None]
    log_start = (
        -0.5 * math.log(4.0 * math.pi)
        + log_norm[:, None]
        + order_float * jnp.log(sine_values)[None, :]
    )
    start_value = jnp.where(
        log_start > underflow_cut, jnp.exp(jnp.maximum(log_start, underflow_cut)), jnp.float32(0.0)
    )

    def advance_block(totals, block_start):
        previous, earlier = totals
        rows_out = []
        for inner in range(degree_block):
            degree = block_start + inner
            degree_float = degree.astype(jnp.float32)
            raise_coef = jnp.sqrt(
                jnp.maximum(4.0 * degree_float * degree_float - 1.0, 0.0)
                / jnp.maximum(degree_float * degree_float - order_float * order_float, 1.0)
            )
            lower_coef = jnp.sqrt(
                jnp.maximum((degree_float - 1.0) ** 2 - order_float * order_float, 0.0)
                / jnp.maximum(4.0 * (degree_float - 1.0) ** 2 - 1.0, 1.0)
            )
            recurred = raise_coef * (cosines[None, :] * previous - lower_coef * earlier)
            current = jnp.where(
                degree < orders[:, None],
                jnp.float32(0.0),
                jnp.where(degree == orders[:, None], start_value, recurred),
            )
            earlier = previous
            previous = current
            rows_out.append(current)
        return ((previous, earlier), jnp.stack(rows_out, axis=0))

    blank = jnp.zeros((orders.shape[0], lat_total), jnp.float32)
    starts = jnp.arange(0, degree_count, degree_block, dtype=jnp.int32)
    unused, table_blocks = lax.scan(advance_block, (blank, blank), starts)
    return table_blocks.reshape(degree_count, orders.shape[0], lat_total)


def quadrature(lat_total):
    colatitude = (jnp.arange(lat_total, dtype=jnp.float32) + 0.5) * (math.pi / lat_total)
    return 2.0 * math.pi * math.pi / lat_total * jnp.sin(colatitude)


def fourier_table(longitudes, lon_total, mode_count):
    mode_index = jnp.arange(mode_count, dtype=jnp.int32)
    phase_index = longitudes[:, None] * mode_index[None, :] % lon_total
    angles = phase_index.astype(jnp.float32) * (2.0 * math.pi / lon_total)
    return (jnp.stack([jnp.cos(angles), -jnp.sin(angles)], axis=1) / lon_total).astype(jnp.bfloat16)


def synthesis_table(longitudes, lon_total, mode_count):
    mode_index = jnp.arange(mode_count, dtype=jnp.int32)
    phase_index = mode_index[:, None] * longitudes[None, :] % lon_total
    angles = phase_index.astype(jnp.float32) * (2.0 * math.pi / lon_total)
    doubling = jnp.where(mode_index == 0, 1.0, 2.0).astype(jnp.float32)[:, None]
    return jnp.stack([doubling * jnp.cos(angles), -doubling * jnp.sin(angles)], axis=0).astype(
        jnp.bfloat16
    )


def banded_shards(
    grid_state, conv_weight, spectral_gain, spectral_weight, norm_gain, expand_weight, reduce_weight
):
    lat_rows, sector_width, channel_total = grid_state.shape
    lat_count = lax.axis_size("lat")
    lon_count = lax.axis_size("lon")
    lat_total = lat_rows * lat_count
    lon_total = sector_width * lon_count
    mode_count = M
    order_share = mode_count // lat_count
    channel_share = channel_total // lon_count
    lat_position = lax.axis_index("lat")
    wrapped = padded_2(grid_state, (("lon", 1),), 1, True)
    padded = padded_2(wrapped, (("lat", 0),), 1, False)
    padded_wide = padded.astype(jnp.float32)
    filtered = jnp.zeros((lat_rows, sector_width, channel_total), jnp.float32)
    for row_shift in range(3):
        for col_shift in range(3):
            filtered = (
                filtered
                + conv_weight[row_shift, col_shift]
                * padded_wide[
                    row_shift : row_shift + lat_rows, col_shift : col_shift + sector_width
                ]
            )
    first_section = (grid_state.astype(jnp.float32) + jax.nn.gelu(filtered)).astype(jnp.bfloat16)
    gathered = lax.all_to_all(first_section, "lon", split_axis=2, concat_axis=1, tiled=True)
    forward_table = fourier_table(jnp.arange(lon_total, dtype=jnp.int32), lon_total, mode_count)
    spectrum = jnp.einsum(
        "tpc,prm->tmrc", gathered, forward_table, preferred_element_type=jnp.float32
    ).astype(jnp.bfloat16)
    cycle_spectrum = lax.all_to_all(spectrum, "lat", split_axis=1, concat_axis=0, tiled=True)
    orders = lat_position * order_share + jnp.arange(order_share, dtype=jnp.int32)
    legendre = legendre_table(orders, lat_total, mode_count)
    analysis_table = (legendre * quadrature(lat_total)[None, None, :]).astype(jnp.bfloat16)
    coefficients = jnp.einsum(
        "lmt,tmrc->lmrc", analysis_table, cycle_spectrum, preferred_element_type=jnp.float32
    )
    gain_real = spectral_gain[0][:, None, :]
    gain_imag = spectral_gain[1][:, None, :]
    coef_real = coefficients[:, :, 0, :]
    coef_imag = coefficients[:, :, 1, :]
    gained = jnp.stack(
        [
            gain_real * coef_real - gain_imag * coef_imag,
            gain_real * coef_imag + gain_imag * coef_real,
        ],
        axis=2,
    ).astype(jnp.bfloat16)
    blank = jnp.zeros((mode_count * order_share, channel_share), jnp.float32)
    portion = lax.all_gather(gained, "lon", axis=3, tiled=True)
    width_part = portion.shape[3]
    weight_rows = lax.slice_in_dim(spectral_weight, 0, width_part, axis=1)
    real_part = portion[:, :, 0, :].reshape(-1, width_part)
    imag_part = portion[:, :, 1, :].reshape(-1, width_part)
    real_sum = (
        blank
        + jnp.dot(real_part, weight_rows[0], preferred_element_type=jnp.float32)
        - jnp.dot(imag_part, weight_rows[1], preferred_element_type=jnp.float32)
    )
    imag_sum = (
        blank
        + jnp.dot(real_part, weight_rows[1], preferred_element_type=jnp.float32)
        + jnp.dot(imag_part, weight_rows[0], preferred_element_type=jnp.float32)
    )
    mixed = jnp.stack(
        [
            real_sum.reshape(mode_count, order_share, channel_share),
            imag_sum.reshape(mode_count, order_share, channel_share),
        ],
        axis=2,
    ).astype(jnp.bfloat16)
    synthesis_legendre = legendre.astype(jnp.bfloat16)
    cycle_modes = jnp.einsum(
        "lmt,lmrc->tmrc", synthesis_legendre, mixed, preferred_element_type=jnp.float32
    ).astype(jnp.bfloat16)
    band_modes = lax.all_to_all(cycle_modes, "lat", split_axis=0, concat_axis=1, tiled=True)
    inverse_table = synthesis_table(jnp.arange(lon_total, dtype=jnp.int32), lon_total, mode_count)
    all_lons = jnp.einsum(
        "tmrc,rmp->tpc", band_modes, inverse_table, preferred_element_type=jnp.float32
    )
    spectral_out = lax.all_to_all(
        all_lons.astype(jnp.bfloat16), "lon", split_axis=1, concat_axis=2, tiled=True
    ).astype(all_lons.dtype)
    second_section = (first_section.astype(jnp.float32) + spectral_out).astype(jnp.bfloat16)
    second_wide = second_section.astype(jnp.float32)
    scale_values = lax.rsqrt(jnp.mean(second_wide * second_wide, axis=-1, keepdims=True) + norm_eps)
    normed = (second_wide * norm_gain * scale_values).astype(jnp.bfloat16)
    flat_rows = normed.reshape(-1, channel_total)
    hidden = jax.nn.gelu(
        jnp.dot(flat_rows, expand_weight, preferred_element_type=jnp.float32)
    ).astype(jnp.bfloat16)
    update = jnp.dot(hidden, reduce_weight, preferred_element_type=jnp.float32)
    block_output = (second_wide.reshape(-1, channel_total) + update).astype(jnp.bfloat16)
    return block_output.reshape(lat_rows, sector_width, channel_total)


contract_last = (((1,), (1,)), ((), ()))


def legendre_constant(lat_total, mode_count):
    colatitude = (np.arange(lat_total // 2) + 0.5) * (math.pi / lat_total)
    cosines, sines = np.cos(colatitude)[:, None], np.sin(colatitude)[:, None]
    orders = np.arange(mode_count, dtype=np.float64)
    ranks = np.arange(1, mode_count, dtype=np.float64)
    log_terms = 0.5 * np.log((2.0 * ranks + 1.0) / (2.0 * ranks))
    log_norm = np.concatenate([np.zeros(1), np.cumsum(log_terms)])
    log_start = -0.5 * math.log(4.0 * math.pi) + log_norm + orders * np.log(sines)
    start = np.where(
        log_start > underflow_cut, np.exp(np.maximum(log_start, underflow_cut)), 0.0
    )
    table = np.zeros((lat_total // 2, mode_count, mode_count))
    previous = np.zeros_like(start)
    earlier = np.zeros_like(start)
    for degree in range(mode_count):
        raised = np.sqrt(
            np.maximum(4.0 * degree * degree - 1.0, 0.0)
            / np.maximum(degree * degree - orders * orders, 1.0)
        )
        lowered = np.sqrt(
            np.maximum((degree - 1.0) ** 2 - orders * orders, 0.0)
            / max(4.0 * (degree - 1.0) ** 2 - 1.0, 1.0)
        )
        recurred = raised * (cosines * previous - lowered * earlier)
        current = np.where(degree < orders, 0.0, np.where(degree == orders, start, recurred))
        earlier, previous = previous, current
        table[:, degree, :] = current
    return table


def parity_tables(lat_total, mode_count):
    table = legendre_constant(lat_total, mode_count)
    return np.stack([table[:, :, 0::2], table[:, :, 1::2]]).astype(jnp.bfloat16)


def analysis_constant(sectors, width, span, mode_count):
    lon_total = sectors * width
    out = np.zeros((2, sectors, span, 2, mode_count // 2))
    for parity in range(2):
        modes = np.arange(parity, mode_count, 2)
        for sector in range(sectors):
            longitudes = sector * width + np.arange(width)
            angles = (longitudes[:, None] * modes[None, :] % lon_total) * (2 * math.pi / lon_total)
            out[parity, sector, :width, 0] = np.cos(angles) / lon_total
            out[parity, sector, :width, 1] = -np.sin(angles) / lon_total
    return out.reshape(2, sectors, span, mode_count).astype(jnp.bfloat16)


def synthesis_constant(sectors, width, padded, mode_count):
    lon_total = sectors * width
    out = np.zeros((sectors, 2, 2, padded, 2, mode_count // 2))
    for sector in range(sectors):
        longitudes = sector * width + np.arange(width)
        for half in range(2):
            modes = np.arange((sector + half) % 2, mode_count, 2)
            doubling = np.where(modes == 0, 1.0, 2.0)[None, :]
            angles = (longitudes[:, None] * modes[None, :] % lon_total) * (2 * math.pi / lon_total)
            cosine, sine = doubling * np.cos(angles), doubling * np.sin(angles)
            out[sector, half, 0, :width, 0] = cosine
            out[sector, half, 0, :width, 1] = -sine
            out[sector, half, 1, :width, 0] = sine
            out[sector, half, 1, :width, 1] = cosine
    return out.reshape(sectors, 2, 2 * padded, mode_count).astype(jnp.bfloat16)


def gelu(value):
    inner = value * (0.7978845608028654 + (0.7978845608028654 * 0.044715) * (value * value))
    half = 0.5 * value
    return half + half * jnp.tanh(inner)


def pack_body(chips, share, width, grid_ref, out_ref, wide_ref):
    span = wide_ref.shape[1]
    tail = width // 8 * 8
    flipped = []
    for row in range(2):
        wide_ref[row, tail:span, :] = jnp.zeros((span - tail, chips * share), jnp.float32)
        wide_ref[row, 0:width, :] = grid_ref[row].astype(jnp.float32)
        flipped.append(wide_ref[row].T)
    rest = flipped[0][:, LANES:] + pltpu.roll(flipped[1][:, LANES:], width - LANES, axis=1)
    for chip in range(chips):
        at = slice(chip * share, (chip + 1) * share)
        block = jnp.concatenate(
            [flipped[0][at, :LANES], flipped[1][at, :LANES], rest[at]], axis=0
        )
        out_ref[chip] = block.astype(jnp.bfloat16)


def spectral_body(
    lat_count, columns, share, width,
    parity_ref, own_ref, other_any, gain_ref, tap_ref, legendre_ref, table_ref, out_ref,
    field_ref, exact_ref, west_ref, east_ref, first_ref, modes_ref, other_ref, sem,
):
    lat_total = 2 * lat_count
    north = lat_total // 2
    sectors = 2 * columns
    edge = width - LANES
    span = 2 * LANES
    orders = legendre_ref.shape[2]
    parity = parity_ref[0]
    arrival = pltpu.make_async_copy(other_any, other_ref, sem)
    arrival.start()
    for source, core in ((own_ref, parity), (other_ref, 1 - parity)):
        if source is other_ref:
            arrival.wait()
        for column in range(columns):
            sector = 2 * column + core
            for band in range(lat_count):
                block = source[column * lat_count + band].astype(jnp.float32)
                rest = block[2 * share :]
                high = jnp.concatenate([rest, pltpu.roll(rest, LANES - edge, axis=1)], axis=0)
                whole = jnp.concatenate([block[: 2 * share], high], axis=1)
                rows = slice(2 * band * share, 2 * (band + 1) * share)
                exact_ref[sector, rows, :] = whole.astype(jnp.bfloat16)
                field_ref[sector, 2 * band] = whole[:share]
                field_ref[sector, 2 * band + 1] = whole[share:]

    took = lax.broadcasted_iota(jnp.int32, (2 * span, 2 * span), 0)
    gave = lax.broadcasted_iota(jnp.int32, (2 * span, 2 * span), 1)
    one, zero = jnp.float32(1.0), jnp.float32(0.0)
    picks = jnp.where((took + 1 == gave) & (took < span - 1), one, zero)
    picks = jnp.where((took == span + edge - 1) & (gave == 0), one, picks)
    picks = jnp.where((took + span - 1 == gave) & (took > 0) & (took < width), one, picks)
    picks = jnp.where((took == span + LANES) & (gave == span + width - 1), one, picks)
    picks = picks.astype(jnp.bfloat16)

    def shift_sector(sector, unused):
        after = lax.rem(sector + 1, sectors)
        before = lax.rem(sector + sectors - 1, sectors)
        beside = jnp.dot(
            jnp.concatenate(
                [exact_ref[sector], exact_ref[before, :, LANES:], exact_ref[after, :, :LANES]],
                axis=1,
            ),
            picks,
            preferred_element_type=jnp.float32,
        )
        west_ref[sector] = beside[:, :span].reshape(lat_total, share, span)
        east_ref[sector] = beside[:, span:].reshape(lat_total, share, span)
        return unused

    lax.fori_loop(0, sectors, shift_sector, 0)

    def filter_sector(sector, unused):
        def filter_rows(tile, unused):
            rows = pl.ds(pl.multiple_of(tile * 8, 8), 8)
            taps = []
            for k in range(9):
                tap = tap_ref[k, rows, :]
                taps.append(jnp.concatenate([tap, tap], axis=1))
            held, total, ahead = None, None, None

            def finish(t, value, sum_):
                first_ref[sector, pl.ds(pl.multiple_of(t * share + tile * 8, 8), 8), :] = value + gelu(sum_)

            for t in range(lat_total):
                value = field_ref[sector, t, rows, :]
                west = west_ref[sector, t, rows, :]
                east = east_ref[sector, t, rows, :]

                def weigh(row):
                    return (
                        taps[3 * row] * west + taps[3 * row + 1] * value + taps[3 * row + 2] * east
                    )

                if t > 0:
                    finish(t - 1, held, total + weigh(2))
                total = weigh(1) if t == 0 else ahead + weigh(1)
                ahead = weigh(0)
                held = value
            finish(lat_total - 1, held, total)
            return unused

        return lax.fori_loop(0, share // 8, filter_rows, unused)

    lax.fori_loop(0, sectors, filter_sector, 0)

    modes = None
    for sector in range(sectors):
        part = jnp.dot(
            first_ref[sector].astype(jnp.bfloat16),
            table_ref[sector],
            preferred_element_type=jnp.float32,
        )
        modes = part if modes is None else modes + part
    modes_ref[...] = modes

    sign = (1 - 2 * parity).astype(jnp.float32)
    folded = [[], []]
    for t in range(north):
        weight = 2.0 * math.pi * math.pi / lat_total * math.sin(math.pi * (t + 0.5) / lat_total)
        upper = weight * modes_ref[t * share : (t + 1) * share, :]
        mirror = lat_total - 1 - t
        lower = (weight * sign) * modes_ref[mirror * share : (mirror + 1) * share, :]
        folded[0].append(upper + lower)
        folded[1].append(upper - lower)

    sums = [[None] * north, [None] * north]

    def add(half, t, kernel, value):
        real = kernel[0] * value[:, :orders] - kernel[1] * value[:, orders:]
        imag = kernel[0] * value[:, orders:] + kernel[1] * value[:, :orders]
        had = sums[half][t]
        sums[half][t] = (real, imag) if had is None else (had[0] + real, had[1] + imag)

    for t in range(north):
        products = jnp.concatenate(
            [legendre_ref[t] * legendre_ref[s] for s in range(t, north)], axis=1
        )
        kernels = jnp.dot(gain_ref[...], products, preferred_element_type=jnp.float32)
        for s in range(t, north):
            at = slice((s - t) * orders, (s - t + 1) * orders)
            for half in range(2):
                base = 2 * half * share
                kernel = (kernels[base : base + share, at], kernels[base + share : base + 2 * share, at])
                add(half, t, kernel, folded[half][s])
                if s != t:
                    add(half, s, kernel, folded[half][t])

    for t in range(north):
        for part in range(2):
            even, odd = sums[0][t][part], sums[1][t][part]
            for place, value in ((t, even + odd), (lat_total - 1 - t, sign * (even - odd))):
                at = (place % 2) * 2 * orders + part * orders
                value = value.astype(jnp.bfloat16)
                for column in range(columns):
                    out_ref[column, place // 2, :, at : at + orders] = value


def stage_body(
    place_ref, own_ref, table_ref,
    mix_a_ref, mix_b_ref, mix_c_ref, mix_d_ref,
    field_ref, mix_ref, sems,
):
    place = place_ref[0]
    held = mix_a_ref.shape[1]
    loads = []
    for k, source in enumerate((mix_a_ref, mix_b_ref, mix_c_ref, mix_d_ref)):
        sector = 2 * (place // 2 if k < 2 else 1 - place // 2) + (
            place % 2 if k % 2 == 0 else 1 - place % 2
        )
        rows = pl.ds(pl.multiple_of(sector * held, held), held)
        loads.append(pltpu.make_async_copy(source, mix_ref.at[:, rows, :], sems.at[k]))
    for load in loads:
        load.start()
    modes = table_ref.shape[2]
    for row in range(2):
        field_ref[row] = lax.dot_general(
            table_ref[0], own_ref[:, row * modes : (row + 1) * modes], contract_last,
            preferred_element_type=jnp.float32,
        )
    for load in loads:
        load.wait()


def finish_body(
    width, padded,
    field_ref, other_ref, first_ref, gain_ref, table_ref, mix_ref, expand_ref, reduce_ref,
    marker_ref, out_ref,
):
    modes = table_ref.shape[2]
    real, imag = [], []
    for row in range(2):
        field = field_ref[row] + lax.dot_general(
            table_ref[1], other_ref[:, row * modes : (row + 1) * modes], contract_last,
            preferred_element_type=jnp.float32,
        )
        real.append(field[:padded])
        imag.append(field[padded:])
    real = jnp.concatenate(real, axis=0).astype(jnp.bfloat16)
    imag = jnp.concatenate(imag, axis=0).astype(jnp.bfloat16)
    spectral_out = lax.dot_general(
        real, mix_ref[0], contract_last, preferred_element_type=jnp.float32
    ) - lax.dot_general(imag, mix_ref[1], contract_last, preferred_element_type=jnp.float32)
    second = (first_ref[...].astype(jnp.float32) + spectral_out).astype(jnp.bfloat16)
    wide = second.astype(jnp.float32)
    scale = lax.rsqrt(jnp.mean(wide * wide, axis=-1, keepdims=True) + norm_eps)
    normed = (wide * gain_ref[...] * scale).astype(jnp.bfloat16)
    hidden = gelu(jnp.dot(normed, expand_ref[...], preferred_element_type=jnp.float32))
    update = jnp.dot(
        hidden.astype(jnp.bfloat16), reduce_ref[...], preferred_element_type=jnp.float32
    )
    result = wide + update
    for row in range(2):
        out_ref[row] = result[row * padded : row * padded + width].astype(jnp.bfloat16)


def local_body(
    width, padded, above_ref, grid_ref, below_ref, west_ref, east_ref, tap_ref,
    out_ref, marker_ref, tall_ref,
):
    marker_ref[...] = jnp.zeros_like(marker_ref)
    west, east = west_ref[...].astype(jnp.float32), east_ref[...].astype(jnp.float32)
    for k, row in enumerate((above_ref[...], grid_ref[0], grid_ref[1], below_ref[...])):
        tall_ref[k, 8 + width // 8 * 8 :, :] = jnp.zeros(
            (padded + 8 - width // 8 * 8, row.shape[1]), jnp.float32
        )
        tall_ref[k, 8 : 8 + width, :] = row.astype(jnp.float32)
        tall_ref[k, 7:8, :] = west[k : k + 1]
        tall_ref[k, 8 + width : 9 + width, :] = east[k : k + 1]
    inside = lax.broadcasted_iota(jnp.int32, (padded, LANES), 0) < width
    for piece in range(tall_ref.shape[2] // LANES):
        lanes = slice(piece * LANES, (piece + 1) * LANES)
        total = [None, None]
        for k in range(4):
            for col in range(3):
                value = tall_ref[k, 7 + col : 7 + col + padded, lanes]
                for row in range(2):
                    if 0 <= k - row < 3:
                        tap = tap_ref[3 * (k - row) + col : 3 * (k - row) + col + 1, lanes]
                        part = tap * value
                        total[row] = part if total[row] is None else total[row] + part
        for row in range(2):
            value = tall_ref[1 + row, 8 : 8 + padded, lanes] + gelu(total[row])
            value = jnp.where(inside, value, 0.0)
            total[row] = value
        out_ref[:, lanes] = jnp.concatenate(total, axis=0).astype(jnp.bfloat16)


def own_part(constant, at):
    return lax.dynamic_index_in_dim(jnp.asarray(constant), at, 0, keepdims=False)


def in_hbm(count):
    return [pl.BlockSpec(memory_space=pl.ANY)] * count


def in_vmem(count):
    return [pl.BlockSpec(memory_space=pltpu.VMEM)] * count


def chip_shards(
    grid_state, conv_weight, spectral_gain, spectral_weight, norm_gain, expand_weight, reduce_weight
):
    lat_rows, width, channels = grid_state.shape
    lat_count, columns = lax.axis_size("lat"), lax.axis_size("x")
    chips, sectors = lat_count * columns, 2 * columns
    share = channels // chips
    lat_total = lat_rows * lat_count
    orders = M // 2
    span = 2 * LANES
    padded = -(-width // 8) * 8
    lat_at, column, core = lax.axis_index("lat"), lax.axis_index("x"), lax.axis_index("core")
    swap = [(0, 1), (1, 0)]
    over_chips = ("x", "lat")

    packed = pl.pallas_call(
        functools.partial(pack_body, chips, share, width),
        out_shape=jax.ShapeDtypeStruct((chips, 3 * share, LANES), jnp.bfloat16),
        in_specs=in_vmem(1),
        out_specs=in_vmem(1)[0],
        scratch_shapes=[pltpu.VMEM((2, span, channels), jnp.float32)],
        compiler_params=pltpu.CompilerParams(vmem_limit_bytes=16 << 20),
        name="pack",
    )(grid_state)
    grid_first = grid_state
    packed, later = lax.optimization_barrier(
        (packed, (grid_state, conv_weight, spectral_gain, spectral_weight))
    )
    grid_state, conv_weight, spectral_gain, spectral_weight = later
    own = lax.all_to_all(packed, over_chips, split_axis=0, concat_axis=0, tiled=True)

    own_mix = spectral_weight.transpose(0, 2, 1)
    held = own_mix.shape[1]

    across_mix = lax.ppermute(own_mix, "x", [(i, 1 - i) for i in range(columns)])
    across_mix, spectral_gain = lax.optimization_barrier((across_mix, spectral_gain))
    blocks = held // share
    piece = lax.dynamic_slice_in_dim(
        spectral_gain, (lat_at % blocks) * share, share, axis=2
    ).transpose(0, 2, 1)
    piece_other = lax.ppermute(piece, "core", swap)
    gains = jnp.where(core == lat_at // blocks, piece, piece_other)
    even = (jnp.arange(M) % 2 == 0)[None, :]
    gain_rows = jnp.concatenate(
        [
            jnp.where(even, gains[0], 0.0),
            jnp.where(even, gains[1], 0.0),
            jnp.where(even, 0.0, gains[0]),
            jnp.where(even, 0.0, gains[1]),
        ],
        axis=0,
    ).astype(jnp.bfloat16)
    chip = column * lat_count + lat_at
    taps = lax.dynamic_slice_in_dim(conv_weight.reshape(9, channels), chip * share, share, axis=1)
    taps = jnp.broadcast_to(taps[:, :, None], (9, share, LANES))

    legendre = own_part(parity_tables(lat_total, M), core)
    analysis = own_part(analysis_constant(sectors, width, span, M), core)
    table = own_part(synthesis_constant(sectors, width, padded, M), 2 * column + core)

    own, across_mix = lax.optimization_barrier((own, across_mix))
    other = lax.ppermute(own, "core", swap)
    above = lax.ppermute(grid_first[1], "lat", [(i, i + 1) for i in range(lat_count - 1)])
    below = lax.ppermute(grid_first[0], "lat", [(i + 1, i) for i in range(lat_count - 1)])

    bands = pl.pallas_call(
        functools.partial(spectral_body, lat_count, columns, share, width),
        out_shape=jax.ShapeDtypeStruct((columns, lat_count, share, 2 * M), jnp.bfloat16),
        in_specs=[pl.BlockSpec(memory_space=pltpu.SMEM)]
        + in_vmem(1) + in_hbm(1) + in_vmem(4),
        out_specs=in_vmem(1)[0],
        scratch_shapes=[
            pltpu.VMEM((sectors, lat_total, share, span), jnp.float32),
            pltpu.VMEM((sectors, lat_total * share, span), jnp.bfloat16),
            pltpu.VMEM((sectors, lat_total, share, span), jnp.float32),
            pltpu.VMEM((sectors, lat_total, share, span), jnp.float32),
            pltpu.VMEM((sectors, lat_total * share, span), jnp.float32),
            pltpu.VMEM((lat_total * share, M), jnp.float32),
            pltpu.VMEM(own.shape, jnp.bfloat16),
            pltpu.SemaphoreType.DMA,
        ],
        cost_estimate=pl.CostEstimate(flops=9 * 10**9, bytes_accessed=0, transcendentals=0),
        compiler_params=pltpu.CompilerParams(vmem_limit_bytes=28 << 20),
        name="spectral",
    )(core[None], own, other, gain_rows, taps, legendre, analysis)
    bands, above, below, across_mix = lax.optimization_barrier((bands, above, below, across_mix))
    beside_mix = lax.ppermute(own_mix, "core", swap)
    far_mix = lax.ppermute(across_mix, "core", swap)
    ring = [(i, (i + 1) % sectors) for i in range(sectors)]
    tall = (above, grid_state[0], grid_state[1], below)
    west = lax.ppermute(
        jnp.stack([row[width - 1] for row in tall]), ("x", "core"), ring
    )
    east = lax.ppermute(
        jnp.stack([row[0] for row in tall]), ("x", "core"), [(j, i) for i, j in ring]
    )
    first_rows, marker = pl.pallas_call(
        functools.partial(local_body, width, padded),
        out_shape=[
            jax.ShapeDtypeStruct((2 * padded, channels), jnp.bfloat16),
            jax.ShapeDtypeStruct((8, LANES), jnp.float32),
        ],
        in_specs=in_vmem(6),
        out_specs=in_vmem(2),
        scratch_shapes=[pltpu.VMEM((4, padded + 16, channels), jnp.float32)],
        cost_estimate=pl.CostEstimate(flops=8 * 10**9, bytes_accessed=0, transcendentals=0),
        compiler_params=pltpu.CompilerParams(vmem_limit_bytes=16 << 20),
        name="local",
    )(above, grid_state, below, west, east, conv_weight.reshape(9, channels))
    back = lax.all_to_all(
        bands.reshape(chips, share, 2 * M), over_chips, split_axis=0, concat_axis=0, tiled=True
    ).reshape(channels, 2 * M)
    back, marker, table = lax.optimization_barrier((back, marker, table))
    back_other = lax.ppermute(back, "core", swap)

    field, mixing = pl.pallas_call(
        stage_body,
        out_shape=[
            jax.ShapeDtypeStruct((2, 2 * padded, channels), jnp.float32),
            jax.ShapeDtypeStruct((2, channels, channels), jnp.bfloat16),
        ],
        in_specs=[pl.BlockSpec(memory_space=pltpu.SMEM)] + in_vmem(2) + in_hbm(4),
        out_specs=in_vmem(2),
        scratch_shapes=[pltpu.SemaphoreType.DMA((4,))],
        cost_estimate=pl.CostEstimate(flops=12 * 10**9, bytes_accessed=0, transcendentals=0),
        compiler_params=pltpu.CompilerParams(vmem_limit_bytes=16 << 20),
        name="stage",
    )(
        (2 * column + core)[None], back, table,
        own_mix, beside_mix, across_mix, far_mix,
    )

    return pl.pallas_call(
        functools.partial(finish_body, width, padded),
        out_shape=jax.ShapeDtypeStruct(grid_state.shape, jnp.bfloat16),
        in_specs=in_vmem(9),
        out_specs=in_vmem(1)[0],
        cost_estimate=pl.CostEstimate(flops=3 * 10**9, bytes_accessed=0, transcendentals=0),
        compiler_params=pltpu.CompilerParams(vmem_limit_bytes=16 << 20),
        name="finish",
    )(
        field, back_other, first_rows, norm_gain[None, :], table, mixing, expand_weight,
        reduce_weight, marker,
    )


def solution(mesh):
    lat_count, lon_count = mesh.shape["lat"], mesh.shape["lon"]
    columns = lon_count // 2
    cored = Mesh(mesh.devices.reshape(lat_count, columns, 2), ("lat", "x", "core"))

    def run(grid_state, *rest):
        lat_total, lon_total, channels = grid_state.shape
        chips = lat_count * columns
        width = lon_total // lon_count
        fits = (
            columns == 2
            and lat_total == 2 * lat_count
            and lat_total <= 32
            and channels % (8 * chips) == 0
            and lat_count % 2 == 0
            and (channels // lon_count) * 2 == (channels // chips) * lat_count
            and LANES + 2 <= width
            and 2 * (width - LANES) <= LANES
        )
        if fits:
            body, on, lat, lon = chip_shards, cored, "lat", ("x", "core")
        else:
            body, on, lat, lon = banded_shards, mesh, "lat", "lon"
        return jax.shard_map(
            body,
            mesh=on,
            in_specs=(
                P(lat, lon, None), P(), P(None, None, lon), P(None, None, lon), P(), P(), P(),
            ),
            out_specs=P(lat, lon, None),
            check_vma=False,
        )(grid_state, *rest)

    return run
```

```python
import functools
import math

import jax
import jax.numpy as jnp
import numpy as np
from jax import lax
from jax.experimental import pallas as pl
from jax.experimental.pallas import tpu as pltpu
from jax.sharding import Mesh
from jax.sharding import PartitionSpec as P

M = 256
LANES = 128


norm_eps = 1e-06
underflow_cut = -60.0
degree_block = 16


def padded_2(value, sides, width, wrap):
    for axis, dim in sides:
        count, length = (lax.axis_size(axis), value.shape[dim])
        up = [(i, (i + 1) % count) for i in range(count if wrap else count - 1)]
        down = [(j, i) for i, j in up]
        last = lax.slice_in_dim(value, length - width, length, axis=dim)
        initial = lax.slice_in_dim(value, 0, width, axis=dim)
        before = lax.ppermute(last, axis, up)
        after = lax.ppermute(initial, axis, down)
        value = jnp.concatenate([before, value, after], axis=dim)
    return value


def legendre_table(orders, lat_total, degree_count):
    colatitude = (jnp.arange(lat_total, dtype=jnp.float32) + 0.5) * (math.pi / lat_total)
    cosines = jnp.cos(colatitude)
    sine_values = jnp.sin(colatitude)
    rank_values = jnp.arange(1, degree_count + 1, dtype=jnp.int32)
    rank_float = rank_values.astype(jnp.float32)
    log_terms = 0.5 * jnp.log((2.0 * rank_float + 1.0) / (2.0 * rank_float))
    log_norm = jnp.sum(
        jnp.where(rank_values[None, :] <= orders[:, None], log_terms[None, :], jnp.float32(0.0)),
        axis=1,
    )
    order_float = orders.astype(jnp.float32)[:, None]
    log_start = (
        -0.5 * math.log(4.0 * math.pi)
        + log_norm[:, None]
        + order_float * jnp.log(sine_values)[None, :]
    )
    start_value = jnp.where(
        log_start > underflow_cut, jnp.exp(jnp.maximum(log_start, underflow_cut)), jnp.float32(0.0)
    )

    def advance_block(totals, block_start):
        previous, earlier = totals
        rows_out = []
        for inner in range(degree_block):
            degree = block_start + inner
            degree_float = degree.astype(jnp.float32)
            raise_coef = jnp.sqrt(
                jnp.maximum(4.0 * degree_float * degree_float - 1.0, 0.0)
                / jnp.maximum(degree_float * degree_float - order_float * order_float, 1.0)
            )
            lower_coef = jnp.sqrt(
                jnp.maximum((degree_float - 1.0) ** 2 - order_float * order_float, 0.0)
                / jnp.maximum(4.0 * (degree_float - 1.0) ** 2 - 1.0, 1.0)
            )
            recurred = raise_coef * (cosines[None, :] * previous - lower_coef * earlier)
            current = jnp.where(
                degree < orders[:, None],
                jnp.float32(0.0),
                jnp.where(degree == orders[:, None], start_value, recurred),
            )
            earlier = previous
            previous = current
            rows_out.append(current)
        return ((previous, earlier), jnp.stack(rows_out, axis=0))

    blank = jnp.zeros((orders.shape[0], lat_total), jnp.float32)
    starts = jnp.arange(0, degree_count, degree_block, dtype=jnp.int32)
    unused, table_blocks = lax.scan(advance_block, (blank, blank), starts)
    return table_blocks.reshape(degree_count, orders.shape[0], lat_total)


def quadrature(lat_total):
    colatitude = (jnp.arange(lat_total, dtype=jnp.float32) + 0.5) * (math.pi / lat_total)
    return 2.0 * math.pi * math.pi / lat_total * jnp.sin(colatitude)


def fourier_table(longitudes, lon_total, mode_count):
    mode_index = jnp.arange(mode_count, dtype=jnp.int32)
    phase_index = longitudes[:, None] * mode_index[None, :] % lon_total
    angles = phase_index.astype(jnp.float32) * (2.0 * math.pi / lon_total)
    return (jnp.stack([jnp.cos(angles), -jnp.sin(angles)], axis=1) / lon_total).astype(jnp.bfloat16)


def synthesis_table(longitudes, lon_total, mode_count):
    mode_index = jnp.arange(mode_count, dtype=jnp.int32)
    phase_index = mode_index[:, None] * longitudes[None, :] % lon_total
    angles = phase_index.astype(jnp.float32) * (2.0 * math.pi / lon_total)
    doubling = jnp.where(mode_index == 0, 1.0, 2.0).astype(jnp.float32)[:, None]
    return jnp.stack([doubling * jnp.cos(angles), -doubling * jnp.sin(angles)], axis=0).astype(
        jnp.bfloat16
    )


def banded_shards(
    grid_state, conv_weight, spectral_gain, spectral_weight, norm_gain, expand_weight, reduce_weight
):
    lat_rows, sector_width, channel_total = grid_state.shape
    lat_count = lax.axis_size("lat")
    lon_count = lax.axis_size("lon")
    lat_total = lat_rows * lat_count
    lon_total = sector_width * lon_count
    mode_count = M
    order_share = mode_count // lat_count
    channel_share = channel_total // lon_count
    lat_position = lax.axis_index("lat")
    wrapped = padded_2(grid_state, (("lon", 1),), 1, True)
    padded = padded_2(wrapped, (("lat", 0),), 1, False)
    padded_wide = padded.astype(jnp.float32)
    filtered = jnp.zeros((lat_rows, sector_width, channel_total), jnp.float32)
    for row_shift in range(3):
        for col_shift in range(3):
            filtered = (
                filtered
                + conv_weight[row_shift, col_shift]
                * padded_wide[
                    row_shift : row_shift + lat_rows, col_shift : col_shift + sector_width
                ]
            )
    first_section = (grid_state.astype(jnp.float32) + jax.nn.gelu(filtered)).astype(jnp.bfloat16)
    gathered = lax.all_to_all(first_section, "lon", split_axis=2, concat_axis=1, tiled=True)
    forward_table = fourier_table(jnp.arange(lon_total, dtype=jnp.int32), lon_total, mode_count)
    spectrum = jnp.einsum(
        "tpc,prm->tmrc", gathered, forward_table, preferred_element_type=jnp.float32
    ).astype(jnp.bfloat16)
    cycle_spectrum = lax.all_to_all(spectrum, "lat", split_axis=1, concat_axis=0, tiled=True)
    orders = lat_position * order_share + jnp.arange(order_share, dtype=jnp.int32)
    legendre = legendre_table(orders, lat_total, mode_count)
    analysis_table = (legendre * quadrature(lat_total)[None, None, :]).astype(jnp.bfloat16)
    coefficients = jnp.einsum(
        "lmt,tmrc->lmrc", analysis_table, cycle_spectrum, preferred_element_type=jnp.float32
    )
    gain_real = spectral_gain[0][:, None, :]
    gain_imag = spectral_gain[1][:, None, :]
    coef_real = coefficients[:, :, 0, :]
    coef_imag = coefficients[:, :, 1, :]
    gained = jnp.stack(
        [
            gain_real * coef_real - gain_imag * coef_imag,
            gain_real * coef_imag + gain_imag * coef_real,
        ],
        axis=2,
    ).astype(jnp.bfloat16)
    blank = jnp.zeros((mode_count * order_share, channel_share), jnp.float32)
    portion = lax.all_gather(gained, "lon", axis=3, tiled=True)
    width_part = portion.shape[3]
    weight_rows = lax.slice_in_dim(spectral_weight, 0, width_part, axis=1)
    real_part = portion[:, :, 0, :].reshape(-1, width_part)
    imag_part = portion[:, :, 1, :].reshape(-1, width_part)
    real_sum = (
        blank
        + jnp.dot(real_part, weight_rows[0], preferred_element_type=jnp.float32)
        - jnp.dot(imag_part, weight_rows[1], preferred_element_type=jnp.float32)
    )
    imag_sum = (
        blank
        + jnp.dot(real_part, weight_rows[1], preferred_element_type=jnp.float32)
        + jnp.dot(imag_part, weight_rows[0], preferred_element_type=jnp.float32)
    )
    mixed = jnp.stack(
        [
            real_sum.reshape(mode_count, order_share, channel_share),
            imag_sum.reshape(mode_count, order_share, channel_share),
        ],
        axis=2,
    ).astype(jnp.bfloat16)
    synthesis_legendre = legendre.astype(jnp.bfloat16)
    cycle_modes = jnp.einsum(
        "lmt,lmrc->tmrc", synthesis_legendre, mixed, preferred_element_type=jnp.float32
    ).astype(jnp.bfloat16)
    band_modes = lax.all_to_all(cycle_modes, "lat", split_axis=0, concat_axis=1, tiled=True)
    inverse_table = synthesis_table(jnp.arange(lon_total, dtype=jnp.int32), lon_total, mode_count)
    all_lons = jnp.einsum(
        "tmrc,rmp->tpc", band_modes, inverse_table, preferred_element_type=jnp.float32
    )
    spectral_out = lax.all_to_all(
        all_lons.astype(jnp.bfloat16), "lon", split_axis=1, concat_axis=2, tiled=True
    ).astype(all_lons.dtype)
    second_section = (first_section.astype(jnp.float32) + spectral_out).astype(jnp.bfloat16)
    second_wide = second_section.astype(jnp.float32)
    scale_values = lax.rsqrt(jnp.mean(second_wide * second_wide, axis=-1, keepdims=True) + norm_eps)
    normed = (second_wide * norm_gain * scale_values).astype(jnp.bfloat16)
    flat_rows = normed.reshape(-1, channel_total)
    hidden = jax.nn.gelu(
        jnp.dot(flat_rows, expand_weight, preferred_element_type=jnp.float32)
    ).astype(jnp.bfloat16)
    update = jnp.dot(hidden, reduce_weight, preferred_element_type=jnp.float32)
    block_output = (second_wide.reshape(-1, channel_total) + update).astype(jnp.bfloat16)
    return block_output.reshape(lat_rows, sector_width, channel_total)


contract_last = (((1,), (1,)), ((), ()))


def legendre_constant(lat_total, mode_count):
    colatitude = (np.arange(lat_total // 2) + 0.5) * (math.pi / lat_total)
    cosines, sines = np.cos(colatitude)[:, None], np.sin(colatitude)[:, None]
    orders = np.arange(mode_count, dtype=np.float64)
    ranks = np.arange(1, mode_count, dtype=np.float64)
    log_terms = 0.5 * np.log((2.0 * ranks + 1.0) / (2.0 * ranks))
    log_norm = np.concatenate([np.zeros(1), np.cumsum(log_terms)])
    log_start = -0.5 * math.log(4.0 * math.pi) + log_norm + orders * np.log(sines)
    start = np.where(
        log_start > underflow_cut, np.exp(np.maximum(log_start, underflow_cut)), 0.0
    )
    table = np.zeros((lat_total // 2, mode_count, mode_count))
    previous = np.zeros_like(start)
    earlier = np.zeros_like(start)
    for degree in range(mode_count):
        raised = np.sqrt(
            np.maximum(4.0 * degree * degree - 1.0, 0.0)
            / np.maximum(degree * degree - orders * orders, 1.0)
        )
        lowered = np.sqrt(
            np.maximum((degree - 1.0) ** 2 - orders * orders, 0.0)
            / max(4.0 * (degree - 1.0) ** 2 - 1.0, 1.0)
        )
        recurred = raised * (cosines * previous - lowered * earlier)
        current = np.where(degree < orders, 0.0, np.where(degree == orders, start, recurred))
        earlier, previous = previous, current
        table[:, degree, :] = current
    return table


def parity_tables(lat_total, mode_count):
    table = legendre_constant(lat_total, mode_count)
    return np.stack([table[:, :, 0::2], table[:, :, 1::2]]).astype(jnp.bfloat16)


def analysis_constant(sectors, width, span, mode_count):
    lon_total = sectors * width
    out = np.zeros((2, sectors, span, 2, mode_count // 2))
    for parity in range(2):
        modes = np.arange(parity, mode_count, 2)
        for sector in range(sectors):
            longitudes = sector * width + np.arange(width)
            angles = (longitudes[:, None] * modes[None, :] % lon_total) * (2 * math.pi / lon_total)
            out[parity, sector, :width, 0] = np.cos(angles) / lon_total
            out[parity, sector, :width, 1] = -np.sin(angles) / lon_total
    return out.reshape(2, sectors, span, mode_count).astype(jnp.bfloat16)


def synthesis_constant(sectors, width, padded, mode_count):
    lon_total = sectors * width
    out = np.zeros((sectors, 2, 2, padded, 2, mode_count // 2))
    for sector in range(sectors):
        longitudes = sector * width + np.arange(width)
        for half in range(2):
            modes = np.arange((sector + half) % 2, mode_count, 2)
            doubling = np.where(modes == 0, 1.0, 2.0)[None, :]
            angles = (longitudes[:, None] * modes[None, :] % lon_total) * (2 * math.pi / lon_total)
            cosine, sine = doubling * np.cos(angles), doubling * np.sin(angles)
            out[sector, half, 0, :width, 0] = cosine
            out[sector, half, 0, :width, 1] = -sine
            out[sector, half, 1, :width, 0] = sine
            out[sector, half, 1, :width, 1] = cosine
    return out.reshape(sectors, 2, 2 * padded, mode_count).astype(jnp.bfloat16)


def gelu(value):
    inner = value * (0.7978845608028654 + (0.7978845608028654 * 0.044715) * (value * value))
    half = 0.5 * value
    return half + half * jnp.tanh(inner)


def pack_body(chips, share, width, grid_ref, out_ref, wide_ref):
    span = wide_ref.shape[1]
    tail = width // 8 * 8
    flipped = []
    for row in range(2):
        wide_ref[row, tail:span, :] = jnp.zeros((span - tail, chips * share), jnp.float32)
        wide_ref[row, 0:width, :] = grid_ref[row].astype(jnp.float32)
        flipped.append(wide_ref[row].T)
    rest = flipped[0][:, LANES:] + pltpu.roll(flipped[1][:, LANES:], width - LANES, axis=1)
    for chip in range(chips):
        at = slice(chip * share, (chip + 1) * share)
        block = jnp.concatenate(
            [flipped[0][at, :LANES], flipped[1][at, :LANES], rest[at]], axis=0
        )
        out_ref[chip] = block.astype(jnp.bfloat16)


def spectral_body(
    lat_count, columns, share, width,
    parity_ref, own_ref, other_ref, gain_ref, tap_ref, legendre_ref, table_ref, out_ref,
    field_ref, exact_ref, west_ref, east_ref, first_ref, modes_ref,
):
    lat_total = 2 * lat_count
    north = lat_total // 2
    sectors = 2 * columns
    edge = width - LANES
    span = 2 * LANES
    orders = legendre_ref.shape[2]
    parity = parity_ref[0]
    for source, core in ((own_ref, parity), (other_ref, 1 - parity)):
        for column in range(columns):
            sector = 2 * column + core
            for band in range(lat_count):
                block = source[column * lat_count + band].astype(jnp.float32)
                rest = block[2 * share :]
                high = jnp.concatenate([rest, pltpu.roll(rest, LANES - edge, axis=1)], axis=0)
                whole = jnp.concatenate([block[: 2 * share], high], axis=1)
                rows = slice(2 * band * share, 2 * (band + 1) * share)
                exact_ref[sector, rows, :] = whole.astype(jnp.bfloat16)
                field_ref[sector, 2 * band] = whole[:share]
                field_ref[sector, 2 * band + 1] = whole[share:]

    took = lax.broadcasted_iota(jnp.int32, (span, span), 0)
    gave = lax.broadcasted_iota(jnp.int32, (span, span), 1)
    one, zero = jnp.float32(1.0), jnp.float32(0.0)

    inner = jnp.where((took + 1 == gave + LANES) & (gave < LANES), one, zero)
    inner = jnp.where((took == gave - LANES + 1) & (gave >= LANES), one, inner)
    inner = inner.astype(jnp.bfloat16)
    to_west = jnp.where((took == gave + LANES - 1) & (gave > 0), one, zero)
    to_west = jnp.where((took == edge - 1) & (gave == 0), one, to_west)
    to_west = to_west[:, :LANES].astype(jnp.bfloat16)
    to_east = jnp.where((took == gave + 1) & (gave < edge - 1), one, zero)
    to_east = jnp.where((took == LANES) & (gave == edge - 1), one, to_east)
    to_east = to_east[:, :LANES].astype(jnp.bfloat16)

    def spread(value):
        return value.reshape(lat_total, share, LANES)

    for sector in range(sectors):
        middle = jnp.dot(exact_ref[sector], inner, preferred_element_type=jnp.float32)
        west_ref[sector, :, :, LANES:] = spread(middle[:, :LANES])
        east_ref[sector, :, :, :LANES] = spread(middle[:, LANES:])
        before = jnp.concatenate(
            [exact_ref[(sector - 1) % sectors, :, LANES:], exact_ref[sector, :, :LANES]], axis=1
        )
        west_ref[sector, :, :, :LANES] = spread(
            jnp.dot(before, to_west, preferred_element_type=jnp.float32)
        )
        after = jnp.concatenate(
            [exact_ref[sector, :, LANES:], exact_ref[(sector + 1) % sectors, :, :LANES]], axis=1
        )
        east_ref[sector, :, :, LANES:] = spread(
            jnp.dot(after, to_east, preferred_element_type=jnp.float32)
        )

    def filter_sector(sector, unused):
        def filter_rows(tile, unused):
            rows = pl.ds(pl.multiple_of(tile * 8, 8), 8)
            taps = []
            for k in range(9):
                tap = tap_ref[k, rows, :]
                taps.append(jnp.concatenate([tap, tap], axis=1))
            held, total, ahead = None, None, None

            def finish(t, value, sum_):
                first_ref[sector, pl.ds(pl.multiple_of(t * share + tile * 8, 8), 8), :] = value + gelu(sum_)

            for t in range(lat_total):
                value = field_ref[sector, t, rows, :]
                west = west_ref[sector, t, rows, :]
                east = east_ref[sector, t, rows, :]

                def weigh(row):
                    return (
                        taps[3 * row] * west + taps[3 * row + 1] * value + taps[3 * row + 2] * east
                    )

                if t > 0:
                    finish(t - 1, held, total + weigh(2))
                total = weigh(1) if t == 0 else ahead + weigh(1)
                ahead = weigh(0)
                held = value
            finish(lat_total - 1, held, total)
            return unused

        return lax.fori_loop(0, share // 8, filter_rows, unused)

    lax.fori_loop(0, sectors, filter_sector, 0)

    modes = None
    for sector in range(sectors):
        part = jnp.dot(
            first_ref[sector].astype(jnp.bfloat16),
            table_ref[sector],
            preferred_element_type=jnp.float32,
        )
        modes = part if modes is None else modes + part
    modes_ref[...] = modes

    sign = (1 - 2 * parity).astype(jnp.float32)
    folded = [[], []]
    for t in range(north):
        weight = 2.0 * math.pi * math.pi / lat_total * math.sin(math.pi * (t + 0.5) / lat_total)
        upper = weight * modes_ref[t * share : (t + 1) * share, :]
        mirror = lat_total - 1 - t
        lower = (weight * sign) * modes_ref[mirror * share : (mirror + 1) * share, :]
        folded[0].append(upper + lower)
        folded[1].append(upper - lower)

    sums = [[None] * north, [None] * north]

    def add(half, t, kernel, value):
        real = kernel[0] * value[:, :orders] - kernel[1] * value[:, orders:]
        imag = kernel[0] * value[:, orders:] + kernel[1] * value[:, :orders]
        had = sums[half][t]
        sums[half][t] = (real, imag) if had is None else (had[0] + real, had[1] + imag)

    for t in range(north):
        products = jnp.concatenate(
            [legendre_ref[t] * legendre_ref[s] for s in range(t, north)], axis=1
        )
        kernels = jnp.dot(gain_ref[...], products, preferred_element_type=jnp.float32)
        for s in range(t, north):
            at = slice((s - t) * orders, (s - t + 1) * orders)
            for half in range(2):
                base = 2 * half * share
                kernel = (kernels[base : base + share, at], kernels[base + share : base + 2 * share, at])
                add(half, t, kernel, folded[half][s])
                if s != t:
                    add(half, s, kernel, folded[half][t])

    for t in range(north):
        for part in range(2):
            even, odd = sums[0][t][part], sums[1][t][part]
            for place, value in ((t, even + odd), (lat_total - 1 - t, sign * (even - odd))):
                at = (place % 2) * 2 * orders + part * orders
                value = value.astype(jnp.bfloat16)
                for column in range(columns):
                    out_ref[column, place // 2, :, at : at + orders] = value


def stage_body(
    place_ref, own_ref, table_ref,
    mix_a_ref, mix_b_ref, mix_c_ref, mix_d_ref,
    field_ref, mix_ref, sems,
):
    place = place_ref[0]
    held = mix_a_ref.shape[1]
    loads = []
    for k, source in enumerate((mix_a_ref, mix_b_ref, mix_c_ref, mix_d_ref)):
        sector = 2 * (place // 2 if k < 2 else 1 - place // 2) + (
            place % 2 if k % 2 == 0 else 1 - place % 2
        )
        rows = pl.ds(pl.multiple_of(sector * held, held), held)
        loads.append(pltpu.make_async_copy(source, mix_ref.at[:, rows, :], sems.at[k]))
    for load in loads:
        load.start()
    modes = table_ref.shape[2]
    for row in range(2):
        field_ref[row] = lax.dot_general(
            table_ref[0], own_ref[:, row * modes : (row + 1) * modes], contract_last,
            preferred_element_type=jnp.float32,
        )
    for load in loads:
        load.wait()


def finish_body(
    width, padded,
    field_ref, other_ref, first_ref, gain_ref, table_ref, mix_ref, expand_ref, reduce_ref,
    marker_ref, out_ref,
):
    modes = table_ref.shape[2]
    real, imag = [], []
    for row in range(2):
        field = field_ref[row] + lax.dot_general(
            table_ref[1], other_ref[:, row * modes : (row + 1) * modes], contract_last,
            preferred_element_type=jnp.float32,
        )
        real.append(field[:padded])
        imag.append(field[padded:])
    real = jnp.concatenate(real, axis=0).astype(jnp.bfloat16)
    imag = jnp.concatenate(imag, axis=0).astype(jnp.bfloat16)
    spectral_out = lax.dot_general(
        real, mix_ref[0], contract_last, preferred_element_type=jnp.float32
    ) - lax.dot_general(imag, mix_ref[1], contract_last, preferred_element_type=jnp.float32)
    second = (first_ref[...].astype(jnp.float32) + spectral_out).astype(jnp.bfloat16)
    wide = second.astype(jnp.float32)
    scale = lax.rsqrt(jnp.mean(wide * wide, axis=-1, keepdims=True) + norm_eps)
    normed = (wide * gain_ref[...] * scale).astype(jnp.bfloat16)
    hidden = gelu(jnp.dot(normed, expand_ref[...], preferred_element_type=jnp.float32))
    update = jnp.dot(
        hidden.astype(jnp.bfloat16), reduce_ref[...], preferred_element_type=jnp.float32
    )
    result = wide + update
    for row in range(2):
        out_ref[row] = result[row * padded : row * padded + width].astype(jnp.bfloat16)


def local_body(
    width, padded, above_ref, grid_ref, below_ref, west_ref, east_ref, tap_ref,
    out_ref, marker_ref, tall_ref,
):
    marker_ref[...] = jnp.zeros_like(marker_ref)
    west, east = west_ref[...].astype(jnp.float32), east_ref[...].astype(jnp.float32)
    for k, row in enumerate((above_ref[...], grid_ref[0], grid_ref[1], below_ref[...])):
        tall_ref[k, 8 + width // 8 * 8 :, :] = jnp.zeros(
            (padded + 8 - width // 8 * 8, row.shape[1]), jnp.float32
        )
        tall_ref[k, 8 : 8 + width, :] = row.astype(jnp.float32)
        tall_ref[k, 7:8, :] = west[k : k + 1]
        tall_ref[k, 8 + width : 9 + width, :] = east[k : k + 1]
    inside = lax.broadcasted_iota(jnp.int32, (padded, LANES), 0) < width
    for piece in range(tall_ref.shape[2] // LANES):
        lanes = slice(piece * LANES, (piece + 1) * LANES)
        total = [None, None]
        for k in range(4):
            for col in range(3):
                value = tall_ref[k, 7 + col : 7 + col + padded, lanes]
                for row in range(2):
                    if 0 <= k - row < 3:
                        tap = tap_ref[3 * (k - row) + col : 3 * (k - row) + col + 1, lanes]
                        part = tap * value
                        total[row] = part if total[row] is None else total[row] + part
        for row in range(2):
            value = tall_ref[1 + row, 8 : 8 + padded, lanes] + gelu(total[row])
            value = jnp.where(inside, value, 0.0)
            total[row] = value
        out_ref[:, lanes] = jnp.concatenate(total, axis=0).astype(jnp.bfloat16)


def own_part(constant, at):
    return lax.dynamic_index_in_dim(jnp.asarray(constant), at, 0, keepdims=False)


def in_hbm(count):
    return [pl.BlockSpec(memory_space=pl.ANY)] * count


def in_vmem(count):
    return [pl.BlockSpec(memory_space=pltpu.VMEM)] * count


def chip_shards(
    grid_state, conv_weight, spectral_gain, spectral_weight, norm_gain, expand_weight, reduce_weight
):
    lat_rows, width, channels = grid_state.shape
    lat_count, columns = lax.axis_size("lat"), lax.axis_size("x")
    chips, sectors = lat_count * columns, 2 * columns
    share = channels // chips
    lat_total = lat_rows * lat_count
    orders = M // 2
    span = 2 * LANES
    padded = -(-width // 8) * 8
    lat_at, column, core = lax.axis_index("lat"), lax.axis_index("x"), lax.axis_index("core")
    swap = [(0, 1), (1, 0)]
    over_chips = ("x", "lat")

    packed = pl.pallas_call(
        functools.partial(pack_body, chips, share, width),
        out_shape=jax.ShapeDtypeStruct((chips, 3 * share, LANES), jnp.bfloat16),
        in_specs=in_vmem(1),
        out_specs=in_vmem(1)[0],
        scratch_shapes=[pltpu.VMEM((2, span, channels), jnp.float32)],
        compiler_params=pltpu.CompilerParams(vmem_limit_bytes=16 << 20),
        name="pack",
    )(grid_state)
    grid_first = grid_state
    packed, later = lax.optimization_barrier(
        (packed, (grid_state, conv_weight, spectral_gain, spectral_weight))
    )
    grid_state, conv_weight, spectral_gain, spectral_weight = later
    own = lax.all_to_all(packed, over_chips, split_axis=0, concat_axis=0, tiled=True)

    own_mix = spectral_weight.transpose(0, 2, 1)
    held = own_mix.shape[1]

    across_mix = lax.ppermute(own_mix, "x", [(i, 1 - i) for i in range(columns)])
    across_mix, spectral_gain = lax.optimization_barrier((across_mix, spectral_gain))
    blocks = held // share
    piece = lax.dynamic_slice_in_dim(
        spectral_gain, (lat_at % blocks) * share, share, axis=2
    ).transpose(0, 2, 1)
    piece_other = lax.ppermute(piece, "core", swap)
    gains = jnp.where(core == lat_at // blocks, piece, piece_other)
    even = (jnp.arange(M) % 2 == 0)[None, :]
    gain_rows = jnp.concatenate(
        [
            jnp.where(even, gains[0], 0.0),
            jnp.where(even, gains[1], 0.0),
            jnp.where(even, 0.0, gains[0]),
            jnp.where(even, 0.0, gains[1]),
        ],
        axis=0,
    ).astype(jnp.bfloat16)
    chip = column * lat_count + lat_at
    taps = lax.dynamic_slice_in_dim(conv_weight.reshape(9, channels), chip * share, share, axis=1)
    taps = jnp.broadcast_to(taps[:, :, None], (9, share, LANES))

    legendre = own_part(parity_tables(lat_total, M), core)
    analysis = own_part(analysis_constant(sectors, width, span, M), core)
    table = own_part(synthesis_constant(sectors, width, padded, M), 2 * column + core)

    own, across_mix = lax.optimization_barrier((own, across_mix))
    other = lax.ppermute(own, "core", swap)
    above = lax.ppermute(grid_first[1], "lat", [(i, i + 1) for i in range(lat_count - 1)])
    below = lax.ppermute(grid_first[0], "lat", [(i + 1, i) for i in range(lat_count - 1)])

    bands = pl.pallas_call(
        functools.partial(spectral_body, lat_count, columns, share, width),
        out_shape=jax.ShapeDtypeStruct((columns, lat_count, share, 2 * M), jnp.bfloat16),
        in_specs=[pl.BlockSpec(memory_space=pltpu.SMEM)] + in_vmem(6),
        out_specs=in_vmem(1)[0],
        scratch_shapes=[
            pltpu.VMEM((sectors, lat_total, share, span), jnp.float32),
            pltpu.VMEM((sectors, lat_total * share, span), jnp.bfloat16),
            pltpu.VMEM((sectors, lat_total, share, span), jnp.float32),
            pltpu.VMEM((sectors, lat_total, share, span), jnp.float32),
            pltpu.VMEM((sectors, lat_total * share, span), jnp.float32),
            pltpu.VMEM((lat_total * share, M), jnp.float32),
        ],
        cost_estimate=pl.CostEstimate(flops=9 * 10**9, bytes_accessed=0, transcendentals=0),
        compiler_params=pltpu.CompilerParams(vmem_limit_bytes=28 << 20),
        name="spectral",
    )(core[None], own, other, gain_rows, taps, legendre, analysis)
    bands, above, below, across_mix = lax.optimization_barrier((bands, above, below, across_mix))
    beside_mix = lax.ppermute(own_mix, "core", swap)
    far_mix = lax.ppermute(across_mix, "core", swap)
    ring = [(i, (i + 1) % sectors) for i in range(sectors)]
    tall = (above, grid_state[0], grid_state[1], below)
    west = lax.ppermute(
        jnp.stack([row[width - 1] for row in tall]), ("x", "core"), ring
    )
    east = lax.ppermute(
        jnp.stack([row[0] for row in tall]), ("x", "core"), [(j, i) for i, j in ring]
    )
    first_rows, marker = pl.pallas_call(
        functools.partial(local_body, width, padded),
        out_shape=[
            jax.ShapeDtypeStruct((2 * padded, channels), jnp.bfloat16),
            jax.ShapeDtypeStruct((8, LANES), jnp.float32),
        ],
        in_specs=in_vmem(6),
        out_specs=in_vmem(2),
        scratch_shapes=[pltpu.VMEM((4, padded + 16, channels), jnp.float32)],
        cost_estimate=pl.CostEstimate(flops=8 * 10**9, bytes_accessed=0, transcendentals=0),
        compiler_params=pltpu.CompilerParams(vmem_limit_bytes=16 << 20),
        name="local",
    )(above, grid_state, below, west, east, conv_weight.reshape(9, channels))
    back = lax.all_to_all(
        bands.reshape(chips, share, 2 * M), over_chips, split_axis=0, concat_axis=0, tiled=True
    ).reshape(channels, 2 * M)
    back, marker, table = lax.optimization_barrier((back, marker, table))
    back_other = lax.ppermute(back, "core", swap)

    field, mixing = pl.pallas_call(
        stage_body,
        out_shape=[
            jax.ShapeDtypeStruct((2, 2 * padded, channels), jnp.float32),
            jax.ShapeDtypeStruct((2, channels, channels), jnp.bfloat16),
        ],
        in_specs=[pl.BlockSpec(memory_space=pltpu.SMEM)] + in_vmem(2) + in_hbm(4),
        out_specs=in_vmem(2),
        scratch_shapes=[pltpu.SemaphoreType.DMA((4,))],
        cost_estimate=pl.CostEstimate(flops=12 * 10**9, bytes_accessed=0, transcendentals=0),
        compiler_params=pltpu.CompilerParams(vmem_limit_bytes=16 << 20),
        name="stage",
    )(
        (2 * column + core)[None], back, table,
        own_mix, beside_mix, across_mix, far_mix,
    )

    return pl.pallas_call(
        functools.partial(finish_body, width, padded),
        out_shape=jax.ShapeDtypeStruct(grid_state.shape, jnp.bfloat16),
        in_specs=in_vmem(9),
        out_specs=in_vmem(1)[0],
        cost_estimate=pl.CostEstimate(flops=3 * 10**9, bytes_accessed=0, transcendentals=0),
        compiler_params=pltpu.CompilerParams(vmem_limit_bytes=16 << 20),
        name="finish",
    )(
        field, back_other, first_rows, norm_gain[None, :], table, mixing, expand_weight,
        reduce_weight, marker,
    )


def solution(mesh):
    lat_count, lon_count = mesh.shape["lat"], mesh.shape["lon"]
    columns = lon_count // 2
    cored = Mesh(mesh.devices.reshape(lat_count, columns, 2), ("lat", "x", "core"))

    def run(grid_state, *rest):
        lat_total, lon_total, channels = grid_state.shape
        chips = lat_count * columns
        width = lon_total // lon_count
        fits = (
            columns == 2
            and lat_total == 2 * lat_count
            and lat_total <= 32
            and channels % (8 * chips) == 0
            and lat_count % 2 == 0
            and (channels // lon_count) * 2 == (channels // chips) * lat_count
            and LANES + 2 <= width
            and 2 * (width - LANES) <= LANES
        )
        if fits:
            body, on, lat, lon = chip_shards, cored, "lat", ("x", "core")
        else:
            body, on, lat, lon = banded_shards, mesh, "lat", "lon"
        return jax.shard_map(
            body,
            mesh=on,
            in_specs=(
                P(lat, lon, None), P(), P(None, None, lon), P(None, None, lon), P(), P(), P(),
            ),
            out_specs=P(lat, lon, None),
            check_vma=False,
        )(grid_state, *rest)

    return run
```

```python
import functools
import math

import jax
import jax.numpy as jnp
import numpy as np
from jax import lax
from jax.experimental import pallas as pl
from jax.experimental.pallas import tpu as pltpu
from jax.sharding import Mesh
from jax.sharding import PartitionSpec as P

M = 256
LANES = 128


norm_eps = 1e-06
underflow_cut = -60.0
degree_block = 16


def padded_2(value, sides, width, wrap):
    for axis, dim in sides:
        count, length = (lax.axis_size(axis), value.shape[dim])
        up = [(i, (i + 1) % count) for i in range(count if wrap else count - 1)]
        down = [(j, i) for i, j in up]
        last = lax.slice_in_dim(value, length - width, length, axis=dim)
        initial = lax.slice_in_dim(value, 0, width, axis=dim)
        before = lax.ppermute(last, axis, up)
        after = lax.ppermute(initial, axis, down)
        value = jnp.concatenate([before, value, after], axis=dim)
    return value


def legendre_table(orders, lat_total, degree_count):
    colatitude = (jnp.arange(lat_total, dtype=jnp.float32) + 0.5) * (math.pi / lat_total)
    cosines = jnp.cos(colatitude)
    sine_values = jnp.sin(colatitude)
    rank_values = jnp.arange(1, degree_count + 1, dtype=jnp.int32)
    rank_float = rank_values.astype(jnp.float32)
    log_terms = 0.5 * jnp.log((2.0 * rank_float + 1.0) / (2.0 * rank_float))
    log_norm = jnp.sum(
        jnp.where(rank_values[None, :] <= orders[:, None], log_terms[None, :], jnp.float32(0.0)),
        axis=1,
    )
    order_float = orders.astype(jnp.float32)[:, None]
    log_start = (
        -0.5 * math.log(4.0 * math.pi)
        + log_norm[:, None]
        + order_float * jnp.log(sine_values)[None, :]
    )
    start_value = jnp.where(
        log_start > underflow_cut, jnp.exp(jnp.maximum(log_start, underflow_cut)), jnp.float32(0.0)
    )

    def advance_block(totals, block_start):
        previous, earlier = totals
        rows_out = []
        for inner in range(degree_block):
            degree = block_start + inner
            degree_float = degree.astype(jnp.float32)
            raise_coef = jnp.sqrt(
                jnp.maximum(4.0 * degree_float * degree_float - 1.0, 0.0)
                / jnp.maximum(degree_float * degree_float - order_float * order_float, 1.0)
            )
            lower_coef = jnp.sqrt(
                jnp.maximum((degree_float - 1.0) ** 2 - order_float * order_float, 0.0)
                / jnp.maximum(4.0 * (degree_float - 1.0) ** 2 - 1.0, 1.0)
            )
            recurred = raise_coef * (cosines[None, :] * previous - lower_coef * earlier)
            current = jnp.where(
                degree < orders[:, None],
                jnp.float32(0.0),
                jnp.where(degree == orders[:, None], start_value, recurred),
            )
            earlier = previous
            previous = current
            rows_out.append(current)
        return ((previous, earlier), jnp.stack(rows_out, axis=0))

    blank = jnp.zeros((orders.shape[0], lat_total), jnp.float32)
    starts = jnp.arange(0, degree_count, degree_block, dtype=jnp.int32)
    unused, table_blocks = lax.scan(advance_block, (blank, blank), starts)
    return table_blocks.reshape(degree_count, orders.shape[0], lat_total)


def quadrature(lat_total):
    colatitude = (jnp.arange(lat_total, dtype=jnp.float32) + 0.5) * (math.pi / lat_total)
    return 2.0 * math.pi * math.pi / lat_total * jnp.sin(colatitude)


def fourier_table(longitudes, lon_total, mode_count):
    mode_index = jnp.arange(mode_count, dtype=jnp.int32)
    phase_index = longitudes[:, None] * mode_index[None, :] % lon_total
    angles = phase_index.astype(jnp.float32) * (2.0 * math.pi / lon_total)
    return (jnp.stack([jnp.cos(angles), -jnp.sin(angles)], axis=1) / lon_total).astype(jnp.bfloat16)


def synthesis_table(longitudes, lon_total, mode_count):
    mode_index = jnp.arange(mode_count, dtype=jnp.int32)
    phase_index = mode_index[:, None] * longitudes[None, :] % lon_total
    angles = phase_index.astype(jnp.float32) * (2.0 * math.pi / lon_total)
    doubling = jnp.where(mode_index == 0, 1.0, 2.0).astype(jnp.float32)[:, None]
    return jnp.stack([doubling * jnp.cos(angles), -doubling * jnp.sin(angles)], axis=0).astype(
        jnp.bfloat16
    )


def banded_shards(
    grid_state, conv_weight, spectral_gain, spectral_weight, norm_gain, expand_weight, reduce_weight
):
    lat_rows, sector_width, channel_total = grid_state.shape
    lat_count = lax.axis_size("lat")
    lon_count = lax.axis_size("lon")
    lat_total = lat_rows * lat_count
    lon_total = sector_width * lon_count
    mode_count = M
    order_share = mode_count // lat_count
    channel_share = channel_total // lon_count
    lat_position = lax.axis_index("lat")
    wrapped = padded_2(grid_state, (("lon", 1),), 1, True)
    padded = padded_2(wrapped, (("lat", 0),), 1, False)
    padded_wide = padded.astype(jnp.float32)
    filtered = jnp.zeros((lat_rows, sector_width, channel_total), jnp.float32)
    for row_shift in range(3):
        for col_shift in range(3):
            filtered = (
                filtered
                + conv_weight[row_shift, col_shift]
                * padded_wide[
                    row_shift : row_shift + lat_rows, col_shift : col_shift + sector_width
                ]
            )
    first_section = (grid_state.astype(jnp.float32) + jax.nn.gelu(filtered)).astype(jnp.bfloat16)
    gathered = lax.all_to_all(first_section, "lon", split_axis=2, concat_axis=1, tiled=True)
    forward_table = fourier_table(jnp.arange(lon_total, dtype=jnp.int32), lon_total, mode_count)
    spectrum = jnp.einsum(
        "tpc,prm->tmrc", gathered, forward_table, preferred_element_type=jnp.float32
    ).astype(jnp.bfloat16)
    cycle_spectrum = lax.all_to_all(spectrum, "lat", split_axis=1, concat_axis=0, tiled=True)
    orders = lat_position * order_share + jnp.arange(order_share, dtype=jnp.int32)
    legendre = legendre_table(orders, lat_total, mode_count)
    analysis_table = (legendre * quadrature(lat_total)[None, None, :]).astype(jnp.bfloat16)
    coefficients = jnp.einsum(
        "lmt,tmrc->lmrc", analysis_table, cycle_spectrum, preferred_element_type=jnp.float32
    )
    gain_real = spectral_gain[0][:, None, :]
    gain_imag = spectral_gain[1][:, None, :]
    coef_real = coefficients[:, :, 0, :]
    coef_imag = coefficients[:, :, 1, :]
    gained = jnp.stack(
        [
            gain_real * coef_real - gain_imag * coef_imag,
            gain_real * coef_imag + gain_imag * coef_real,
        ],
        axis=2,
    ).astype(jnp.bfloat16)
    blank = jnp.zeros((mode_count * order_share, channel_share), jnp.float32)
    portion = lax.all_gather(gained, "lon", axis=3, tiled=True)
    width_part = portion.shape[3]
    weight_rows = lax.slice_in_dim(spectral_weight, 0, width_part, axis=1)
    real_part = portion[:, :, 0, :].reshape(-1, width_part)
    imag_part = portion[:, :, 1, :].reshape(-1, width_part)
    real_sum = (
        blank
        + jnp.dot(real_part, weight_rows[0], preferred_element_type=jnp.float32)
        - jnp.dot(imag_part, weight_rows[1], preferred_element_type=jnp.float32)
    )
    imag_sum = (
        blank
        + jnp.dot(real_part, weight_rows[1], preferred_element_type=jnp.float32)
        + jnp.dot(imag_part, weight_rows[0], preferred_element_type=jnp.float32)
    )
    mixed = jnp.stack(
        [
            real_sum.reshape(mode_count, order_share, channel_share),
            imag_sum.reshape(mode_count, order_share, channel_share),
        ],
        axis=2,
    ).astype(jnp.bfloat16)
    synthesis_legendre = legendre.astype(jnp.bfloat16)
    cycle_modes = jnp.einsum(
        "lmt,lmrc->tmrc", synthesis_legendre, mixed, preferred_element_type=jnp.float32
    ).astype(jnp.bfloat16)
    band_modes = lax.all_to_all(cycle_modes, "lat", split_axis=0, concat_axis=1, tiled=True)
    inverse_table = synthesis_table(jnp.arange(lon_total, dtype=jnp.int32), lon_total, mode_count)
    all_lons = jnp.einsum(
        "tmrc,rmp->tpc", band_modes, inverse_table, preferred_element_type=jnp.float32
    )
    spectral_out = lax.all_to_all(
        all_lons.astype(jnp.bfloat16), "lon", split_axis=1, concat_axis=2, tiled=True
    ).astype(all_lons.dtype)
    second_section = (first_section.astype(jnp.float32) + spectral_out).astype(jnp.bfloat16)
    second_wide = second_section.astype(jnp.float32)
    scale_values = lax.rsqrt(jnp.mean(second_wide * second_wide, axis=-1, keepdims=True) + norm_eps)
    normed = (second_wide * norm_gain * scale_values).astype(jnp.bfloat16)
    flat_rows = normed.reshape(-1, channel_total)
    hidden = jax.nn.gelu(
        jnp.dot(flat_rows, expand_weight, preferred_element_type=jnp.float32)
    ).astype(jnp.bfloat16)
    update = jnp.dot(hidden, reduce_weight, preferred_element_type=jnp.float32)
    block_output = (second_wide.reshape(-1, channel_total) + update).astype(jnp.bfloat16)
    return block_output.reshape(lat_rows, sector_width, channel_total)


contract_last = (((1,), (1,)), ((), ()))


def legendre_constant(lat_total, mode_count):
    colatitude = (np.arange(lat_total // 2) + 0.5) * (math.pi / lat_total)
    cosines, sines = np.cos(colatitude)[:, None], np.sin(colatitude)[:, None]
    orders = np.arange(mode_count, dtype=np.float64)
    ranks = np.arange(1, mode_count, dtype=np.float64)
    log_terms = 0.5 * np.log((2.0 * ranks + 1.0) / (2.0 * ranks))
    log_norm = np.concatenate([np.zeros(1), np.cumsum(log_terms)])
    log_start = -0.5 * math.log(4.0 * math.pi) + log_norm + orders * np.log(sines)
    start = np.where(
        log_start > underflow_cut, np.exp(np.maximum(log_start, underflow_cut)), 0.0
    )
    table = np.zeros((lat_total // 2, mode_count, mode_count))
    previous = np.zeros_like(start)
    earlier = np.zeros_like(start)
    for degree in range(mode_count):
        raised = np.sqrt(
            np.maximum(4.0 * degree * degree - 1.0, 0.0)
            / np.maximum(degree * degree - orders * orders, 1.0)
        )
        lowered = np.sqrt(
            np.maximum((degree - 1.0) ** 2 - orders * orders, 0.0)
            / max(4.0 * (degree - 1.0) ** 2 - 1.0, 1.0)
        )
        recurred = raised * (cosines * previous - lowered * earlier)
        current = np.where(degree < orders, 0.0, np.where(degree == orders, start, recurred))
        earlier, previous = previous, current
        table[:, degree, :] = current
    return table


def parity_tables(lat_total, mode_count):
    table = legendre_constant(lat_total, mode_count)
    return np.stack([table[:, :, 0::2], table[:, :, 1::2]]).astype(jnp.bfloat16)


def analysis_constant(sectors, width, span, mode_count):
    lon_total = sectors * width
    out = np.zeros((2, sectors, span, 2, mode_count // 2))
    for parity in range(2):
        modes = np.arange(parity, mode_count, 2)
        for sector in range(sectors):
            longitudes = sector * width + np.arange(width)
            angles = (longitudes[:, None] * modes[None, :] % lon_total) * (2 * math.pi / lon_total)
            out[parity, sector, :width, 0] = np.cos(angles) / lon_total
            out[parity, sector, :width, 1] = -np.sin(angles) / lon_total
    return out.reshape(2, sectors, span, mode_count).astype(jnp.bfloat16)


def synthesis_constant(sectors, width, padded, mode_count):
    lon_total = sectors * width
    out = np.zeros((sectors, 2, 2, padded, 2, mode_count // 2))
    for sector in range(sectors):
        longitudes = sector * width + np.arange(width)
        for half in range(2):
            modes = np.arange((sector + half) % 2, mode_count, 2)
            doubling = np.where(modes == 0, 1.0, 2.0)[None, :]
            angles = (longitudes[:, None] * modes[None, :] % lon_total) * (2 * math.pi / lon_total)
            cosine, sine = doubling * np.cos(angles), doubling * np.sin(angles)
            out[sector, half, 0, :width, 0] = cosine
            out[sector, half, 0, :width, 1] = -sine
            out[sector, half, 1, :width, 0] = sine
            out[sector, half, 1, :width, 1] = cosine
    return out.reshape(sectors, 2, 2 * padded, mode_count).astype(jnp.bfloat16)


def gelu(value):
    inner = value * (0.7978845608028654 + (0.7978845608028654 * 0.044715) * (value * value))
    half = 0.5 * value
    return half + half * jnp.tanh(inner)


def pack_body(chips, share, width, grid_ref, out_ref, wide_ref):
    span = wide_ref.shape[1]
    tail = width // 8 * 8
    flipped = []
    for row in range(2):
        wide_ref[row, tail:span, :] = jnp.zeros((span - tail, chips * share), jnp.float32)
        wide_ref[row, 0:width, :] = grid_ref[row].astype(jnp.float32)
        flipped.append(wide_ref[row].T)
    rest = flipped[0][:, LANES:] + pltpu.roll(flipped[1][:, LANES:], width - LANES, axis=1)
    for chip in range(chips):
        at = slice(chip * share, (chip + 1) * share)
        block = jnp.concatenate(
            [flipped[0][at, :LANES], flipped[1][at, :LANES], rest[at]], axis=0
        )
        out_ref[chip] = block.astype(jnp.bfloat16)


def spectral_body(
    lat_count, columns, share, width,
    parity_ref, own_ref, other_ref, gain_ref, tap_ref, legendre_ref, table_ref, out_ref,
    field_ref, exact_ref, west_ref, east_ref, first_ref, modes_ref,
):
    lat_total = 2 * lat_count
    north = lat_total // 2
    sectors = 2 * columns
    edge = width - LANES
    span = 2 * LANES
    orders = legendre_ref.shape[2]
    parity = parity_ref[0]
    for source, core in ((own_ref, parity), (other_ref, 1 - parity)):
        for column in range(columns):
            sector = 2 * column + core
            for band in range(lat_count):
                block = source[column * lat_count + band].astype(jnp.float32)
                rest = block[2 * share :]
                high = jnp.concatenate([rest, pltpu.roll(rest, LANES - edge, axis=1)], axis=0)
                whole = jnp.concatenate([block[: 2 * share], high], axis=1)
                rows = slice(2 * band * share, 2 * (band + 1) * share)
                exact_ref[sector, rows, :] = whole.astype(jnp.bfloat16)
                field_ref[sector, 2 * band] = whole[:share]
                field_ref[sector, 2 * band + 1] = whole[share:]

    took = lax.broadcasted_iota(jnp.int32, (span, span), 0)
    gave = lax.broadcasted_iota(jnp.int32, (span, span), 1)
    one, zero = jnp.float32(1.0), jnp.float32(0.0)

    inner = jnp.where((took + 1 == gave + LANES) & (gave < LANES), one, zero)
    inner = jnp.where((took == gave - LANES + 1) & (gave >= LANES), one, inner)
    inner = inner.astype(jnp.bfloat16)
    to_west = jnp.where((took == gave + LANES - 1) & (gave > 0), one, zero)
    to_west = jnp.where((took == edge - 1) & (gave == 0), one, to_west)
    to_west = to_west[:, :LANES].astype(jnp.bfloat16)
    to_east = jnp.where((took == gave + 1) & (gave < edge - 1), one, zero)
    to_east = jnp.where((took == LANES) & (gave == edge - 1), one, to_east)
    to_east = to_east[:, :LANES].astype(jnp.bfloat16)

    def spread(value):
        return value.reshape(lat_total, share, LANES)

    for sector in range(sectors):
        middle = jnp.dot(exact_ref[sector], inner, preferred_element_type=jnp.float32)
        west_ref[sector, :, :, LANES:] = spread(middle[:, :LANES])
        east_ref[sector, :, :, :LANES] = spread(middle[:, LANES:])
        before = jnp.concatenate(
            [exact_ref[(sector - 1) % sectors, :, LANES:], exact_ref[sector, :, :LANES]], axis=1
        )
        west_ref[sector, :, :, :LANES] = spread(
            jnp.dot(before, to_west, preferred_element_type=jnp.float32)
        )
        after = jnp.concatenate(
            [exact_ref[sector, :, LANES:], exact_ref[(sector + 1) % sectors, :, :LANES]], axis=1
        )
        east_ref[sector, :, :, LANES:] = spread(
            jnp.dot(after, to_east, preferred_element_type=jnp.float32)
        )

    def filter_sector(sector, unused):
        def filter_rows(tile, unused):
            rows = pl.ds(pl.multiple_of(tile * 8, 8), 8)
            taps = []
            for k in range(9):
                tap = tap_ref[k, rows, :]
                taps.append(jnp.concatenate([tap, tap], axis=1))
            held, total, ahead = None, None, None

            def finish(t, value, sum_):
                first_ref[sector, pl.ds(pl.multiple_of(t * share + tile * 8, 8), 8), :] = value + gelu(sum_)

            for t in range(lat_total):
                value = field_ref[sector, t, rows, :]
                west = west_ref[sector, t, rows, :]
                east = east_ref[sector, t, rows, :]

                def weigh(row):
                    return (
                        taps[3 * row] * west + taps[3 * row + 1] * value + taps[3 * row + 2] * east
                    )

                if t > 0:
                    finish(t - 1, held, total + weigh(2))
                total = weigh(1) if t == 0 else ahead + weigh(1)
                ahead = weigh(0)
                held = value
            finish(lat_total - 1, held, total)
            return unused

        return lax.fori_loop(0, share // 8, filter_rows, unused)

    lax.fori_loop(0, sectors, filter_sector, 0)

    modes = None
    for sector in range(sectors):
        part = jnp.dot(
            first_ref[sector].astype(jnp.bfloat16),
            table_ref[sector],
            preferred_element_type=jnp.float32,
        )
        modes = part if modes is None else modes + part
    modes_ref[...] = modes

    sign = (1 - 2 * parity).astype(jnp.float32)
    folded = [[], []]
    for t in range(north):
        weight = 2.0 * math.pi * math.pi / lat_total * math.sin(math.pi * (t + 0.5) / lat_total)
        upper = weight * modes_ref[t * share : (t + 1) * share, :]
        mirror = lat_total - 1 - t
        lower = (weight * sign) * modes_ref[mirror * share : (mirror + 1) * share, :]
        folded[0].append(upper + lower)
        folded[1].append(upper - lower)

    sums = [[None] * north, [None] * north]

    def add(half, t, kernel, value):
        real = kernel[0] * value[:, :orders] - kernel[1] * value[:, orders:]
        imag = kernel[0] * value[:, orders:] + kernel[1] * value[:, :orders]
        had = sums[half][t]
        sums[half][t] = (real, imag) if had is None else (had[0] + real, had[1] + imag)

    for t in range(north):
        products = jnp.concatenate(
            [legendre_ref[t] * legendre_ref[s] for s in range(t, north)], axis=1
        )
        kernels = jnp.dot(gain_ref[...], products, preferred_element_type=jnp.float32)
        for s in range(t, north):
            at = slice((s - t) * orders, (s - t + 1) * orders)
            for half in range(2):
                base = 2 * half * share
                kernel = (kernels[base : base + share, at], kernels[base + share : base + 2 * share, at])
                add(half, t, kernel, folded[half][s])
                if s != t:
                    add(half, s, kernel, folded[half][t])

    for t in range(north):
        for part in range(2):
            even, odd = sums[0][t][part], sums[1][t][part]
            for place, value in ((t, even + odd), (lat_total - 1 - t, sign * (even - odd))):
                at = (place % 2) * 2 * orders + part * orders
                value = value.astype(jnp.bfloat16)
                for column in range(columns):
                    out_ref[column, place // 2, :, at : at + orders] = value


def stage_body(
    place_ref, own_ref, table_ref,
    mix_a_ref, mix_b_ref, mix_c_ref, mix_d_ref,
    field_ref, mix_ref, sems,
):
    place = place_ref[0]
    held = mix_a_ref.shape[1]
    loads = []
    for k, source in enumerate((mix_a_ref, mix_b_ref, mix_c_ref, mix_d_ref)):
        sector = 2 * (place // 2 if k < 2 else 1 - place // 2) + (
            place % 2 if k % 2 == 0 else 1 - place % 2
        )
        rows = pl.ds(pl.multiple_of(sector * held, held), held)
        loads.append(pltpu.make_async_copy(source, mix_ref.at[:, rows, :], sems.at[k]))
    for load in loads:
        load.start()
    modes = table_ref.shape[2]
    for row in range(2):
        field_ref[row] = lax.dot_general(
            table_ref[0], own_ref[:, row * modes : (row + 1) * modes], contract_last,
            preferred_element_type=jnp.float32,
        )
    for load in loads:
        load.wait()


def finish_body(
    width, padded,
    field_ref, other_ref, first_ref, gain_ref, table_ref, mix_ref, expand_ref, reduce_ref,
    marker_ref, out_ref,
):
    modes = table_ref.shape[2]
    real, imag = [], []
    for row in range(2):
        field = field_ref[row] + lax.dot_general(
            table_ref[1], other_ref[:, row * modes : (row + 1) * modes], contract_last,
            preferred_element_type=jnp.float32,
        )
        real.append(field[:padded])
        imag.append(field[padded:])
    real = jnp.concatenate(real, axis=0).astype(jnp.bfloat16)
    imag = jnp.concatenate(imag, axis=0).astype(jnp.bfloat16)
    spectral_out = lax.dot_general(
        real, mix_ref[0], contract_last, preferred_element_type=jnp.float32
    ) - lax.dot_general(imag, mix_ref[1], contract_last, preferred_element_type=jnp.float32)
    second = (first_ref[...].astype(jnp.float32) + spectral_out).astype(jnp.bfloat16)
    wide = second.astype(jnp.float32)
    scale = lax.rsqrt(jnp.mean(wide * wide, axis=-1, keepdims=True) + norm_eps)
    normed = (wide * gain_ref[...] * scale).astype(jnp.bfloat16)
    hidden = gelu(jnp.dot(normed, expand_ref[...], preferred_element_type=jnp.float32))
    update = jnp.dot(
        hidden.astype(jnp.bfloat16), reduce_ref[...], preferred_element_type=jnp.float32
    )
    result = wide + update
    for row in range(2):
        out_ref[row] = result[row * padded : row * padded + width].astype(jnp.bfloat16)


def local_body(
    width, padded, above_ref, grid_ref, below_ref, west_ref, east_ref, tap_ref,
    out_ref, marker_ref, tall_ref,
):
    marker_ref[...] = jnp.zeros_like(marker_ref)
    west, east = west_ref[...].astype(jnp.float32), east_ref[...].astype(jnp.float32)
    for k, row in enumerate((above_ref[...], grid_ref[0], grid_ref[1], below_ref[...])):
        tall_ref[k, 8 + width // 8 * 8 :, :] = jnp.zeros(
            (padded + 8 - width // 8 * 8, row.shape[1]), jnp.float32
        )
        tall_ref[k, 8 : 8 + width, :] = row.astype(jnp.float32)
        tall_ref[k, 7:8, :] = west[k : k + 1]
        tall_ref[k, 8 + width : 9 + width, :] = east[k : k + 1]
    inside = lax.broadcasted_iota(jnp.int32, (padded, LANES), 0) < width
    for piece in range(tall_ref.shape[2] // LANES):
        lanes = slice(piece * LANES, (piece + 1) * LANES)
        total = [None, None]
        for k in range(4):
            for col in range(3):
                value = tall_ref[k, 7 + col : 7 + col + padded, lanes]
                for row in range(2):
                    if 0 <= k - row < 3:
                        tap = tap_ref[3 * (k - row) + col : 3 * (k - row) + col + 1, lanes]
                        part = tap * value
                        total[row] = part if total[row] is None else total[row] + part
        for row in range(2):
            value = tall_ref[1 + row, 8 : 8 + padded, lanes] + gelu(total[row])
            value = jnp.where(inside, value, 0.0)
            total[row] = value
        out_ref[:, lanes] = jnp.concatenate(total, axis=0).astype(jnp.bfloat16)


def own_part(constant, at):
    return lax.dynamic_index_in_dim(jnp.asarray(constant), at, 0, keepdims=False)


def in_hbm(count):
    return [pl.BlockSpec(memory_space=pl.ANY)] * count


def in_vmem(count):
    return [pl.BlockSpec(memory_space=pltpu.VMEM)] * count


def chip_shards(
    grid_state, conv_weight, spectral_gain, spectral_weight, norm_gain, expand_weight, reduce_weight
):
    lat_rows, width, channels = grid_state.shape
    lat_count, columns = lax.axis_size("lat"), lax.axis_size("x")
    chips, sectors = lat_count * columns, 2 * columns
    share = channels // chips
    lat_total = lat_rows * lat_count
    orders = M // 2
    span = 2 * LANES
    padded = -(-width // 8) * 8
    lat_at, column, core = lax.axis_index("lat"), lax.axis_index("x"), lax.axis_index("core")
    swap = [(0, 1), (1, 0)]
    over_chips = ("x", "lat")

    packed = pl.pallas_call(
        functools.partial(pack_body, chips, share, width),
        out_shape=jax.ShapeDtypeStruct((chips, 3 * share, LANES), jnp.bfloat16),
        in_specs=in_vmem(1),
        out_specs=in_vmem(1)[0],
        scratch_shapes=[pltpu.VMEM((2, span, channels), jnp.float32)],
        compiler_params=pltpu.CompilerParams(vmem_limit_bytes=16 << 20),
        name="pack",
    )(grid_state)
    grid_first = grid_state
    packed, later = lax.optimization_barrier(
        (packed, (grid_state, conv_weight, spectral_gain))
    )
    grid_state, conv_weight, spectral_gain = later
    own = lax.all_to_all(packed, over_chips, split_axis=0, concat_axis=0, tiled=True)

    own_mix = spectral_weight.transpose(0, 2, 1)
    held = own_mix.shape[1]

    across_mix = lax.ppermute(own_mix, "x", [(i, 1 - i) for i in range(columns)])
    across_mix, spectral_gain = lax.optimization_barrier((across_mix, spectral_gain))
    blocks = held // share
    piece = lax.dynamic_slice_in_dim(
        spectral_gain, (lat_at % blocks) * share, share, axis=2
    ).transpose(0, 2, 1)
    piece_other = lax.ppermute(piece, "core", swap)
    gains = jnp.where(core == lat_at // blocks, piece, piece_other)
    even = (jnp.arange(M) % 2 == 0)[None, :]
    gain_rows = jnp.concatenate(
        [
            jnp.where(even, gains[0], 0.0),
            jnp.where(even, gains[1], 0.0),
            jnp.where(even, 0.0, gains[0]),
            jnp.where(even, 0.0, gains[1]),
        ],
        axis=0,
    ).astype(jnp.bfloat16)
    chip = column * lat_count + lat_at
    taps = lax.dynamic_slice_in_dim(conv_weight.reshape(9, channels), chip * share, share, axis=1)
    taps = jnp.broadcast_to(taps[:, :, None], (9, share, LANES))

    legendre = own_part(parity_tables(lat_total, M), core)
    analysis = own_part(analysis_constant(sectors, width, span, M), core)
    table = own_part(synthesis_constant(sectors, width, padded, M), 2 * column + core)

    own, across_mix = lax.optimization_barrier((own, across_mix))
    other = lax.ppermute(own, "core", swap)
    above = lax.ppermute(grid_first[1], "lat", [(i, i + 1) for i in range(lat_count - 1)])
    below = lax.ppermute(grid_first[0], "lat", [(i + 1, i) for i in range(lat_count - 1)])

    bands = pl.pallas_call(
        functools.partial(spectral_body, lat_count, columns, share, width),
        out_shape=jax.ShapeDtypeStruct((columns, lat_count, share, 2 * M), jnp.bfloat16),
        in_specs=[pl.BlockSpec(memory_space=pltpu.SMEM)] + in_vmem(6),
        out_specs=in_vmem(1)[0],
        scratch_shapes=[
            pltpu.VMEM((sectors, lat_total, share, span), jnp.float32),
            pltpu.VMEM((sectors, lat_total * share, span), jnp.bfloat16),
            pltpu.VMEM((sectors, lat_total, share, span), jnp.float32),
            pltpu.VMEM((sectors, lat_total, share, span), jnp.float32),
            pltpu.VMEM((sectors, lat_total * share, span), jnp.float32),
            pltpu.VMEM((lat_total * share, M), jnp.float32),
        ],
        cost_estimate=pl.CostEstimate(flops=9 * 10**9, bytes_accessed=0, transcendentals=0),
        compiler_params=pltpu.CompilerParams(vmem_limit_bytes=28 << 20),
        name="spectral",
    )(core[None], own, other, gain_rows, taps, legendre, analysis)
    bands, above, below, across_mix = lax.optimization_barrier((bands, above, below, across_mix))
    beside_mix = lax.ppermute(own_mix, "core", swap)
    far_mix = lax.ppermute(across_mix, "core", swap)
    ring = [(i, (i + 1) % sectors) for i in range(sectors)]
    tall = (above, grid_state[0], grid_state[1], below)
    west = lax.ppermute(
        jnp.stack([row[width - 1] for row in tall]), ("x", "core"), ring
    )
    east = lax.ppermute(
        jnp.stack([row[0] for row in tall]), ("x", "core"), [(j, i) for i, j in ring]
    )
    first_rows, marker = pl.pallas_call(
        functools.partial(local_body, width, padded),
        out_shape=[
            jax.ShapeDtypeStruct((2 * padded, channels), jnp.bfloat16),
            jax.ShapeDtypeStruct((8, LANES), jnp.float32),
        ],
        in_specs=in_vmem(6),
        out_specs=in_vmem(2),
        scratch_shapes=[pltpu.VMEM((4, padded + 16, channels), jnp.float32)],
        cost_estimate=pl.CostEstimate(flops=8 * 10**9, bytes_accessed=0, transcendentals=0),
        compiler_params=pltpu.CompilerParams(vmem_limit_bytes=16 << 20),
        name="local",
    )(above, grid_state, below, west, east, conv_weight.reshape(9, channels))
    back = lax.all_to_all(
        bands.reshape(chips, share, 2 * M), over_chips, split_axis=0, concat_axis=0, tiled=True
    ).reshape(channels, 2 * M)
    back, marker, table = lax.optimization_barrier((back, marker, table))
    back_other = lax.ppermute(back, "core", swap)

    field, mixing = pl.pallas_call(
        stage_body,
        out_shape=[
            jax.ShapeDtypeStruct((2, 2 * padded, channels), jnp.float32),
            jax.ShapeDtypeStruct((2, channels, channels), jnp.bfloat16),
        ],
        in_specs=[pl.BlockSpec(memory_space=pltpu.SMEM)] + in_vmem(2) + in_hbm(4),
        out_specs=in_vmem(2),
        scratch_shapes=[pltpu.SemaphoreType.DMA((4,))],
        cost_estimate=pl.CostEstimate(flops=12 * 10**9, bytes_accessed=0, transcendentals=0),
        compiler_params=pltpu.CompilerParams(vmem_limit_bytes=16 << 20),
        name="stage",
    )(
        (2 * column + core)[None], back, table,
        own_mix, beside_mix, across_mix, far_mix,
    )

    return pl.pallas_call(
        functools.partial(finish_body, width, padded),
        out_shape=jax.ShapeDtypeStruct(grid_state.shape, jnp.bfloat16),
        in_specs=in_vmem(9),
        out_specs=in_vmem(1)[0],
        cost_estimate=pl.CostEstimate(flops=3 * 10**9, bytes_accessed=0, transcendentals=0),
        compiler_params=pltpu.CompilerParams(vmem_limit_bytes=16 << 20),
        name="finish",
    )(
        field, back_other, first_rows, norm_gain[None, :], table, mixing, expand_weight,
        reduce_weight, marker,
    )


def solution(mesh):
    lat_count, lon_count = mesh.shape["lat"], mesh.shape["lon"]
    columns = lon_count // 2
    cored = Mesh(mesh.devices.reshape(lat_count, columns, 2), ("lat", "x", "core"))

    def run(grid_state, *rest):
        lat_total, lon_total, channels = grid_state.shape
        chips = lat_count * columns
        width = lon_total // lon_count
        fits = (
            columns == 2
            and lat_total == 2 * lat_count
            and lat_total <= 32
            and channels % (8 * chips) == 0
            and lat_count % 2 == 0
            and (channels // lon_count) * 2 == (channels // chips) * lat_count
            and LANES + 2 <= width
            and 2 * (width - LANES) <= LANES
        )
        if fits:
            body, on, lat, lon = chip_shards, cored, "lat", ("x", "core")
        else:
            body, on, lat, lon = banded_shards, mesh, "lat", "lon"
        return jax.shard_map(
            body,
            mesh=on,
            in_specs=(
                P(lat, lon, None), P(), P(None, None, lon), P(None, None, lon), P(), P(), P(),
            ),
            out_specs=P(lat, lon, None),
            check_vma=False,
        )(grid_state, *rest)

    return run
```

```python
import functools
import math

import jax
import jax.numpy as jnp
import numpy as np
from jax import lax
from jax.experimental import pallas as pl
from jax.experimental.pallas import tpu as pltpu
from jax.sharding import Mesh
from jax.sharding import PartitionSpec as P

M = 256
LANES = 128


norm_eps = 1e-06
underflow_cut = -60.0
degree_block = 16


def padded_2(value, sides, width, wrap):
    for axis, dim in sides:
        count, length = (lax.axis_size(axis), value.shape[dim])
        up = [(i, (i + 1) % count) for i in range(count if wrap else count - 1)]
        down = [(j, i) for i, j in up]
        last = lax.slice_in_dim(value, length - width, length, axis=dim)
        initial = lax.slice_in_dim(value, 0, width, axis=dim)
        before = lax.ppermute(last, axis, up)
        after = lax.ppermute(initial, axis, down)
        value = jnp.concatenate([before, value, after], axis=dim)
    return value


def legendre_table(orders, lat_total, degree_count):
    colatitude = (jnp.arange(lat_total, dtype=jnp.float32) + 0.5) * (math.pi / lat_total)
    cosines = jnp.cos(colatitude)
    sine_values = jnp.sin(colatitude)
    rank_values = jnp.arange(1, degree_count + 1, dtype=jnp.int32)
    rank_float = rank_values.astype(jnp.float32)
    log_terms = 0.5 * jnp.log((2.0 * rank_float + 1.0) / (2.0 * rank_float))
    log_norm = jnp.sum(
        jnp.where(rank_values[None, :] <= orders[:, None], log_terms[None, :], jnp.float32(0.0)),
        axis=1,
    )
    order_float = orders.astype(jnp.float32)[:, None]
    log_start = (
        -0.5 * math.log(4.0 * math.pi)
        + log_norm[:, None]
        + order_float * jnp.log(sine_values)[None, :]
    )
    start_value = jnp.where(
        log_start > underflow_cut, jnp.exp(jnp.maximum(log_start, underflow_cut)), jnp.float32(0.0)
    )

    def advance_block(totals, block_start):
        previous, earlier = totals
        rows_out = []
        for inner in range(degree_block):
            degree = block_start + inner
            degree_float = degree.astype(jnp.float32)
            raise_coef = jnp.sqrt(
                jnp.maximum(4.0 * degree_float * degree_float - 1.0, 0.0)
                / jnp.maximum(degree_float * degree_float - order_float * order_float, 1.0)
            )
            lower_coef = jnp.sqrt(
                jnp.maximum((degree_float - 1.0) ** 2 - order_float * order_float, 0.0)
                / jnp.maximum(4.0 * (degree_float - 1.0) ** 2 - 1.0, 1.0)
            )
            recurred = raise_coef * (cosines[None, :] * previous - lower_coef * earlier)
            current = jnp.where(
                degree < orders[:, None],
                jnp.float32(0.0),
                jnp.where(degree == orders[:, None], start_value, recurred),
            )
            earlier = previous
            previous = current
            rows_out.append(current)
        return ((previous, earlier), jnp.stack(rows_out, axis=0))

    blank = jnp.zeros((orders.shape[0], lat_total), jnp.float32)
    starts = jnp.arange(0, degree_count, degree_block, dtype=jnp.int32)
    unused, table_blocks = lax.scan(advance_block, (blank, blank), starts)
    return table_blocks.reshape(degree_count, orders.shape[0], lat_total)


def quadrature(lat_total):
    colatitude = (jnp.arange(lat_total, dtype=jnp.float32) + 0.5) * (math.pi / lat_total)
    return 2.0 * math.pi * math.pi / lat_total * jnp.sin(colatitude)


def fourier_table(longitudes, lon_total, mode_count):
    mode_index = jnp.arange(mode_count, dtype=jnp.int32)
    phase_index = longitudes[:, None] * mode_index[None, :] % lon_total
    angles = phase_index.astype(jnp.float32) * (2.0 * math.pi / lon_total)
    return (jnp.stack([jnp.cos(angles), -jnp.sin(angles)], axis=1) / lon_total).astype(jnp.bfloat16)


def synthesis_table(longitudes, lon_total, mode_count):
    mode_index = jnp.arange(mode_count, dtype=jnp.int32)
    phase_index = mode_index[:, None] * longitudes[None, :] % lon_total
    angles = phase_index.astype(jnp.float32) * (2.0 * math.pi / lon_total)
    doubling = jnp.where(mode_index == 0, 1.0, 2.0).astype(jnp.float32)[:, None]
    return jnp.stack([doubling * jnp.cos(angles), -doubling * jnp.sin(angles)], axis=0).astype(
        jnp.bfloat16
    )


def banded_shards(
    grid_state, conv_weight, spectral_gain, spectral_weight, norm_gain, expand_weight, reduce_weight
):
    lat_rows, sector_width, channel_total = grid_state.shape
    lat_count = lax.axis_size("lat")
    lon_count = lax.axis_size("lon")
    lat_total = lat_rows * lat_count
    lon_total = sector_width * lon_count
    mode_count = M
    order_share = mode_count // lat_count
    channel_share = channel_total // lon_count
    lat_position = lax.axis_index("lat")
    wrapped = padded_2(grid_state, (("lon", 1),), 1, True)
    padded = padded_2(wrapped, (("lat", 0),), 1, False)
    padded_wide = padded.astype(jnp.float32)
    filtered = jnp.zeros((lat_rows, sector_width, channel_total), jnp.float32)
    for row_shift in range(3):
        for col_shift in range(3):
            filtered = (
                filtered
                + conv_weight[row_shift, col_shift]
                * padded_wide[
                    row_shift : row_shift + lat_rows, col_shift : col_shift + sector_width
                ]
            )
    first_section = (grid_state.astype(jnp.float32) + jax.nn.gelu(filtered)).astype(jnp.bfloat16)
    gathered = lax.all_to_all(first_section, "lon", split_axis=2, concat_axis=1, tiled=True)
    forward_table = fourier_table(jnp.arange(lon_total, dtype=jnp.int32), lon_total, mode_count)
    spectrum = jnp.einsum(
        "tpc,prm->tmrc", gathered, forward_table, preferred_element_type=jnp.float32
    ).astype(jnp.bfloat16)
    cycle_spectrum = lax.all_to_all(spectrum, "lat", split_axis=1, concat_axis=0, tiled=True)
    orders = lat_position * order_share + jnp.arange(order_share, dtype=jnp.int32)
    legendre = legendre_table(orders, lat_total, mode_count)
    analysis_table = (legendre * quadrature(lat_total)[None, None, :]).astype(jnp.bfloat16)
    coefficients = jnp.einsum(
        "lmt,tmrc->lmrc", analysis_table, cycle_spectrum, preferred_element_type=jnp.float32
    )
    gain_real = spectral_gain[0][:, None, :]
    gain_imag = spectral_gain[1][:, None, :]
    coef_real = coefficients[:, :, 0, :]
    coef_imag = coefficients[:, :, 1, :]
    gained = jnp.stack(
        [
            gain_real * coef_real - gain_imag * coef_imag,
            gain_real * coef_imag + gain_imag * coef_real,
        ],
        axis=2,
    ).astype(jnp.bfloat16)
    blank = jnp.zeros((mode_count * order_share, channel_share), jnp.float32)
    portion = lax.all_gather(gained, "lon", axis=3, tiled=True)
    width_part = portion.shape[3]
    weight_rows = lax.slice_in_dim(spectral_weight, 0, width_part, axis=1)
    real_part = portion[:, :, 0, :].reshape(-1, width_part)
    imag_part = portion[:, :, 1, :].reshape(-1, width_part)
    real_sum = (
        blank
        + jnp.dot(real_part, weight_rows[0], preferred_element_type=jnp.float32)
        - jnp.dot(imag_part, weight_rows[1], preferred_element_type=jnp.float32)
    )
    imag_sum = (
        blank
        + jnp.dot(real_part, weight_rows[1], preferred_element_type=jnp.float32)
        + jnp.dot(imag_part, weight_rows[0], preferred_element_type=jnp.float32)
    )
    mixed = jnp.stack(
        [
            real_sum.reshape(mode_count, order_share, channel_share),
            imag_sum.reshape(mode_count, order_share, channel_share),
        ],
        axis=2,
    ).astype(jnp.bfloat16)
    synthesis_legendre = legendre.astype(jnp.bfloat16)
    cycle_modes = jnp.einsum(
        "lmt,lmrc->tmrc", synthesis_legendre, mixed, preferred_element_type=jnp.float32
    ).astype(jnp.bfloat16)
    band_modes = lax.all_to_all(cycle_modes, "lat", split_axis=0, concat_axis=1, tiled=True)
    inverse_table = synthesis_table(jnp.arange(lon_total, dtype=jnp.int32), lon_total, mode_count)
    all_lons = jnp.einsum(
        "tmrc,rmp->tpc", band_modes, inverse_table, preferred_element_type=jnp.float32
    )
    spectral_out = lax.all_to_all(
        all_lons.astype(jnp.bfloat16), "lon", split_axis=1, concat_axis=2, tiled=True
    ).astype(all_lons.dtype)
    second_section = (first_section.astype(jnp.float32) + spectral_out).astype(jnp.bfloat16)
    second_wide = second_section.astype(jnp.float32)
    scale_values = lax.rsqrt(jnp.mean(second_wide * second_wide, axis=-1, keepdims=True) + norm_eps)
    normed = (second_wide * norm_gain * scale_values).astype(jnp.bfloat16)
    flat_rows = normed.reshape(-1, channel_total)
    hidden = jax.nn.gelu(
        jnp.dot(flat_rows, expand_weight, preferred_element_type=jnp.float32)
    ).astype(jnp.bfloat16)
    update = jnp.dot(hidden, reduce_weight, preferred_element_type=jnp.float32)
    block_output = (second_wide.reshape(-1, channel_total) + update).astype(jnp.bfloat16)
    return block_output.reshape(lat_rows, sector_width, channel_total)


contract_last = (((1,), (1,)), ((), ()))


def legendre_constant(lat_total, mode_count):
    colatitude = (np.arange(lat_total // 2) + 0.5) * (math.pi / lat_total)
    cosines, sines = np.cos(colatitude)[:, None], np.sin(colatitude)[:, None]
    orders = np.arange(mode_count, dtype=np.float64)
    ranks = np.arange(1, mode_count, dtype=np.float64)
    log_terms = 0.5 * np.log((2.0 * ranks + 1.0) / (2.0 * ranks))
    log_norm = np.concatenate([np.zeros(1), np.cumsum(log_terms)])
    log_start = -0.5 * math.log(4.0 * math.pi) + log_norm + orders * np.log(sines)
    start = np.where(
        log_start > underflow_cut, np.exp(np.maximum(log_start, underflow_cut)), 0.0
    )
    table = np.zeros((lat_total // 2, mode_count, mode_count))
    previous = np.zeros_like(start)
    earlier = np.zeros_like(start)
    for degree in range(mode_count):
        raised = np.sqrt(
            np.maximum(4.0 * degree * degree - 1.0, 0.0)
            / np.maximum(degree * degree - orders * orders, 1.0)
        )
        lowered = np.sqrt(
            np.maximum((degree - 1.0) ** 2 - orders * orders, 0.0)
            / max(4.0 * (degree - 1.0) ** 2 - 1.0, 1.0)
        )
        recurred = raised * (cosines * previous - lowered * earlier)
        current = np.where(degree < orders, 0.0, np.where(degree == orders, start, recurred))
        earlier, previous = previous, current
        table[:, degree, :] = current
    return table


def parity_tables(lat_total, mode_count):
    table = legendre_constant(lat_total, mode_count)
    return np.stack([table[:, :, 0::2], table[:, :, 1::2]]).astype(jnp.bfloat16)


def analysis_constant(sectors, width, span, mode_count):
    lon_total = sectors * width
    out = np.zeros((2, sectors, span, 2, mode_count // 2))
    for parity in range(2):
        modes = np.arange(parity, mode_count, 2)
        for sector in range(sectors):
            longitudes = sector * width + np.arange(width)
            angles = (longitudes[:, None] * modes[None, :] % lon_total) * (2 * math.pi / lon_total)
            out[parity, sector, :width, 0] = np.cos(angles) / lon_total
            out[parity, sector, :width, 1] = -np.sin(angles) / lon_total
    return out.reshape(2, sectors, span, mode_count).astype(jnp.bfloat16)


def synthesis_constant(sectors, width, padded, mode_count):
    lon_total = sectors * width
    out = np.zeros((sectors, 2, 2, padded, 2, mode_count // 2))
    for sector in range(sectors):
        longitudes = sector * width + np.arange(width)
        for half in range(2):
            modes = np.arange((sector + half) % 2, mode_count, 2)
            doubling = np.where(modes == 0, 1.0, 2.0)[None, :]
            angles = (longitudes[:, None] * modes[None, :] % lon_total) * (2 * math.pi / lon_total)
            cosine, sine = doubling * np.cos(angles), doubling * np.sin(angles)
            out[sector, half, 0, :width, 0] = cosine
            out[sector, half, 0, :width, 1] = -sine
            out[sector, half, 1, :width, 0] = sine
            out[sector, half, 1, :width, 1] = cosine
    return out.reshape(sectors, 2, 2 * padded, mode_count).astype(jnp.bfloat16)


def gelu_of_double(half):
    inner = half * (1.5957691216057308 + (8 * 0.7978845608028654 * 0.044715) * (half * half))
    return half + half * jnp.tanh(inner)


def gelu(value):
    inner = value * (0.7978845608028654 + (0.7978845608028654 * 0.044715) * (value * value))
    half = 0.5 * value
    return half + half * jnp.tanh(inner)


def pack_body(chips, share, width, grid_ref, out_ref, wide_ref):
    span = wide_ref.shape[1]
    tail = width // 8 * 8
    flipped = []
    for row in range(2):
        wide_ref[row, tail:span, :] = jnp.zeros((span - tail, chips * share), jnp.float32)
        wide_ref[row, 0:width, :] = grid_ref[row].astype(jnp.float32)
        flipped.append(wide_ref[row].T)
    rest = flipped[0][:, LANES:] + pltpu.roll(flipped[1][:, LANES:], width - LANES, axis=1)
    for chip in range(chips):
        at = slice(chip * share, (chip + 1) * share)
        block = jnp.concatenate(
            [flipped[0][at, :LANES], flipped[1][at, :LANES], rest[at]], axis=0
        )
        out_ref[chip] = block.astype(jnp.bfloat16)


def spectral_body(
    lat_count, columns, share, width,
    parity_ref, own_ref, other_ref, gain_ref, tap_ref, legendre_ref, table_ref, out_ref,
    field_ref, exact_ref, west_ref, east_ref, first_ref, modes_ref,
):
    lat_total = 2 * lat_count
    north = lat_total // 2
    sectors = 2 * columns
    edge = width - LANES
    span = 2 * LANES
    orders = legendre_ref.shape[2]
    parity = parity_ref[0]
    for source, core in ((own_ref, parity), (other_ref, 1 - parity)):
        for column in range(columns):
            sector = 2 * column + core
            for band in range(lat_count):
                block = source[column * lat_count + band].astype(jnp.float32)
                rest = block[2 * share :]
                high = jnp.concatenate([rest, pltpu.roll(rest, LANES - edge, axis=1)], axis=0)
                whole = jnp.concatenate([block[: 2 * share], high], axis=1)
                rows = slice(2 * band * share, 2 * (band + 1) * share)
                exact_ref[sector, rows, :] = whole.astype(jnp.bfloat16)
                field_ref[sector, 2 * band] = whole[:share]
                field_ref[sector, 2 * band + 1] = whole[share:]

    took = lax.broadcasted_iota(jnp.int32, (span, span), 0)
    gave = lax.broadcasted_iota(jnp.int32, (span, span), 1)
    one, zero = jnp.float32(1.0), jnp.float32(0.0)

    inner = jnp.where((took + 1 == gave + LANES) & (gave < LANES), one, zero)
    inner = jnp.where((took == gave - LANES + 1) & (gave >= LANES), one, inner)
    inner = inner.astype(jnp.bfloat16)
    to_west = jnp.where((took == gave + LANES - 1) & (gave > 0), one, zero)
    to_west = jnp.where((took == edge - 1) & (gave == 0), one, to_west)
    to_west = to_west[:, :LANES].astype(jnp.bfloat16)
    to_east = jnp.where((took == gave + 1) & (gave < edge - 1), one, zero)
    to_east = jnp.where((took == LANES) & (gave == edge - 1), one, to_east)
    to_east = to_east[:, :LANES].astype(jnp.bfloat16)

    def spread(value):
        return value.reshape(lat_total, share, LANES)

    for sector in range(sectors):
        middle = jnp.dot(exact_ref[sector], inner, preferred_element_type=jnp.float32)
        west_ref[sector, :, :, LANES:] = spread(middle[:, :LANES])
        east_ref[sector, :, :, :LANES] = spread(middle[:, LANES:])
        before = jnp.concatenate(
            [exact_ref[(sector - 1) % sectors, :, LANES:], exact_ref[sector, :, :LANES]], axis=1
        )
        west_ref[sector, :, :, :LANES] = spread(
            jnp.dot(before, to_west, preferred_element_type=jnp.float32)
        )
        after = jnp.concatenate(
            [exact_ref[sector, :, LANES:], exact_ref[(sector + 1) % sectors, :, :LANES]], axis=1
        )
        east_ref[sector, :, :, LANES:] = spread(
            jnp.dot(after, to_east, preferred_element_type=jnp.float32)
        )

    def filter_sector(sector, unused):
        def filter_rows(tile, unused):
            rows = pl.ds(pl.multiple_of(tile * 8, 8), 8)
            taps = []
            for k in range(9):
                tap = tap_ref[k, rows, :]
                taps.append(jnp.concatenate([tap, tap], axis=1))
            held, total, ahead = None, None, None

            def finish(t, value, sum_):
                first_ref[sector, pl.ds(pl.multiple_of(t * share + tile * 8, 8), 8), :] = value + gelu_of_double(sum_)

            for t in range(lat_total):
                value = field_ref[sector, t, rows, :]
                west = west_ref[sector, t, rows, :]
                east = east_ref[sector, t, rows, :]

                def weigh(row):
                    return (
                        taps[3 * row] * west + taps[3 * row + 1] * value + taps[3 * row + 2] * east
                    )

                if t > 0:
                    finish(t - 1, held, total + weigh(2))
                total = weigh(1) if t == 0 else ahead + weigh(1)
                ahead = weigh(0)
                held = value
            finish(lat_total - 1, held, total)
            return unused

        return lax.fori_loop(0, share // 8, filter_rows, unused)

    for sector in range(sectors):
        filter_sector(sector, 0)

    modes = None
    for sector in range(sectors):
        part = jnp.dot(
            first_ref[sector].astype(jnp.bfloat16),
            table_ref[sector],
            preferred_element_type=jnp.float32,
        )
        modes = part if modes is None else modes + part
    modes_ref[...] = modes

    sign = (1 - 2 * parity).astype(jnp.float32)
    folded = [[], []]
    for t in range(north):
        weight = 2.0 * math.pi * math.pi / lat_total * math.sin(math.pi * (t + 0.5) / lat_total)
        upper = weight * modes_ref[t * share : (t + 1) * share, :]
        mirror = lat_total - 1 - t
        lower = (weight * sign) * modes_ref[mirror * share : (mirror + 1) * share, :]
        folded[0].append(upper + lower)
        folded[1].append(upper - lower)

    sums = [[None] * north, [None] * north]

    def add(half, t, kernel, value):
        real = kernel[0] * value[:, :orders] - kernel[1] * value[:, orders:]
        imag = kernel[0] * value[:, orders:] + kernel[1] * value[:, :orders]
        had = sums[half][t]
        sums[half][t] = (real, imag) if had is None else (had[0] + real, had[1] + imag)

    for t in range(north):
        products = jnp.concatenate(
            [legendre_ref[t] * legendre_ref[s] for s in range(t, north)], axis=1
        )
        kernels = jnp.dot(gain_ref[...], products, preferred_element_type=jnp.float32)
        for s in range(t, north):
            at = slice((s - t) * orders, (s - t + 1) * orders)
            for half in range(2):
                base = 2 * half * share
                kernel = (kernels[base : base + share, at], kernels[base + share : base + 2 * share, at])
                add(half, t, kernel, folded[half][s])
                if s != t:
                    add(half, s, kernel, folded[half][t])

    for t in range(north):
        for part in range(2):
            even, odd = sums[0][t][part], sums[1][t][part]
            for place, value in ((t, even + odd), (lat_total - 1 - t, sign * (even - odd))):
                at = (place % 2) * 2 * orders + part * orders
                value = value.astype(jnp.bfloat16)
                for column in range(columns):
                    out_ref[column, place // 2, :, at : at + orders] = value


def stage_body(
    place_ref, own_ref, table_ref,
    mix_a_ref, mix_b_ref, mix_c_ref, mix_d_ref,
    field_ref, mix_ref, sems,
):
    place = place_ref[0]
    held = mix_a_ref.shape[1]
    loads = []
    for k, source in enumerate((mix_a_ref, mix_b_ref, mix_c_ref, mix_d_ref)):
        sector = 2 * (place // 2 if k < 2 else 1 - place // 2) + (
            place % 2 if k % 2 == 0 else 1 - place % 2
        )
        rows = pl.ds(pl.multiple_of(sector * held, held), held)
        loads.append(pltpu.make_async_copy(source, mix_ref.at[:, rows, :], sems.at[k]))
    for load in loads:
        load.start()
    modes = table_ref.shape[2]
    for row in range(2):
        field_ref[row] = lax.dot_general(
            table_ref[0], own_ref[:, row * modes : (row + 1) * modes], contract_last,
            preferred_element_type=jnp.float32,
        )
    for load in loads:
        load.wait()


def finish_body(
    width, padded,
    field_ref, other_ref, first_ref, gain_ref, table_ref, mix_ref, expand_ref, reduce_ref,
    marker_ref, out_ref,
):
    modes = table_ref.shape[2]
    real, imag = [], []
    for row in range(2):
        field = field_ref[row] + lax.dot_general(
            table_ref[1], other_ref[:, row * modes : (row + 1) * modes], contract_last,
            preferred_element_type=jnp.float32,
        )
        real.append(field[:padded])
        imag.append(field[padded:])
    real = jnp.concatenate(real, axis=0).astype(jnp.bfloat16)
    imag = jnp.concatenate(imag, axis=0).astype(jnp.bfloat16)
    spectral_out = lax.dot_general(
        real, mix_ref[0], contract_last, preferred_element_type=jnp.float32
    ) - lax.dot_general(imag, mix_ref[1], contract_last, preferred_element_type=jnp.float32)
    second = (first_ref[...].astype(jnp.float32) + spectral_out).astype(jnp.bfloat16)
    wide = second.astype(jnp.float32)
    scale = lax.rsqrt(jnp.mean(wide * wide, axis=-1, keepdims=True) + norm_eps)
    normed = (wide * gain_ref[...] * scale).astype(jnp.bfloat16)
    hidden = gelu(jnp.dot(normed, expand_ref[...], preferred_element_type=jnp.float32))
    update = jnp.dot(
        hidden.astype(jnp.bfloat16), reduce_ref[...], preferred_element_type=jnp.float32
    )
    result = wide + update
    for row in range(2):
        out_ref[row] = result[row * padded : row * padded + width].astype(jnp.bfloat16)


def local_body(
    width, padded, above_ref, grid_ref, below_ref, west_ref, east_ref, tap_ref,
    out_ref, marker_ref, tall_ref,
):
    marker_ref[...] = jnp.zeros_like(marker_ref)
    west, east = west_ref[...].astype(jnp.float32), east_ref[...].astype(jnp.float32)
    for k, row in enumerate((above_ref[...], grid_ref[0], grid_ref[1], below_ref[...])):
        tall_ref[k, 8 + width // 8 * 8 :, :] = jnp.zeros(
            (padded + 8 - width // 8 * 8, row.shape[1]), jnp.float32
        )
        tall_ref[k, 8 : 8 + width, :] = row.astype(jnp.float32)
        tall_ref[k, 7:8, :] = west[k : k + 1]
        tall_ref[k, 8 + width : 9 + width, :] = east[k : k + 1]
    inside = lax.broadcasted_iota(jnp.int32, (padded, LANES), 0) < width
    for piece in range(tall_ref.shape[2] // LANES):
        lanes = slice(piece * LANES, (piece + 1) * LANES)
        total = [None, None]
        for k in range(4):
            for col in range(3):
                value = tall_ref[k, 7 + col : 7 + col + padded, lanes]
                for row in range(2):
                    if 0 <= k - row < 3:
                        tap = tap_ref[3 * (k - row) + col : 3 * (k - row) + col + 1, lanes]
                        part = tap * value
                        total[row] = part if total[row] is None else total[row] + part
        for row in range(2):
            value = tall_ref[1 + row, 8 : 8 + padded, lanes] + gelu(total[row])
            value = jnp.where(inside, value, 0.0)
            total[row] = value
        out_ref[:, lanes] = jnp.concatenate(total, axis=0).astype(jnp.bfloat16)


def own_part(constant, at):
    return lax.dynamic_index_in_dim(jnp.asarray(constant), at, 0, keepdims=False)


def in_hbm(count):
    return [pl.BlockSpec(memory_space=pl.ANY)] * count


def in_vmem(count):
    return [pl.BlockSpec(memory_space=pltpu.VMEM)] * count


def chip_shards(
    grid_state, conv_weight, spectral_gain, spectral_weight, norm_gain, expand_weight, reduce_weight
):
    lat_rows, width, channels = grid_state.shape
    lat_count, columns = lax.axis_size("lat"), lax.axis_size("x")
    chips, sectors = lat_count * columns, 2 * columns
    share = channels // chips
    lat_total = lat_rows * lat_count
    orders = M // 2
    span = 2 * LANES
    padded = -(-width // 8) * 8
    lat_at, column, core = lax.axis_index("lat"), lax.axis_index("x"), lax.axis_index("core")
    swap = [(0, 1), (1, 0)]
    over_chips = ("x", "lat")

    packed = pl.pallas_call(
        functools.partial(pack_body, chips, share, width),
        out_shape=jax.ShapeDtypeStruct((chips, 3 * share, LANES), jnp.bfloat16),
        in_specs=in_vmem(1),
        out_specs=in_vmem(1)[0],
        scratch_shapes=[pltpu.VMEM((2, span, channels), jnp.float32)],
        compiler_params=pltpu.CompilerParams(vmem_limit_bytes=16 << 20),
        name="pack",
    )(grid_state)
    grid_first = grid_state
    packed, later = lax.optimization_barrier(
        (packed, (grid_state, conv_weight, spectral_gain))
    )
    grid_state, conv_weight, spectral_gain = later
    own = lax.all_to_all(packed, over_chips, split_axis=0, concat_axis=0, tiled=True)

    own_mix = spectral_weight.transpose(0, 2, 1)
    held = own_mix.shape[1]

    across_mix = lax.ppermute(own_mix, "x", [(i, 1 - i) for i in range(columns)])
    across_mix, spectral_gain = lax.optimization_barrier((across_mix, spectral_gain))
    blocks = held // share
    piece = lax.dynamic_slice_in_dim(
        spectral_gain, (lat_at % blocks) * share, share, axis=2
    ).transpose(0, 2, 1)
    piece_other = lax.ppermute(piece, "core", swap)
    gains = jnp.where(core == lat_at // blocks, piece, piece_other)
    even = (jnp.arange(M) % 2 == 0)[None, :]
    gain_rows = jnp.concatenate(
        [
            jnp.where(even, gains[0], 0.0),
            jnp.where(even, gains[1], 0.0),
            jnp.where(even, 0.0, gains[0]),
            jnp.where(even, 0.0, gains[1]),
        ],
        axis=0,
    ).astype(jnp.bfloat16)
    chip = column * lat_count + lat_at
    taps = lax.dynamic_slice_in_dim(conv_weight.reshape(9, channels), chip * share, share, axis=1)
    taps = jnp.broadcast_to(0.5 * taps[:, :, None], (9, share, LANES))

    legendre = own_part(parity_tables(lat_total, M), core)
    analysis = own_part(analysis_constant(sectors, width, span, M), core)
    table = own_part(synthesis_constant(sectors, width, padded, M), 2 * column + core)

    own, across_mix = lax.optimization_barrier((own, across_mix))
    other = lax.ppermute(own, "core", swap)
    above = lax.ppermute(grid_first[1], "lat", [(i, i + 1) for i in range(lat_count - 1)])
    below = lax.ppermute(grid_first[0], "lat", [(i + 1, i) for i in range(lat_count - 1)])

    bands = pl.pallas_call(
        functools.partial(spectral_body, lat_count, columns, share, width),
        out_shape=jax.ShapeDtypeStruct((columns, lat_count, share, 2 * M), jnp.bfloat16),
        in_specs=[pl.BlockSpec(memory_space=pltpu.SMEM)] + in_vmem(6),
        out_specs=in_vmem(1)[0],
        scratch_shapes=[
            pltpu.VMEM((sectors, lat_total, share, span), jnp.float32),
            pltpu.VMEM((sectors, lat_total * share, span), jnp.bfloat16),
            pltpu.VMEM((sectors, lat_total, share, span), jnp.float32),
            pltpu.VMEM((sectors, lat_total, share, span), jnp.float32),
            pltpu.VMEM((sectors, lat_total * share, span), jnp.float32),
            pltpu.VMEM((lat_total * share, M), jnp.float32),
        ],
        cost_estimate=pl.CostEstimate(flops=9 * 10**9, bytes_accessed=0, transcendentals=0),
        compiler_params=pltpu.CompilerParams(vmem_limit_bytes=28 << 20),
        name="spectral",
    )(core[None], own, other, gain_rows, taps, legendre, analysis)
    bands, above, below, across_mix = lax.optimization_barrier((bands, above, below, across_mix))
    beside_mix = lax.ppermute(own_mix, "core", swap)
    far_mix = lax.ppermute(across_mix, "core", swap)
    ring = [(i, (i + 1) % sectors) for i in range(sectors)]
    tall = (above, grid_state[0], grid_state[1], below)
    west = lax.ppermute(
        jnp.stack([row[width - 1] for row in tall]), ("x", "core"), ring
    )
    east = lax.ppermute(
        jnp.stack([row[0] for row in tall]), ("x", "core"), [(j, i) for i, j in ring]
    )
    first_rows, marker = pl.pallas_call(
        functools.partial(local_body, width, padded),
        out_shape=[
            jax.ShapeDtypeStruct((2 * padded, channels), jnp.bfloat16),
            jax.ShapeDtypeStruct((8, LANES), jnp.float32),
        ],
        in_specs=in_vmem(6),
        out_specs=in_vmem(2),
        scratch_shapes=[pltpu.VMEM((4, padded + 16, channels), jnp.float32)],
        cost_estimate=pl.CostEstimate(flops=8 * 10**9, bytes_accessed=0, transcendentals=0),
        compiler_params=pltpu.CompilerParams(vmem_limit_bytes=16 << 20),
        name="local",
    )(above, grid_state, below, west, east, conv_weight.reshape(9, channels))
    back = lax.all_to_all(
        bands.reshape(chips, share, 2 * M), over_chips, split_axis=0, concat_axis=0, tiled=True
    ).reshape(channels, 2 * M)
    back, marker, table = lax.optimization_barrier((back, marker, table))
    back_other = lax.ppermute(back, "core", swap)

    field, mixing = pl.pallas_call(
        stage_body,
        out_shape=[
            jax.ShapeDtypeStruct((2, 2 * padded, channels), jnp.float32),
            jax.ShapeDtypeStruct((2, channels, channels), jnp.bfloat16),
        ],
        in_specs=[pl.BlockSpec(memory_space=pltpu.SMEM)] + in_vmem(2) + in_hbm(4),
        out_specs=in_vmem(2),
        scratch_shapes=[pltpu.SemaphoreType.DMA((4,))],
        cost_estimate=pl.CostEstimate(flops=12 * 10**9, bytes_accessed=0, transcendentals=0),
        compiler_params=pltpu.CompilerParams(vmem_limit_bytes=16 << 20),
        name="stage",
    )(
        (2 * column + core)[None], back, table,
        own_mix, beside_mix, across_mix, far_mix,
    )

    return pl.pallas_call(
        functools.partial(finish_body, width, padded),
        out_shape=jax.ShapeDtypeStruct(grid_state.shape, jnp.bfloat16),
        in_specs=in_vmem(9),
        out_specs=in_vmem(1)[0],
        cost_estimate=pl.CostEstimate(flops=3 * 10**9, bytes_accessed=0, transcendentals=0),
        compiler_params=pltpu.CompilerParams(vmem_limit_bytes=16 << 20),
        name="finish",
    )(
        field, back_other, first_rows, norm_gain[None, :], table, mixing, expand_weight,
        reduce_weight, marker,
    )


def solution(mesh):
    lat_count, lon_count = mesh.shape["lat"], mesh.shape["lon"]
    columns = lon_count // 2
    cored = Mesh(mesh.devices.reshape(lat_count, columns, 2), ("lat", "x", "core"))

    def run(grid_state, *rest):
        lat_total, lon_total, channels = grid_state.shape
        chips = lat_count * columns
        width = lon_total // lon_count
        fits = (
            columns == 2
            and lat_total == 2 * lat_count
            and lat_total <= 32
            and channels % (8 * chips) == 0
            and lat_count % 2 == 0
            and (channels // lon_count) * 2 == (channels // chips) * lat_count
            and LANES + 2 <= width
            and 2 * (width - LANES) <= LANES
        )
        if fits:
            body, on, lat, lon = chip_shards, cored, "lat", ("x", "core")
        else:
            body, on, lat, lon = banded_shards, mesh, "lat", "lon"
        return jax.shard_map(
            body,
            mesh=on,
            in_specs=(
                P(lat, lon, None), P(), P(None, None, lon), P(None, None, lon), P(), P(), P(),
            ),
            out_specs=P(lat, lon, None),
            check_vma=False,
        )(grid_state, *rest)

    return run
```
